32 devices in a mesh: section: 2 (over core), dp: 16 (over z, y, x).
Axes of the slice: x: 2, y: 2, z: 4, core: 2. Of those that a mesh axis runs over, the one named last changes fastest.
Arguments:
- pixels: bfloat16 [8, 2048, 768], P(None, 'dp'), may hold values from -4 to 4
- codes_top: int32 [8, 256, 32], P(None, 'dp'), may hold values from 0 to 511
- codes_bottom: int32 [8, 512, 64], P(None, 'dp'), may hold values from 0 to 511
- valid_rows: int32 [8, 8], replicated, may hold values from 64 to 256
- dead_codes: int32 [2, 8], replicated, may hold values from 0 to 511, as said below
- dead_source: int32 [2, 8], replicated, may hold values from 0 to 262143, as said below
- w_conv: float32 [3, 1152, 64], replicated, may hold values from -0.1875 to 0.1875
- w_res_out: float32 [3, 64, 128], replicated, may hold values from -0.75 to 0.75
- w_from_code: float32 [5, 64, 128], replicated, may hold values from -0.75 to 0.75
- w_to_code: float32 [2, 128, 64], replicated, may hold values from -0.5 to 0.5
- w_pixel: float32 [2, 48, 128], replicated, may hold values from -0.5 to 0.5
- w_down: float32 [4, 128, 128], replicated, may hold values from -0.25 to 0.25
- m_conv: float32 [3, 1152, 64], replicated, may hold values from -9.536743e-07 to 9.536743e-07
- m_res_out: float32 [3, 64, 128], replicated, may hold values from -9.536743e-07 to 9.536743e-07
- m_from_code: float32 [5, 64, 128], replicated, may hold values from -9.536743e-07 to 9.536743e-07
- m_to_code: float32 [2, 128, 64], replicated, may hold values from -9.536743e-07 to 9.536743e-07
- m_pixel: float32 [2, 48, 128], replicated, may hold values from -9.536743e-07 to 9.536743e-07
- m_down: float32 [4, 128, 128], replicated, may hold values from -9.536743e-07 to 9.536743e-07
- v_conv: float32 [3, 1152, 64], replicated, may hold values from 2.625168e-15 to 1.0500672e-14
- v_res_out: float32 [3, 64, 128], replicated, may hold values from 2.625168e-15 to 1.0500672e-14
- v_from_code: float32 [5, 64, 128], replicated, may hold values from 2.625168e-15 to 1.0500672e-14
- v_to_code: float32 [2, 128, 64], replicated, may hold values from 2.625168e-15 to 1.0500672e-14
- v_pixel: float32 [2, 48, 128], replicated, may hold values from 2.625168e-15 to 1.0500672e-14
- v_down: float32 [4, 128, 128], replicated, may hold values from 2.625168e-15 to 1.0500672e-14
- codebook: float32 [2, 512, 64], replicated, may hold values from -5 to 5
- ema_count: float32 [2, 512], replicated, may hold values from 5 to 50
- ema_sum: float32 [2, 512, 64], replicated, may hold values from -60 to 60
Outputs:
- grad_norm: float32 [], replicated
- loss_pair: float32 [2], replicated
- new_conv: float32 [3, 1152, 64], replicated
- new_res_out: float32 [3, 64, 128], replicated
- new_from_code: float32 [5, 64, 128], replicated
- new_to_code: float32 [2, 128, 64], replicated
- new_pixel: float32 [2, 48, 128], replicated
- new_down: float32 [4, 128, 128], replicated
- mom_conv: float32 [3, 1152, 64], replicated
- mom_res_out: float32 [3, 64, 128], replicated
- mom_from_code: float32 [5, 64, 128], replicated
- mom_to_code: float32 [2, 128, 64], replicated
- mom_pixel: float32 [2, 48, 128], replicated
- mom_down: float32 [4, 128, 128], replicated
- sec_conv: float32 [3, 1152, 64], replicated
- sec_res_out: float32 [3, 64, 128], replicated
- sec_from_code: float32 [5, 64, 128], replicated
- sec_to_code: float32 [2, 128, 64], replicated
- sec_pixel: float32 [2, 48, 128], replicated
- sec_down: float32 [4, 128, 128], replicated
- low_conv: bfloat16 [3, 1152, 64], replicated
- low_res_out: bfloat16 [3, 64, 128], replicated
- low_from_code: bfloat16 [5, 64, 128], replicated
- low_to_code: bfloat16 [2, 128, 64], replicated
- low_pixel: bfloat16 [2, 48, 128], replicated
- low_down: bfloat16 [4, 128, 128], replicated
- new_book: float32 [2, 512, 64], replicated
- new_count: float32 [2, 512], replicated
- new_sum: float32 [2, 512, 64], replicated
The draws below stay inside these ranges and needn't reach their ends.
Inputs may be any that keep to these rules, and one draw needn't show every extreme that they name: `dead_codes`: each row holds 8 different codes of one level, row 0 the top level and row 1 the bottom. `dead_source`: row 0 indexes top positions in (micro-batch, row, column) order, below 8 * 8 * (32) squared, one of them 0; row 1 bottom positions, below 8 * 8 * (64) squared, one of them the last.
All inputs are finite; a program needn't handle non-finite values.
Results may differ from the reference program's by a relative error of at most 0.001.
The reference program's roundings to bfloat16 on the way count: a program that leaves them out, or rounds other values in their place, can miss the bound.
Values may be sent and summed in bfloat16 or wider, within the bound.
A program may use at most 576 MiB of HBM per device.

```python
import math
import jax
import jax.numpy as jnp
from jax import lax

C = 128
RC = 64
EMB = 64
K = 512
IMG = 256
MB = 8
DEAD = 8
STEP = 10
IMGS = 8
NPARAMS = 380928


def draw_dead_codes(key, part):
    key = jax.random.fold_in(key, 11)
    first_key, second_key = jax.random.split(key)
    top_codes = jax.random.permutation(first_key, K)[:DEAD]
    bottom_codes = jax.random.permutation(second_key, K)[:DEAD]
    return jnp.stack([top_codes, bottom_codes]).astype(jnp.int32)


def draw_dead_source(key, part):
    key = jax.random.fold_in(key, 12)
    first_key, second_key, third_key, fourth_key = jax.random.split(key, 4)
    top_count = MB * IMGS * (IMG // 8) * (IMG // 8)
    bottom_count = MB * IMGS * (IMG // 4) * (IMG // 4)
    top_source = jax.random.randint(first_key, (DEAD,), 0, top_count)
    bottom_source = jax.random.randint(second_key, (DEAD,), 0, bottom_count)
    slot_ids = jnp.arange(DEAD)
    top_slot = jax.random.randint(third_key, (), 0, DEAD)
    bottom_slot = jax.random.randint(fourth_key, (), 0, DEAD)
    top_source = jnp.where(slot_ids == top_slot, 0, top_source)
    bottom_source = jnp.where(slot_ids == bottom_slot, bottom_count - 1, bottom_source)
    return jnp.stack([top_source, bottom_source]).astype(jnp.int32)


def plant(array, own_key, low, largest):
    extent = array.shape
    place = [jax.random.randint(jax.random.fold_in(own_key, axis), (), 0, extent[axis]) for axis in range(len(extent))]
    array = array.at[tuple(place)].set(low)
    longest = extent.index(max(extent))
    place[longest] = (place[longest] + 1) % extent[longest]
    return array.at[tuple(place)].set(largest)


def steps_of(rng, extent, shards, least, top_value):
    loudness = 1.0
    for dim, blocks in shards:
        steps = jax.random.uniform(jax.random.fold_in(jax.random.fold_in(rng, 6), dim), (blocks,), jnp.float32, least / len(shards), top_value / len(shards))
        loudness = loudness * jnp.repeat(jnp.exp(steps), extent[dim] // blocks).reshape((-1,) + (1,) * (len(extent) - 1 - dim))
    return loudness


def noise(key, shape, scale, reach, pieces=(), kind=jnp.bfloat16):
    entries = jax.random.normal(key, shape, jnp.float32) * scale
    if len(pieces) > 0:
        entries = steps_of(key, shape, pieces, -0.22, 0.18) * entries
    return jnp.clip(entries, min=-reach, max=reach).astype(kind)


def setup_inputs(seed: int = 0) -> dict:
    key_of = jax.random.split(jax.random.key(seed), 28)
    return {
        "pixels": noise(key_of[0], (MB, IMGS * IMG, IMG * 3), 1.0, 4.0, ((1, 16),)),
        "codes_top": plant(jax.random.randint(key_of[1], (MB, IMGS * IMG // 8, IMG // 8), 0, K), jax.random.fold_in(key_of[1], 1), 0, K - 1).astype(jnp.int32),
        "codes_bottom": plant(jax.random.randint(key_of[2], (MB, IMGS * IMG // 4, IMG // 4), 0, K), jax.random.fold_in(key_of[2], 1), 0, K - 1).astype(jnp.int32),
        "valid_rows": plant(jax.random.randint(key_of[3], (MB, IMGS), IMG // 4, IMG + 1), jax.random.fold_in(key_of[3], 1), IMG // 4, IMG).astype(jnp.int32),
        "dead_codes": draw_dead_codes(jax.random.fold_in(key_of[27], 71), 0),
        "dead_source": draw_dead_source(jax.random.fold_in(key_of[27], 71), 0),
        "w_conv": noise(key_of[6], (3, 9 * C, RC), (9 * C) ** -0.5, 0.1875, (), jnp.float32),
        "w_res_out": noise(key_of[7], (3, RC, C), RC ** -0.5, 0.75, (), jnp.float32),
        "w_from_code": noise(key_of[8], (5, EMB, C), EMB ** -0.5, 0.75, (), jnp.float32),
        "w_to_code": noise(key_of[9], (2, C, EMB), C ** -0.5, 0.5, (), jnp.float32),
        "w_pixel": noise(key_of[10], (2, 48, C), C ** -0.5, 0.5, (), jnp.float32),
        "w_down": noise(key_of[11], (4, C, C), (4 * C) ** -0.5, 0.25, (), jnp.float32),
        "m_conv": noise(key_of[12], (3, 9 * C, RC), (0.00011 / NPARAMS ** 0.5), 9.5367431640625e-07, (), jnp.float32),
        "m_res_out": noise(key_of[13], (3, RC, C), (0.00011 / NPARAMS ** 0.5), 9.5367431640625e-07, (), jnp.float32),
        "m_from_code": noise(key_of[14], (5, EMB, C), (0.00011 / NPARAMS ** 0.5), 9.5367431640625e-07, (), jnp.float32),
        "m_to_code": noise(key_of[15], (2, C, EMB), (0.00011 / NPARAMS ** 0.5), 9.5367431640625e-07, (), jnp.float32),
        "m_pixel": noise(key_of[16], (2, 48, C), (0.00011 / NPARAMS ** 0.5), 9.5367431640625e-07, (), jnp.float32),
        "m_down": noise(key_of[17], (4, C, C), (0.00011 / NPARAMS ** 0.5), 9.5367431640625e-07, (), jnp.float32),
        "v_conv": jnp.clip(jnp.exp(jax.random.uniform(key_of[18], (3, 9 * C, RC), jnp.float32, math.log(2.6251679205690744e-15), math.log(1.0500671682276298e-14))), 2.6251679205690744e-15, 1.0500671682276298e-14),
        "v_res_out": jnp.clip(jnp.exp(jax.random.uniform(key_of[19], (3, RC, C), jnp.float32, math.log(2.6251679205690744e-15), math.log(1.0500671682276298e-14))), 2.6251679205690744e-15, 1.0500671682276298e-14),
        "v_from_code": jnp.clip(jnp.exp(jax.random.uniform(key_of[20], (5, EMB, C), jnp.float32, math.log(2.6251679205690744e-15), math.log(1.0500671682276298e-14))), 2.6251679205690744e-15, 1.0500671682276298e-14),
        "v_to_code": jnp.clip(jnp.exp(jax.random.uniform(key_of[21], (2, C, EMB), jnp.float32, math.log(2.6251679205690744e-15), math.log(1.0500671682276298e-14))), 2.6251679205690744e-15, 1.0500671682276298e-14),
        "v_pixel": jnp.clip(jnp.exp(jax.random.uniform(key_of[22], (2, 48, C), jnp.float32, math.log(2.6251679205690744e-15), math.log(1.0500671682276298e-14))), 2.6251679205690744e-15, 1.0500671682276298e-14),
        "v_down": jnp.clip(jnp.exp(jax.random.uniform(key_of[23], (4, C, C), jnp.float32, math.log(2.6251679205690744e-15), math.log(1.0500671682276298e-14))), 2.6251679205690744e-15, 1.0500671682276298e-14),
        "codebook": noise(key_of[24], (2, K, EMB), 1.0, 5.0, (), jnp.float32),
        "ema_count": jnp.clip(jnp.exp(jax.random.uniform(key_of[25], (2, K), jnp.float32, math.log(5.0), math.log(50.0))), 5.0, 50.0),
        "ema_sum": noise(key_of[26], (2, K, EMB), 10.0, 60.0, (), jnp.float32),
    }


@jax.custom_vjp
def low(v):
    return lax.optimization_barrier(v.astype(jnp.bfloat16)).astype(jnp.float32)

@jax.custom_vjp
def low_back(v):
    return v

def low_keep(v):
    return (low(v), None)

def low_pass(kept, grad):
    return (grad,)

def back_keep(v):
    return (v, None)

def back_low(kept, grad):
    return (low(grad),)
low.defvjp(low_keep, low_pass)
low_back.defvjp(back_keep, back_low)
COMMIT_WEIGHT = 0.25
CODE_DECAY = 0.9
CLIP_NORM = 0.001
LEARN_RATE = 0.03
MOMENT_ONE = 0.9
MOMENT_TWO = 0.999
WEIGHT_DECAY = 0.01
ADAM_EPSILON = 1e-08
HIGHEST = lax.Precision.HIGHEST

def product(x, w):
    return low_back(jnp.dot(x, w, precision=HIGHEST))

def conv_same(x, w, height):
    pictures = x.reshape(-1, height, x.shape[1], x.shape[2])
    kernel = w.reshape(3, 3, x.shape[2], w.shape[1])
    result = lax.conv_general_dilated(pictures, kernel, (1, 1), 'SAME', dimension_numbers=('NHWC', 'HWIO', 'NHWC'), precision=HIGHEST)
    return low_back(result.reshape(x.shape[0], x.shape[1], w.shape[1]))

def res_block(x, kernel, w_out, height):
    preact = conv_same(low(x), kernel, height)
    return x + product(low(jax.nn.silu(preact)), w_out)

def patchify(picture):
    num_rows = picture.shape[0] // 4
    num_cols = picture.shape[1] // 12
    return picture.reshape(num_rows, 4, num_cols, 4, 3).transpose(0, 2, 1, 3, 4).reshape(num_rows, num_cols, 48)

def to_blocks(x):
    num_rows, num_cols, channels = x.shape
    return x.reshape(num_rows // 2, 2, num_cols // 2, 2, channels).transpose(0, 2, 1, 3, 4).reshape(num_rows // 2, num_cols // 2, 4 * channels)

def from_blocks(x, channels):
    num_rows, num_cols = (x.shape[0], x.shape[1])
    return x.reshape(num_rows, num_cols, 2, 2, channels).transpose(0, 2, 1, 3, 4).reshape(2 * num_rows, 2 * num_cols, channels)

def forward(weights, pictures, codes_top, codes_bottom, pixel_masks, codebook, valid_count, anchors):
    kernels, outputs, from_code, to_code, pixel_maps, down_maps = [low(w) for w in weights]
    channels = pixel_maps.shape[2]
    up_flat = from_code[1:].transpose(1, 0, 2).reshape(EMB, 4 * channels)
    down_flat = down_maps.reshape(4 * channels, channels)
    numerator = jnp.zeros((), jnp.float32)
    latents = []
    for batch_id in range(MB):
        picture = pictures[batch_id]
        patches = patchify(picture)
        stem_top = low(jax.nn.silu(product(patches, pixel_maps[0])))
        stem_bottom = low_back(low(jax.nn.silu(product(patches, pixel_maps[0]))))
        top_out = res_block(product(to_blocks(stem_top), down_flat), kernels[0], outputs[0], IMG // 8)
        latent_top = product(low(top_out), to_code[0])
        nearest_top = codebook[0][codes_top[batch_id]]
        numerator = numerator + COMMIT_WEIGHT * jnp.sum((latent_top - nearest_top) ** 2)
        if anchors is not None:
            nearest_top = nearest_top + (latent_top - anchors[batch_id][0])
        quant_top = low_back(low(nearest_top))
        upward = from_blocks(product(quant_top, up_flat), channels)
        bottom_out = res_block(stem_bottom + upward, kernels[1], outputs[1], IMG // 4)
        latent_bottom = product(low(bottom_out), to_code[1])
        nearest_bottom = codebook[1][codes_bottom[batch_id]]
        numerator = numerator + COMMIT_WEIGHT * jnp.sum((latent_bottom - nearest_bottom) ** 2)
        if anchors is not None:
            nearest_bottom = nearest_bottom + (latent_bottom - anchors[batch_id][1])
        decoded = res_block(product(low(nearest_bottom), from_code[0]) + upward, kernels[2], outputs[2], IMG // 4)
        rebuilt = product(low(decoded), pixel_maps[1].T)
        numerator = numerator + jnp.sum(patchify(pixel_masks[batch_id]) * (rebuilt - patches) ** 2)
        latents.append((latent_top, latent_bottom))
    return (numerator / valid_count, (numerator, latents))

def adamw(weight, grad, first, second):
    first = MOMENT_ONE * first + (1.0 - MOMENT_ONE) * grad
    second = MOMENT_TWO * second + (1.0 - MOMENT_TWO) * grad * grad
    update = first / (1.0 - MOMENT_ONE ** STEP) / (jnp.sqrt(second / (1.0 - MOMENT_TWO ** STEP)) + ADAM_EPSILON)
    return (weight - LEARN_RATE * (update + WEIGHT_DECAY * weight), first, second)

def reference(pixels, codes_top, codes_bottom, valid_rows, dead_codes, dead_source, w_conv, w_res_out, w_from_code, w_to_code, w_pixel, w_down, m_conv, m_res_out, m_from_code, m_to_code, m_pixel, m_down, v_conv, v_res_out, v_from_code, v_to_code, v_pixel, v_down, codebook, ema_count, ema_sum):
    weights = (w_conv, w_res_out, w_from_code, w_to_code, w_pixel, w_down)
    firsts = (m_conv, m_res_out, m_from_code, m_to_code, m_pixel, m_down)
    seconds = (v_conv, v_res_out, v_from_code, v_to_code, v_pixel, v_down)
    pictures = pixels.astype(jnp.float32)
    row_ids = jnp.arange(IMG)
    row_valid = (row_ids[None, None, :] < valid_rows[:, :, None]).astype(jnp.float32)
    pixel_masks = jnp.broadcast_to(row_valid.reshape(MB, IMGS * IMG, 1), pictures.shape)
    valid_count = 3.0 * IMG * jnp.sum(valid_rows).astype(jnp.float32)
    first_pass = forward(weights, pictures, codes_top, codes_bottom, pixel_masks, codebook, valid_count, None)
    anchors = first_pass[1][1]
    loss_value, pullback, extras = jax.vjp(lambda params: forward(params, pictures, codes_top, codes_bottom, pixel_masks, codebook, valid_count, anchors), weights, has_aux=True)
    gradients = pullback(jnp.ones((), jnp.float32))[0]
    numerator, latents = extras
    grad_norm = jnp.sqrt(sum((jnp.sum(g * g) for g in gradients)))
    factor = CLIP_NORM / jnp.maximum(grad_norm, CLIP_NORM)
    results = [adamw(w, g * factor, m, v) for w, g, m, v in zip(weights, gradients, firsts, seconds)]
    counts_all, sums_all = ([], [])
    for level_id in range(2):
        flat_latent = jnp.concatenate([level_pair[level_id].reshape(-1, EMB) for level_pair in latents], axis=0)
        code_ids = (codes_top, codes_bottom)[level_id].reshape(-1)
        code_used = jax.ops.segment_sum(jnp.ones(code_ids.shape, jnp.float32), code_ids, K)
        summed = jax.ops.segment_sum(flat_latent, code_ids, K)
        counts_next = CODE_DECAY * ema_count[level_id] + (1.0 - CODE_DECAY) * code_used
        sums_next = CODE_DECAY * ema_sum[level_id] + (1.0 - CODE_DECAY) * summed
        dead_match = (jnp.arange(K)[:, None] == dead_codes[level_id][None, :]).astype(jnp.float32)
        dead_taken = lax.optimization_barrier(jnp.sum(dead_match, axis=1))
        replaced = jnp.dot(dead_match, flat_latent[dead_source[level_id]], precision=HIGHEST)
        sums_all.append(jnp.where(dead_taken[:, None] > 0, replaced, sums_next))
        counts_all.append(jnp.where(dead_taken > 0, 1.0, counts_next))
    new_count = jnp.stack(counts_all)
    new_sum = jnp.stack(sums_all)
    new_book = new_sum / new_count[:, :, None]
    loss_pair = jnp.stack([numerator, valid_count])
    return (grad_norm, loss_pair, results[0][0], results[1][0], results[2][0], results[3][0], results[4][0], results[5][0], results[0][1], results[1][1], results[2][1], results[3][1], results[4][1], results[5][1], results[0][2], results[1][2], results[2][2], results[3][2], results[4][2], results[5][2], results[0][0].astype(jnp.bfloat16), results[1][0].astype(jnp.bfloat16), results[2][0].astype(jnp.bfloat16), results[3][0].astype(jnp.bfloat16), results[4][0].astype(jnp.bfloat16), results[5][0].astype(jnp.bfloat16), new_book, new_count, new_sum)
```

```python
import functools

import jax
import jax.numpy as jnp
from jax import lax
from jax.experimental import pallas as pl
from jax.experimental.pallas import tpu as pltpu
from jax.sharding import PartitionSpec as P

STEP = 10
COMMIT_WEIGHT = 0.25
CODE_DECAY = 0.9
CLIP_NORM = 0.001
LEARN_RATE = 0.03
MOMENT_ONE = 0.9
MOMENT_TWO = 0.999
WEIGHT_DECAY = 0.01
ADAM_EPSILON = 1e-08

F32 = jnp.float32
BF16 = jnp.bfloat16
VMEM_LIMIT = 56 * 1024 * 1024
CHUNK = 8

CONV_ROWS = 640
ROW_RES = 3 * CONV_ROWS
ROW_FROM = ROW_RES + 3 * 64
ROW_PIXEL = ROW_FROM + 5 * 64
ROW_DOWN = ROW_PIXEL + 2 * 48
ROW_SUMS = ROW_DOWN + 512
ROW_COUNT = ROW_SUMS + 512
ROW_DEAD = ROW_COUNT + 8
ROW_NUMER = ROW_DEAD + 8
ROW_END = ROW_NUMER + 8


def mm(x, w):
    return lax.dot_general(x, w, (((1,), (0,)), ((), ())), preferred_element_type=F32)


def mm_t(x, w):
    return lax.dot_general(x, w, (((1,), (1,)), ((), ())), preferred_element_type=F32)


def mm_w(x, g):
    return lax.dot_general(x, g, (((0,), (0,)), ((), ())), preferred_element_type=F32)


def lane_iota(shape):
    return lax.broadcasted_iota(jnp.int32, shape, len(shape) - 1)


def low_half(shape):
    return lane_iota(shape) % 128 < 64


def sigmoid(x):
    return 0.5 * jnp.tanh(0.5 * x) + 0.5


def slope(a):
    s = sigmoid(a)
    return s * (1.0 + a * (1.0 - s))


def shift_rows(x, by):
    rows = x.shape[1]
    moved = pltpu.roll(x, by % rows, 1)
    ids = lax.broadcasted_iota(jnp.int32, x.shape, 1)
    edge = 0 if by == 1 else rows - 1
    return jnp.where(ids == edge, 0.0, moved)


def flat(x):
    return x.reshape(x.shape[0] * x.shape[1], x.shape[2])


def pair_diag(w):
    zero = jnp.zeros_like(w)
    return jnp.concatenate(
        [jnp.concatenate([w, zero], axis=1), jnp.concatenate([zero, w], axis=1)], axis=0
    )


def swap_halves(x):
    return pltpu.roll(x, 64, len(x.shape) - 1)


def compute_kernel(
    place,
    valid_s,
    dead_source,
    valid_v,
    pix,
    ct_col,
    cb_col,
    ct_row,
    cb_row,
    w_conv,
    w_res,
    w_from,
    w_to,
    w_pix,
    w_down,
    book,
    out,
    b_fwd,
    b_bwd,
    wo_d,
    from_d,
    to_d,
    up_d,
    pix_d,
    down_b,
    book_a,
    book_b,
    sel,
    patches,
    stem,
    up,
    near,
    near_t,
    xs_dec,
    xs_bot,
    xs_top,
    wide,
    res,
    act_dec,
    act_bot,
    act_top,
    low_dec,
    low_bot,
    low_top,
    lat,
    lat_t,
    resid,
    grad_hi,
    grad_lo,
    d_two,
    d_slots,
    d_two_t,
    d_slots_t,
    gstem,
    gup,
    acc_conv,
    acc_res,
    acc_from,
    acc_up,
    acc_to,
    acc_pix,
    acc_down,
    acc_sums,
    acc_count,
    acc_dead,
    acc_num,
):
    step = pl.program_id(0)
    last = pl.num_programs(0) - 1
    pairs, rows = xs_bot.shape[0], xs_bot.shape[2]
    pairs_t = xs_top.shape[0]
    ch = CHUNK
    ch_t = CHUNK // 2
    valid_count = 3.0 * pix.shape[1] * jnp.sum(valid_v[...].astype(F32))
    loss_slope = 2.0 / valid_count
    commit_slope = loss_slope * COMMIT_WEIGHT

    def loop(total, size, fn):
        def run(k, _):
            fn(pl.multiple_of(k * size, size))
            return 0

        lax.fori_loop(0, total // size, run, 0)

    @pl.when(step == 0)
    def _():
        for ref in (acc_conv, acc_res, acc_from, acc_up, acc_to, acc_pix, acc_down, acc_sums, acc_count, acc_dead, acc_num):
            ref[...] = jnp.zeros(ref.shape, F32)
        wide[...] = jnp.zeros(wide.shape, F32)
        d_two[...] = jnp.zeros(d_two.shape, F32)
        d_two_t[...] = jnp.zeros(d_two_t.shape, F32)
        zero = jnp.zeros((128, 64), F32)
        for k in range(3):
            for i in range(3):
                t = [w_conv[k, pl.ds((i * 3 + j) * 128, 128), :] for j in range(3)]
                even = jnp.concatenate([t[1], t[0], zero, t[2]], axis=1).astype(BF16)
                odd = jnp.concatenate([t[2], t[1], t[0], zero], axis=1).astype(BF16)
                b_fwd[k, pl.ds(i * 256, 128), :] = even
                b_fwd[k, pl.ds(i * 256 + 128, 128), :] = odd
                b_bwd[k, pl.ds(0, 128), pl.ds((2 - i) * 256, 256)] = even
                b_bwd[k, pl.ds(128, 128), pl.ds((2 - i) * 256, 256)] = odd
            wo_d[k] = pair_diag(w_res[k]).astype(BF16)
        from_d[...] = pair_diag(w_from[0]).astype(BF16)
        for k in range(2):
            to_d[k] = pair_diag(w_to[k]).astype(BF16)
        up_d[...] = pair_diag(
            jnp.concatenate([w_from[k] for k in range(1, 5)], axis=1)
        ).astype(BF16)
        lane = lax.broadcasted_iota(jnp.int32, (128, 48), 0)
        tap = lax.broadcasted_iota(jnp.int32, (128, 48), 1)
        for k in range(2):
            low = w_pix[k].astype(BF16)
            for cp in range(2):
                pick = (lane == (tap // 12) * 24 + cp * 12 + tap % 12).astype(F32).astype(BF16)
                pix_d[k, :, pl.ds(cp * 128, 128)] = mm(pick, low).astype(BF16)
        for k in range(4):
            down_b[pl.ds(k * 128, 128), :] = w_down[k].astype(BF16)
        for k in range(2):
            full = book[k]
            hi = full.astype(BF16).astype(F32)
            mid = (full - hi).astype(BF16).astype(F32)
            lo = full - hi - mid
            empty = jnp.zeros_like(full)
            book_a[k] = jnp.concatenate([hi, mid, lo, empty], axis=1).astype(BF16)
            book_b[k] = jnp.concatenate([mid, hi, empty, lo], axis=1).astype(BF16)
        height = pix.shape[1]
        o = lax.broadcasted_iota(jnp.int32, (height, height), 0)
        s = lax.broadcasted_iota(jnp.int32, (height, height), 1)
        quarter = height // 4
        src = 8 * (o % rows) + 4 * ((o % quarter) // rows) + o // quarter
        sel[...] = (s == src).astype(F32).astype(BF16)

    def near_of(col, level):
        n = col.shape[0]
        codes = lax.broadcasted_iota(jnp.int32, (n, book.shape[1]), 1)
        v = []
        for cp, table in ((0, book_a), (1, book_b)):
            hot = (col[:, cp : cp + 1] == codes).astype(F32).astype(BF16)
            v.append(mm(hot, table[level]))
        half = low_half((n, 128))
        hi = jnp.where(half, v[0][:, :128], v[1][:, :128])
        mid = swap_halves(jnp.where(half, v[1][:, :128], v[0][:, :128]))
        lo = jnp.where(half, v[0][:, 128:], v[1][:, 128:])
        return hi, hi + mid + lo

    def top_codes(c0):
        hi, full = near_of(ct_col[0, pl.ds(c0 * rows, ch_t * rows), :], 0)
        near_t[pl.ds(c0 * rows, ch_t * rows), :] = full
        u = mm(hi.astype(BF16), up_d[...]).reshape(ch_t, rows, 1024)
        for cq in range(2):
            for rp in range(2):
                for c in range(ch_t):
                    at = (cq * 2 + rp) * 256
                    up[2 * (c0 + c) + cq, rp] = u[c, :, at : at + 256]

    loop(pairs_t, ch_t, top_codes)

    def put_slots(ref, c0, n, even, odd):
        ref[pl.ds(c0, n), 0] = shift_rows(odd, 1).astype(BF16)
        ref[pl.ds(c0, n), 1] = even.astype(BF16)
        ref[pl.ds(c0, n), 2] = odd.astype(BF16)
        ref[pl.ds(c0, n), 3] = shift_rows(even, -1).astype(BF16)

    def bottom_codes(c0):
        n = ch * 2 * rows
        hi, full = near_of(cb_col[0, pl.ds(c0 * 2 * rows, n), :], 1)
        near[pl.ds(c0 * 2 * rows, n), :] = full
        x = mm(hi.astype(BF16), from_d[...]).reshape(ch, 2, rows, 256) + up[pl.ds(c0, ch)]
        res[pl.ds(c0, ch)] = x
        put_slots(xs_dec, c0, ch, x[:, 0], x[:, 1])

    loop(pairs, ch, bottom_codes)

    def conv_wide(xs, k):
        def run(c0):
            for rp in range(2):
                taps = jnp.concatenate(
                    [flat(xs[pl.ds(c0, ch), rp + t]) for t in range(3)], axis=1
                )
                y = mm(taps, b_fwd[k])
                wide[pl.ds(c0 + 1, ch), rp] = y.reshape(ch, rows, 256)

        loop(pairs, ch, run)

    def gather_wide(c0, n, rp):
        before = wide[pl.ds(c0, n), rp, :, 128:]
        after = wide[pl.ds(c0 + 2, n), rp, :, 128:]
        return wide[pl.ds(c0 + 1, n), rp, :, :128] + jnp.where(low_half(before.shape), before, after)

    conv_wide(xs_dec, 2)

    def decode_out(c0):
        a = jnp.stack([gather_wide(c0, ch, rp) for rp in range(2)], axis=1)
        n = ch * 2 * rows
        a = a.reshape(n, 128)
        act_dec[pl.ds(c0 * 2 * rows, n), :] = a
        hidden = (a * sigmoid(a)).astype(BF16)
        y = res[pl.ds(c0, ch)].reshape(n, 256) + mm(hidden, wo_d[2])
        low = y.astype(BF16)
        low_dec[pl.ds(c0 * 2 * rows, n), :] = low
        resid[pl.ds(c0 * 2 * rows, n), :] = mm_t(low, pix_d[1])

    loop(pairs, ch, decode_out)

    per_tile = 2 * rows
    picked = mm(sel[...], pix[0])
    wide_px = pix.shape[2]
    lanes24 = lane_iota((per_tile, 128))
    for c2 in range(pairs):
        tile = jnp.zeros((per_tile, 128), F32)
        for i in range(4):
            start = 24 * c2
            want = 24 * i
            block = start // 128
            row = picked[i * per_tile : (i + 1) * per_tile]
            part = row[:, block * 128 : block * 128 + 128]
            part = pltpu.roll(part, (want - start % 128) % 128, 1)
            inside = min(24, 128 - start % 128)
            tile = jnp.where((lanes24 >= want) & (lanes24 < want + inside), part, tile)
            if inside < 24:
                part = row[:, block * 128 + 128 : block * 128 + 256]
                part = pltpu.roll(part, want + inside, 1)
                tile = jnp.where((lanes24 >= want + inside) & (lanes24 < want + 24), part, tile)
        patches[c2 * per_tile : (c2 + 1) * per_tile, :] = tile.astype(BF16)

    def stem_of(c0):
        n = ch * 2 * rows
        pre = mm(patches[pl.ds(c0 * 2 * rows, n), :], pix_d[0])
        s = (pre * sigmoid(pre)).astype(BF16)
        stem[pl.ds(c0, ch)] = s.reshape(ch, 2, rows, 256)

    loop(pairs, ch, stem_of)

    def top_in(c0):
        for cq in range(2):
            pieces = [stem[2 * (c0 + c) + cq, rp] for c in range(ch_t) for rp in range(2)]
            taps = jnp.concatenate(
                [jnp.concatenate(pieces[2 * c : 2 * c + 2], axis=1) for c in range(ch_t)], axis=0
            )
            x = mm(taps, down_b[...]).reshape(ch_t, rows, 128)
            grad_hi[pl.ds(c0, ch_t), 0, :, pl.ds(cq * 128, 128)] = x
            xs_top[pl.ds(c0, ch_t), 0, :, pl.ds(cq * 128, 128)] = shift_rows(x, 1).astype(BF16)
            xs_top[pl.ds(c0, ch_t), 1, :, pl.ds(cq * 128, 128)] = x.astype(BF16)
            xs_top[pl.ds(c0, ch_t), 2, :, pl.ds(cq * 128, 128)] = shift_rows(x, -1).astype(BF16)

    loop(pairs_t, ch_t, top_in)

    wide[pairs_t + 1, 0] = jnp.zeros((rows, 256), F32)

    def top_conv(c0):
        taps = jnp.concatenate([flat(xs_top[pl.ds(c0, ch_t), t]) for t in range(3)], axis=1)
        wide[pl.ds(c0 + 1, ch_t), 0] = mm(taps, b_fwd[0]).reshape(ch_t, rows, 256)

    loop(pairs_t, ch_t, top_conv)

    def add_num(x):
        acc_num[...] += jnp.sum(x.reshape(x.shape[0] // 8, 8, 128), axis=0)

    def top_out(c0):
        n = ch_t * rows
        here = pl.ds(c0 * rows, n)
        a = flat(gather_wide(c0, ch_t, 0))
        act_top[here, :] = a
        hidden = (a * sigmoid(a)).astype(BF16)
        y = flat(grad_hi[pl.ds(c0, ch_t), 0]) + mm(hidden, wo_d[0])
        low = y.astype(BF16)
        low_top[here, :] = low
        latent = mm(low, to_d[0])
        lat_t[here, :] = latent
        diff = latent - near_t[here, :]
        add_num(COMMIT_WEIGHT * diff * diff)

    loop(pairs_t, ch_t, top_out)

    def bottom_in(c0):
        x = stem[pl.ds(c0, ch)].astype(F32) + up[pl.ds(c0, ch)]
        res[pl.ds(c0, ch)] = x
        put_slots(xs_bot, c0, ch, x[:, 0], x[:, 1])

    loop(pairs, ch, bottom_in)
    conv_wide(xs_bot, 1)

    def bottom_out(c0):
        n = ch * 2 * rows
        here = pl.ds(c0 * 2 * rows, n)
        a = jnp.stack([gather_wide(c0, ch, rp) for rp in range(2)], axis=1).reshape(n, 128)
        act_bot[here, :] = a
        hidden = (a * sigmoid(a)).astype(BF16)
        y = res[pl.ds(c0, ch)].reshape(n, 256) + mm(hidden, wo_d[1])
        low = y.astype(BF16)
        low_bot[here, :] = low
        latent = mm(low, to_d[1])
        lat[here, :] = latent
        diff = latent - near[here, :]
        add_num(COMMIT_WEIGHT * diff * diff)

    loop(pairs, ch, bottom_out)

    def level_stats(level, lat_ref, row_ref, total):
        size = 256

        def run(p0):
            latent = lat_ref[pl.ds(p0, size), :]
            hi = latent.astype(BF16)
            lo = (latent - hi.astype(F32)).astype(BF16)
            both = jnp.concatenate([hi, lo], axis=1)
            codes = lax.broadcasted_iota(jnp.int32, (book.shape[1], size), 0)
            half = low_half((book.shape[1], 128))
            parts = []
            for cp in range(2):
                hot = (row_ref[0, cp : cp + 1, pl.ds(p0, size)] == codes).astype(F32)
                acc_count[level] += hot[:, :128] + hot[:, 128:]
                s = mm(hot.astype(BF16), both)
                parts.append(s[:, :128] + s[:, 128:])
            acc_sums[level] += jnp.where(half, parts[0], parts[1])

        loop(total, size, run)

    level_stats(0, lat_t, ct_row, pairs_t * rows)
    level_stats(1, lat, cb_row, pairs * 2 * rows)

    micro = place[0] + step
    image = place[1]
    images = valid_s.shape[1]
    for level, lat_ref in ((0, lat_t), (1, lat)):
        side = pairs * (level + 1)
        for r in range(8):
            pos = dead_source[level, r]
            col = lax.rem(pos, side)
            row_all = lax.div(pos, side)
            row = lax.rem(row_all, side)
            img_all = lax.div(row_all, side)
            mine = (lax.rem(img_all, images) == image) & (lax.div(img_all, images) == micro)
            if level == 0:
                local = lax.div(col, 2) * rows + row
            else:
                local = lax.div(col, 2) * (2 * rows) + lax.rem(row, 2) * rows + lax.div(row, 2)
            line = lat_ref[pl.ds(local, 1), :]
            odd = lax.rem(col, 2)
            line = jnp.where(low_half(line.shape) == (odd == 0), line, 0.0)
            line = line + swap_halves(line)
            line = jnp.where(low_half(line.shape) == (level == 0), line, 0.0)
            acc_dead[pl.ds(r, 1), :] += line * mine.astype(F32)

    limit = valid_s[micro, image]

    def decode_back(c0):
        n = ch * 2 * rows
        here = pl.ds(c0 * 2 * rows, n)
        lane = lane_iota((ch, 2, rows, 128))
        pixel_row = (
            8 * lax.broadcasted_iota(jnp.int32, lane.shape, 2)
            + 4 * lax.broadcasted_iota(jnp.int32, lane.shape, 1)
            + lane // 24
        )
        keep = ((pixel_row < limit) & (lane < 96)).astype(F32).reshape(n, 128)
        p = patches[here, :]
        diff = keep * (resid[here, :] - p.astype(F32))
        add_num(diff * diff)
        g_re = (loss_slope * diff).astype(BF16)
        acc_pix[1] += mm_w(g_re, low_dec[here, :])
        g = mm(g_re, pix_d[1])
        grad_hi[pl.ds(c0, ch)] = g.reshape(ch, 2, rows, 256)
        res_back(g, act_dec[here, :], 2, c0)

    def res_back(g, a, k, c0):
        n = ch * 2 * rows
        g_low = g.astype(BF16)
        s = sigmoid(a)
        hidden = (a * s).astype(BF16)
        acc_res[k] += mm_w(hidden, g_low)
        d = (mm_t(g_low, wo_d[k]) * (s * (1.0 + a * (1.0 - s)))).astype(BF16)
        d_two[pl.ds(c0 + 1, ch)] = d.astype(F32).reshape(ch, 2, rows, 128)

    def conv_back(k, xs, c0):
        outs = []
        total = None
        here = d_two[pl.ds(c0 + 1, ch)]
        before = d_two[pl.ds(c0, ch)]
        after = d_two[pl.ds(c0 + 2, ch)]
        d = jnp.concatenate([here, jnp.where(low_half(here.shape), after, before)], axis=3)
        put_slots(d_slots, c0, ch, d[:, 0], d[:, 1])
        for rp in range(2):
            taps = jnp.concatenate(
                [flat(d_slots[pl.ds(c0, ch), rp + t]) for t in range(3)], axis=1
            )
            outs.append(mm_t(taps, b_bwd[k]).reshape(ch, rows, 256))
            part = mm_w(flat(xs[pl.ds(c0, ch), rp + 1]), taps)
            total = part if total is None else total + part
        acc_conv[k] += total
        return jnp.stack(outs, axis=1)

    loop(pairs, ch, decode_back)

    def decode_in_back(c0):
        n = ch * 2 * rows
        here = pl.ds(c0 * 2 * rows, n)
        g = grad_hi[pl.ds(c0, ch)] + conv_back(2, xs_dec, c0)
        gup[pl.ds(c0, ch)] = g
        g_low = g.reshape(n, 256).astype(BF16)
        full = near[here, :]
        acc_from[...] += mm_w(full.astype(BF16), g_low)
        g_lat = mm_t(g_low, from_d[...]) + commit_slope * (lat[here, :] - full)
        g_lat = g_lat.astype(BF16)
        acc_to[1] += mm_w(low_bot[here, :], g_lat)
        grad_hi[pl.ds(c0, ch)] = mm_t(g_lat, to_d[1]).reshape(ch, 2, rows, 256)

    loop(pairs, ch, decode_in_back)

    def bottom_back(c0):
        n = ch * 2 * rows
        res_back(
            grad_hi[pl.ds(c0, ch)].reshape(n, 256), act_bot[pl.ds(c0 * 2 * rows, n), :], 1, c0
        )

    loop(pairs, ch, bottom_back)

    def bottom_in_back(c0):
        g = grad_hi[pl.ds(c0, ch)] + conv_back(1, xs_bot, c0)
        gstem[pl.ds(c0, ch)] = g.astype(BF16)
        total = (g + gup[pl.ds(c0, ch)]).astype(BF16)
        half = ch // 2
        total = total.reshape(half, 2, 2, rows, 256)
        wide_g = jnp.concatenate(
            [total[:, cq, rp].reshape(half * rows, 256) for cq in range(2) for rp in range(2)],
            axis=1,
        )
        t0 = pl.multiple_of(lax.div(c0, 2) * rows, half * rows)
        here = pl.ds(t0, half * rows)
        full = near_t[here, :]
        acc_up[...] += mm_w(full.astype(BF16), wide_g)
        g_q = mm_t(wide_g, up_d[...]).astype(BF16).astype(F32)
        g_lat = (g_q + commit_slope * (lat_t[here, :] - full)).astype(BF16)
        acc_to[0] += mm_w(low_top[here, :], g_lat)
        g_top = mm_t(g_lat, to_d[0])
        grad_lo[here, :] = g_top
        g_low = g_top.astype(BF16)
        a = act_top[here, :]
        s = sigmoid(a)
        acc_res[0] += mm_w((a * s).astype(BF16), g_low)
        d = (mm_t(g_low, wo_d[0]) * (s * (1.0 + a * (1.0 - s)))).astype(BF16)
        d_two_t[pl.ds(lax.div(c0, 2) + 1, half)] = d.astype(F32).reshape(half, rows, 128)

    loop(pairs, ch, bottom_in_back)

    def top_back(c0):
        n = ch_t * rows
        here = d_two_t[pl.ds(c0 + 1, ch_t)]
        before = d_two_t[pl.ds(c0, ch_t)]
        after = d_two_t[pl.ds(c0 + 2, ch_t)]
        d = jnp.concatenate([here, jnp.where(low_half(here.shape), after, before)], axis=2)
        taps = jnp.concatenate(
            [
                flat(shift_rows(d, 1)).astype(BF16),
                flat(d).astype(BF16),
                flat(shift_rows(d, -1)).astype(BF16),
            ],
            axis=1,
        )
        acc_conv[0] += mm_w(flat(xs_top[pl.ds(c0, ch_t), 1]), taps)
        g = grad_lo[pl.ds(c0 * rows, n), :] + mm_t(taps, b_bwd[0])
        g_low = g.astype(BF16).reshape(ch_t, rows, 256)
        for cq in range(2):
            g_cq = flat(g_low[:, :, cq * 128 : cq * 128 + 128])
            pieces = [stem[2 * (c0 + c) + cq, rp] for c in range(ch_t) for rp in range(2)]
            taps_s = jnp.concatenate(
                [jnp.concatenate(pieces[2 * c : 2 * c + 2], axis=1) for c in range(ch_t)], axis=0
            )
            acc_down[...] += mm_w(taps_s, g_cq)
            g_st = mm_t(g_cq, down_b[...]).reshape(ch_t, rows, 512)
            for c in range(ch_t):
                col = 2 * (c0 + c) + cq
                p = patches[pl.ds(pl.multiple_of(col * 2 * rows, 2 * rows), 2 * rows), :]
                sl = slope(mm(p, pix_d[0]))
                g_t = jnp.concatenate([g_st[c, :, :256], g_st[c, :, 256:]], axis=0)
                g_b = gstem[col].reshape(2 * rows, 256).astype(F32)
                both = jnp.concatenate([(g_t * sl).astype(BF16), (g_b * sl).astype(BF16)], axis=0)
                acc_pix[0] += mm_w(jnp.concatenate([p, p], axis=0), both)

    loop(pairs_t, ch_t, top_back)

    @pl.when(step == last)
    def _():
        half = low_half((128, 128))
        zero = jnp.zeros((128, 128), F32)

        def to_sum(k):
            return acc_to[k, :128, :] + swap_halves(acc_to[k, 128:, :])

        for k in range(3):
            twos = []
            for i in range(3):
                lanes = (2 - i) * 256
                e0 = acc_conv[k, :128, lanes : lanes + 128]
                e1 = acc_conv[k, :128, lanes + 128 : lanes + 256]
                o0 = acc_conv[k, 128:, lanes : lanes + 128]
                o1 = acc_conv[k, 128:, lanes + 128 : lanes + 256]
                first = e0 + swap_halves(jnp.where(half, o1, o0))
                out[k * CONV_ROWS + i * 128 : k * CONV_ROWS + i * 128 + 128, :] = first
                twos.append(o0 + swap_halves(e1))
            base = k * CONV_ROWS + 384
            out[base : base + 128, :] = jnp.where(half, twos[0], swap_halves(twos[1]))
            other = swap_halves(to_sum(k)) if k < 2 else zero
            out[base + 128 : base + 256, :] = jnp.where(half, twos[2], other)
            out[ROW_RES + k * 64 : ROW_RES + k * 64 + 64, :] = (
                acc_res[k, :64, :128] + acc_res[k, 64:, 128:]
            )
        out[ROW_FROM : ROW_FROM + 64, :] = acc_from[:64, :128] + acc_from[64:, 128:]
        for k in range(4):
            out[ROW_FROM + (k + 1) * 64 : ROW_FROM + (k + 2) * 64, :] = (
                acc_up[:64, k * 128 : k * 128 + 128] + acc_up[64:, 512 + k * 128 : 640 + k * 128]
            )
        for k in range(2):
            for i in range(4):
                even = acc_pix[k, 24 * i : 24 * i + 12, :128]
                odd = acc_pix[k, 24 * i + 12 : 24 * i + 24, 128:]
                at = ROW_PIXEL + k * 48 + i * 12
                out[at : at + 12, :] = even + odd
        out[ROW_DOWN : ROW_DOWN + 512, :] = acc_down[...]
        top = acc_sums[0] + swap_halves(acc_sums[0])
        bottom = acc_sums[1] + swap_halves(acc_sums[1])
        out[ROW_SUMS : ROW_SUMS + 512, :] = jnp.where(low_half(top.shape), top, bottom)
        same = lax.broadcasted_iota(jnp.int32, (128, 128), 0) == lane_iota((128, 128))
        for level in range(2):
            for b in range(4):
                col = jnp.sum(acc_count[level, b * 128 : b * 128 + 128, :], axis=1, keepdims=True)
                line = jnp.sum(jnp.where(same, col, 0.0), axis=0, keepdims=True)
                at = ROW_COUNT + level * 4 + b
                out[at : at + 1, :] = line
        out[ROW_DEAD : ROW_DEAD + 8, :] = acc_dead[...]
        out[ROW_NUMER : ROW_NUMER + 8, :] = acc_num[...]
        if out.shape[0] > ROW_END:
            out[ROW_END:, :] = jnp.zeros((out.shape[0] - ROW_END, 128), F32)


def compute(place, valid_rows, dead_source, pix, ct, cb, weights, book, total_rows):
    share, height, _ = pix.shape
    pairs = height // 8
    rows = height // 8
    pairs_t = pairs // 2
    n = pairs * 2 * rows
    n_t = pairs_t * rows
    ct_col, ct_row = ct
    cb_col, cb_row = cb
    smem = pl.BlockSpec(memory_space=pltpu.SMEM)

    def whole(x):
        zeros = (0,) * len(x.shape)
        return pl.BlockSpec(x.shape, lambda i: zeros)

    def each(x):
        zeros = (0,) * (len(x.shape) - 1)
        return pl.BlockSpec((1,) + x.shape[1:], lambda i: (i,) + zeros)

    v = pltpu.VMEM
    scratch = [
        v((3, 768, 256), BF16),
        v((3, 256, 768), BF16),
        v((3, 128, 256), BF16),
        v((128, 256), BF16),
        v((2, 256, 128), BF16),
        v((128, 1024), BF16),
        v((2, 128, 256), BF16),
        v((512, 128), BF16),
        v((2, 512, 256), BF16),
        v((2, 512, 256), BF16),
        v((height, height), BF16),
        v((n, 128), BF16),
        v((pairs, 2, rows, 256), BF16),
        v((pairs, 2, rows, 256), F32),
        v((n, 128), F32),
        v((n_t, 128), F32),
        v((pairs, 4, rows, 256), BF16),
        v((pairs, 4, rows, 256), BF16),
        v((pairs_t, 3, rows, 256), BF16),
        v((pairs + 2, 2, rows, 256), F32),
        v((pairs, 2, rows, 256), F32),
        v((n, 128), F32),
        v((n, 128), F32),
        v((n_t, 128), F32),
        v((n, 256), BF16),
        v((n, 256), BF16),
        v((n_t, 256), BF16),
        v((n, 128), F32),
        v((n_t, 128), F32),
        v((n, 128), F32),
        v((pairs, 2, rows, 256), F32),
        v((n_t, 256), F32),
        v((pairs + 2, 2, rows, 128), F32),
        v((pairs, 4, rows, 256), BF16),
        v((pairs_t + 2, rows, 128), F32),
        v((8, 128), BF16),
        v((pairs, 2, rows, 256), BF16),
        v((pairs, 2, rows, 256), F32),
        v((3, 256, 768), F32),
        v((3, 128, 256), F32),
        v((128, 256), F32),
        v((128, 1024), F32),
        v((2, 256, 128), F32),
        v((2, 128, 256), F32),
        v((512, 128), F32),
        v((2, 512, 128), F32),
        v((2, 512, 128), F32),
        v((8, 128), F32),
        v((8, 128), F32),
    ]
    return pl.pallas_call(
        compute_kernel,
        grid=(share,),
        out_shape=jax.ShapeDtypeStruct((total_rows, 128), F32),
        in_specs=[smem, smem, smem, whole(valid_rows), each(pix), each(ct_col), each(cb_col), each(ct_row), each(cb_row)]
        + [whole(w) for w in weights]
        + [whole(book)],
        out_specs=pl.BlockSpec((total_rows, 128), lambda i: (0, 0)),
        scratch_shapes=scratch,
        compiler_params=pltpu.CompilerParams(
            dimension_semantics=("arbitrary",), vmem_limit_bytes=VMEM_LIMIT
        ),
        name="step_compute",
    )(place, valid_rows, dead_source, valid_rows, pix, ct_col, cb_col, ct_row, cb_row, *weights, book)


def update_kernel(dead_codes, valid_v, total, *refs):
    w, m, v = refs[0:6], refs[6:12], refs[12:18]
    ema_count, ema_sum = refs[18:20]
    norm_o, pair_o = refs[20:22]
    new_o, mom_o, sec_o, low_o = refs[22:28], refs[28:34], refs[34:40], refs[40:46]
    book_o, count_o, sum_o = refs[46:49]
    grads = total[0:ROW_SUMS, :]
    squares = jnp.sum(jnp.sum((grads * grads).reshape(ROW_SUMS // 8, 8, 128), axis=0))
    norm = jnp.sqrt(jnp.full((8, 128), squares, F32))
    norm_o[0] = norm[0, 0]
    factor = (CLIP_NORM / jnp.maximum(norm, CLIP_NORM))[0, 0]
    pair_o[0] = jnp.sum(total[ROW_NUMER : ROW_NUMER + 8, :])
    pair_o[1] = 3.0 * 256.0 * jnp.sum(valid_v[...].astype(F32))

    def apply(t, index, grad):
        g = grad * factor
        first = MOMENT_ONE * m[t][index] + (1.0 - MOMENT_ONE) * g
        second = MOMENT_TWO * v[t][index] + (1.0 - MOMENT_TWO) * g * g
        step = first / (1.0 - MOMENT_ONE**STEP) / (
            jnp.sqrt(second / (1.0 - MOMENT_TWO**STEP)) + ADAM_EPSILON
        )
        weight = w[t][index]
        fresh = weight - LEARN_RATE * (step + WEIGHT_DECAY * weight)
        new_o[t][index] = fresh
        mom_o[t][index] = first
        sec_o[t][index] = second
        low_o[t][index] = fresh.astype(BF16)

    for k in range(3):
        base = k * CONV_ROWS
        for i in range(3):
            both = total[base + i * 128 : base + i * 128 + 128, :]
            apply(0, (k, pl.ds((i * 3 + 1) * 128, 128)), both[:, :64])
            apply(0, (k, pl.ds(i * 3 * 128, 128)), swap_halves(both)[:, :64])
        both = total[base + 384 : base + 512, :]
        apply(0, (k, pl.ds(2 * 128, 128)), both[:, :64])
        apply(0, (k, pl.ds(5 * 128, 128)), swap_halves(both)[:, :64])
        both = total[base + 512 : base + 640, :]
        apply(0, (k, pl.ds(8 * 128, 128)), both[:, :64])
        if k < 2:
            apply(3, (k,), swap_halves(both)[:, :64])
        apply(1, (k,), total[ROW_RES + k * 64 : ROW_RES + k * 64 + 64, :])
    for k in range(5):
        apply(2, (k,), total[ROW_FROM + k * 64 : ROW_FROM + k * 64 + 64, :])
    for k in range(2):
        apply(4, (k,), total[ROW_PIXEL + k * 48 : ROW_PIXEL + k * 48 + 48, :])
    for k in range(4):
        apply(5, (k,), total[ROW_DOWN + k * 128 : ROW_DOWN + k * 128 + 128, :])

    same = lax.broadcasted_iota(jnp.int32, (128, 128), 0) == lane_iota((128, 128))
    sums = total[ROW_SUMS : ROW_SUMS + 512, :]
    dead = total[ROW_DEAD : ROW_DEAD + 8, :]
    for level in range(2):
        mine = (sums if level == 0 else swap_halves(sums))[:, :64]
        lines = (dead if level == 0 else swap_halves(dead))[:, :64]
        sum_o[level] = CODE_DECAY * ema_sum[level] + (1.0 - CODE_DECAY) * mine
        for r in range(8):
            sum_o[level, pl.ds(dead_codes[level, r], 1), :] = lines[r : r + 1]
        for b in range(4):
            at = ROW_COUNT + level * 4 + b
            used = total[at : at + 1, :]
            count = CODE_DECAY * ema_count[level : level + 1, b * 128 : b * 128 + 128] + (
                1.0 - CODE_DECAY
            ) * used
            ids = lane_iota((1, 128)) + b * 128
            for r in range(8):
                count = jnp.where(ids == dead_codes[level, r], 1.0, count)
            count_o[level : level + 1, b * 128 : b * 128 + 128] = count
            col = jnp.sum(jnp.where(same, count, 0.0), axis=1, keepdims=True)
            book_o[level, b * 128 : b * 128 + 128, :] = (
                sum_o[level, b * 128 : b * 128 + 128, :] / col
            )


def update(dead_codes, valid_rows, total, weights, firsts, seconds, ema_count, ema_sum):
    sds = jax.ShapeDtypeStruct
    shapes = [sds((1,), F32), sds((2,), F32)]
    for _ in range(3):
        shapes += [sds(w.shape, F32) for w in weights]
    shapes += [sds(w.shape, BF16) for w in weights]
    shapes += [sds(ema_sum.shape, F32), sds(ema_count.shape, F32), sds(ema_sum.shape, F32)]
    vm = pl.BlockSpec(memory_space=pltpu.VMEM)
    sm = pl.BlockSpec(memory_space=pltpu.SMEM)
    return pl.pallas_call(
        update_kernel,
        out_shape=shapes,
        in_specs=[sm] + [vm] * 22,
        out_specs=[sm, sm] + [vm] * 27,
        compiler_params=pltpu.CompilerParams(vmem_limit_bytes=VMEM_LIMIT),
        name="step_update",
    )(dead_codes, valid_rows, total, *weights, *firsts, *seconds, ema_count, ema_sum)


def body(sections, devices, *args):
    pixels, codes_top, codes_bottom, valid_rows, dead_codes, dead_source = args[:6]
    weights, firsts, seconds = args[6:12], args[12:18], args[18:24]
    codebook, ema_count, ema_sum = args[24:27]
    batches, part_rows, lanes = pixels.shape
    height = lanes // 3
    parts = height // part_rows
    share = batches // (sections * parts)
    section = lax.axis_index("section")
    device = lax.axis_index("dp")
    part = device % parts
    image = device // parts

    def regroup(x):
        pieces = []
        for k in range(parts):
            target = (part + k) % parts
            piece = lax.dynamic_slice_in_dim(x, (section * parts + target) * share, share, 0)
            if k > 0:
                pairs = [
                    (base + p, base + (p + k) % parts)
                    for base in range(0, devices, parts)
                    for p in range(parts)
                ]
                piece = lax.ppermute(piece, "dp", pairs)
            pieces.append(piece)
        ordered = [lax.select_n((part - p) % parts, *pieces) if parts == 2 else None for p in range(parts)]
        return jnp.stack(ordered, axis=1).reshape(share, parts * x.shape[1], x.shape[2])

    def code_layouts(codes, level):
        side = codes.shape[1]
        if level == 0:
            x = codes.reshape(share, side, side // 2, 2)
            col = x.transpose(0, 2, 1, 3).reshape(share, side * side // 2, 2)
            row = x.transpose(0, 3, 2, 1).reshape(share, 2, side * side // 2)
        else:
            x = codes.reshape(share, side // 2, 2, side // 2, 2)
            col = x.transpose(0, 3, 2, 1, 4).reshape(share, side * side // 2, 2)
            row = x.transpose(0, 4, 3, 2, 1).reshape(share, 2, side * side // 2)
        return col, row

    ct = code_layouts(regroup(codes_top), 0)
    cb = code_layouts(regroup(codes_bottom), 1)
    pix = regroup(pixels)
    place = jnp.stack([(section * parts + part) * share, image]).astype(jnp.int32)
    multiple = 8 * sections * devices
    total_rows = -(-ROW_END // multiple) * multiple
    packed = compute(place, valid_rows, dead_source, pix, ct, cb, weights, codebook, total_rows)
    total = lax.psum(packed, ("section", "dp"))
    outs = update(dead_codes, valid_rows, total, weights, firsts, seconds, ema_count, ema_sum)
    return (outs[0].reshape(()),) + tuple(outs[1:])


def solution(mesh):
    return jax.shard_map(
        functools.partial(body, mesh.shape["section"], mesh.shape["dp"]),
        mesh=mesh,
        in_specs=(P(None, "dp", None),) * 3 + (P(),) * 24,
        out_specs=(P(),) * 29,
        check_vma=False,
    )
```

```python
import functools

import jax
import jax.numpy as jnp
from jax import lax
from jax.experimental import pallas as pl
from jax.experimental.pallas import tpu as pltpu
from jax.sharding import PartitionSpec as P

STEP = 10
COMMIT_WEIGHT = 0.25
CODE_DECAY = 0.9
CLIP_NORM = 0.001
LEARN_RATE = 0.03
MOMENT_ONE = 0.9
MOMENT_TWO = 0.999
WEIGHT_DECAY = 0.01
ADAM_EPSILON = 1e-08

F32 = jnp.float32
BF16 = jnp.bfloat16
VMEM_LIMIT = 56 * 1024 * 1024
CHUNK = 8

TAP_ROWS = 64
CONV_ROWS = 9 * TAP_ROWS
ROW_RES = 3 * CONV_ROWS
ROW_FROM = ROW_RES + 3 * 64
ROW_TO = ROW_FROM + 5 * 64
ROW_PIXEL = ROW_TO + 2 * 64
ROW_DOWN = ROW_PIXEL + 2 * 48
ROW_SUMS = ROW_DOWN + 512
ROW_COUNT = ROW_SUMS + 512
ROW_DEAD = ROW_COUNT + 8
ROW_NUMER = ROW_DEAD + 8
ROW_END = ROW_NUMER + 8


def mm(x, w):
    return lax.dot_general(x, w, (((1,), (0,)), ((), ())), preferred_element_type=F32)


def mm_t(x, w):
    return lax.dot_general(x, w, (((1,), (1,)), ((), ())), preferred_element_type=F32)


def mm_w(x, g):
    return lax.dot_general(x, g, (((0,), (0,)), ((), ())), preferred_element_type=F32)


def lane_iota(shape):
    return lax.broadcasted_iota(jnp.int32, shape, len(shape) - 1)


def low_half(shape):
    return lane_iota(shape) % 128 < 64


def sigmoid(x):
    return 0.5 * jnp.tanh(0.5 * x) + 0.5


def slope(a):
    s = sigmoid(a)
    return s * (1.0 + a * (1.0 - s))


def shift_rows(x, by):
    rows = x.shape[1]
    moved = pltpu.roll(x, by % rows, 1)
    ids = lax.broadcasted_iota(jnp.int32, x.shape, 1)
    edge = 0 if by == 1 else rows - 1
    return jnp.where(ids == edge, 0.0, moved)


def flat(x):
    return x.reshape(x.shape[0] * x.shape[1], x.shape[2])


def pair_diag(w):
    zero = jnp.zeros_like(w)
    return jnp.concatenate(
        [jnp.concatenate([w, zero], axis=1), jnp.concatenate([zero, w], axis=1)], axis=0
    )


def swap_halves(x):
    return pltpu.roll(x, 64, len(x.shape) - 1)


def compute_kernel(
    place,
    valid_s,
    dead_source,
    valid_v,
    pix,
    pix_far,
    ct_near,
    ct_far,
    cb_near,
    cb_far,
    w_conv,
    w_res,
    w_from,
    w_to,
    w_pix,
    w_down,
    book,
    out,
    b_fwd,
    b_bwd,
    wo_d,
    from_d,
    to_d,
    up_d,
    pix_d,
    down_b,
    book_a,
    book_b,
    sel,
    hot_t,
    hot_b,
    patches,
    stem,
    up,
    near,
    near_t,
    xs_dec,
    xs_bot,
    xs_top,
    wide,
    res,
    act_dec,
    act_bot,
    act_top,
    low_dec,
    low_bot,
    low_top,
    lat,
    lat_t,
    resid,
    grad_hi,
    grad_lo,
    d_two,
    d_slots,
    d_two_t,
    d_slots_t,
    gstem,
    gup,
    acc_conv,
    acc_res,
    acc_from,
    acc_up,
    acc_to,
    acc_pix,
    acc_down,
    acc_sums,
    acc_count,
    acc_dead,
    acc_num,
):
    step = pl.program_id(0)
    last = pl.num_programs(0) - 1
    pairs, rows = xs_bot.shape[0], xs_bot.shape[2]
    pairs_t = xs_top.shape[0]
    ch = CHUNK
    ch_t = CHUNK // 2
    height = 2 * pix.shape[1]
    valid_count = 3.0 * height * jnp.sum(valid_v[...].astype(F32))
    loss_slope = 2.0 / valid_count
    commit_slope = loss_slope * COMMIT_WEIGHT

    def loop(total, size, fn):
        def run(k, _):
            fn(pl.multiple_of(k * size, size))
            return 0

        lax.fori_loop(0, total // size, run, 0)

    def picker(src, start):
        size = src.shape[0]
        at = lax.broadcasted_iota(jnp.int32, src.shape, 1) + start
        at = jnp.where(at >= size, at - size, at)
        return (at == src).astype(F32).astype(BF16)

    @pl.when(step == 0)
    def _():
        for ref in (acc_conv, acc_res, acc_from, acc_up, acc_to, acc_pix, acc_down, acc_sums, acc_count, acc_dead, acc_num):
            ref[...] = jnp.zeros(ref.shape, F32)
        wide[...] = jnp.zeros(wide.shape, F32)
        d_two[...] = jnp.zeros(d_two.shape, F32)
        d_two_t[...] = jnp.zeros(d_two_t.shape, F32)
        zero = jnp.zeros((64, 128), F32)
        for k in range(3):
            for i in range(3):
                t = [w_conv[k, :, pl.ds((i * 3 + j) * 128, 128)] for j in range(3)]
                even = jnp.concatenate([t[1], t[0], zero, t[2]], axis=0).astype(BF16)
                odd = jnp.concatenate([t[2], t[1], t[0], zero], axis=0).astype(BF16)
                both = jnp.concatenate([even, odd], axis=1)
                b_fwd[k, :, pl.ds(i * 256, 256)] = both
                b_bwd[k, pl.ds((2 - i) * 256, 256), :] = both
            wo_d[k] = pair_diag(w_res[k]).astype(BF16)
        from_d[...] = pair_diag(w_from[0]).astype(BF16)
        for k in range(2):
            to_d[k] = pair_diag(w_to[k]).astype(BF16)
        up_d[...] = pair_diag(
            jnp.concatenate([w_from[k] for k in range(1, 5)], axis=1)
        ).astype(BF16)
        lane = lax.broadcasted_iota(jnp.int32, (128, 48), 0)
        tap = lax.broadcasted_iota(jnp.int32, (128, 48), 1)
        for k in range(2):
            low = w_pix[k].astype(BF16)
            for cp in range(2):
                pick = (lane == (tap // 12) * 24 + cp * 12 + tap % 12).astype(F32).astype(BF16)
                pix_d[k, :, pl.ds(cp * 128, 128)] = mm(pick, low).astype(BF16)
        for k in range(4):
            down_b[pl.ds(k * 128, 128), :] = w_down[k].astype(BF16)
        for k in range(2):
            full = book[k]
            hi = full.astype(BF16).astype(F32)
            mid = (full - hi).astype(BF16).astype(F32)
            lo = full - hi - mid
            empty = jnp.zeros_like(full)
            book_a[k] = jnp.concatenate([hi, mid, lo, empty], axis=0).astype(BF16)
            book_b[k] = jnp.concatenate([mid, hi, empty, lo], axis=0).astype(BF16)
        o = lax.broadcasted_iota(jnp.int32, (height, height), 0)
        quarter = height // 4
        src = 8 * (o % rows) + 4 * ((o % quarter) // rows) + o // quarter
        sel[...] = picker(src, place[2] * (height // 2))

    def codes_of(near_ref, far_ref, split):
        both = jnp.concatenate([near_ref[0], far_ref[0]], axis=0).astype(F32)
        size = both.shape[0]
        o = lax.broadcasted_iota(jnp.int32, (size, size), 0)
        src = 2 * (o % rows) + o // rows if split else o
        pick = picker(src, place[2] * (size // 2))
        high = jnp.floor(both * (1.0 / 256.0))
        low = both - 256.0 * high
        codes = 256.0 * mm(pick, high.astype(BF16)) + mm(pick, low.astype(BF16))
        pad = jnp.zeros((size, 128 - size), F32)
        return jnp.concatenate([codes, pad], axis=1)

    codes_t = codes_of(ct_near, ct_far, False)
    codes_b = codes_of(cb_near, cb_far, True)

    def near_of(codes, level, c0, n, hot_ref):
        size = codes.shape[0]
        here = pl.ds(pl.multiple_of(c0 * size, size), n * size)
        moved = pltpu.roll(codes, lax.rem(128 - 2 * c0, 128), 1)
        ids = lax.broadcasted_iota(jnp.int32, (size, 512), 1).astype(F32)
        v = []
        used = jnp.zeros((8, 512), F32)
        for cp, table in ((0, book_a), (1, book_b)):
            for j in range(n):
                hot = (moved[:, 2 * j + cp : 2 * j + cp + 1] == ids).astype(F32)
                used = used + jnp.sum(hot.reshape(size // 8, 8, 512), axis=0)
                at = pl.ds(pl.multiple_of((c0 + j) * size, size), size)
                hot_ref[at, pl.ds(cp * 512, 512)] = hot.astype(BF16)
            v.append(mm_t(hot_ref[here, pl.ds(cp * 512, 512)], table[level]))
        acc_count[level] += used
        half = low_half((n * size, 128))
        hi = jnp.where(half, v[0][:, :128], v[1][:, :128])
        mid = swap_halves(jnp.where(half, v[1][:, :128], v[0][:, :128]))
        lo = jnp.where(half, v[0][:, 128:], v[1][:, 128:])
        return hi, hi + mid + lo

    def top_codes(c0):
        hi, full = near_of(codes_t, 0, c0, ch_t, hot_t)
        near_t[pl.ds(c0 * rows, ch_t * rows), :] = full
        u = mm(hi.astype(BF16), up_d[...]).reshape(ch_t, rows, 1024)
        for cq in range(2):
            for rp in range(2):
                for c in range(ch_t):
                    at = (cq * 2 + rp) * 256
                    up[2 * (c0 + c) + cq, rp] = u[c, :, at : at + 256]

    loop(pairs_t, ch_t, top_codes)

    def put_slots(ref, c0, n, even, odd):
        ref[pl.ds(c0, n), 0] = shift_rows(odd, 1).astype(BF16)
        ref[pl.ds(c0, n), 1] = even.astype(BF16)
        ref[pl.ds(c0, n), 2] = odd.astype(BF16)
        ref[pl.ds(c0, n), 3] = shift_rows(even, -1).astype(BF16)

    def bottom_codes(c0):
        n = ch * 2 * rows
        hi, full = near_of(codes_b, 1, c0, ch, hot_b)
        near[pl.ds(c0 * 2 * rows, n), :] = full
        x = mm(hi.astype(BF16), from_d[...]).reshape(ch, 2, rows, 256) + up[pl.ds(c0, ch)]
        res[pl.ds(c0, ch)] = x
        put_slots(xs_dec, c0, ch, x[:, 0], x[:, 1])

    loop(pairs, ch, bottom_codes)

    def conv_wide(xs, k):
        def run(c0):
            for rp in range(2):
                taps = jnp.concatenate(
                    [flat(xs[pl.ds(c0, ch), rp + t]) for t in range(3)], axis=1
                )
                y = mm_t(taps, b_fwd[k])
                wide[pl.ds(c0 + 1, ch), rp] = y.reshape(ch, rows, 256)

        loop(pairs, ch, run)

    def gather_wide(c0, n, rp):
        before = wide[pl.ds(c0, n), rp, :, 128:]
        after = wide[pl.ds(c0 + 2, n), rp, :, 128:]
        return wide[pl.ds(c0 + 1, n), rp, :, :128] + jnp.where(low_half(before.shape), before, after)

    conv_wide(xs_dec, 2)

    def decode_out(c0):
        a = jnp.stack([gather_wide(c0, ch, rp) for rp in range(2)], axis=1)
        n = ch * 2 * rows
        a = a.reshape(n, 128)
        act_dec[pl.ds(c0 * 2 * rows, n), :] = a
        hidden = (a * sigmoid(a)).astype(BF16)
        y = res[pl.ds(c0, ch)].reshape(n, 256) + mm(hidden, wo_d[2])
        low = y.astype(BF16)
        low_dec[pl.ds(c0 * 2 * rows, n), :] = low
        resid[pl.ds(c0 * 2 * rows, n), :] = mm_t(low, pix_d[1])

    loop(pairs, ch, decode_out)

    per_tile = 2 * rows
    picked = mm(sel[...], jnp.concatenate([pix[0], pix_far[0]], axis=0))
    lanes24 = lane_iota((per_tile, 128))
    for c2 in range(pairs):
        tile = jnp.zeros((per_tile, 128), F32)
        for i in range(4):
            start = 24 * c2
            want = 24 * i
            block = start // 128
            row = picked[i * per_tile : (i + 1) * per_tile]
            part = row[:, block * 128 : block * 128 + 128]
            part = pltpu.roll(part, (want - start % 128) % 128, 1)
            inside = min(24, 128 - start % 128)
            tile = jnp.where((lanes24 >= want) & (lanes24 < want + inside), part, tile)
            if inside < 24:
                part = row[:, block * 128 + 128 : block * 128 + 256]
                part = pltpu.roll(part, want + inside, 1)
                tile = jnp.where((lanes24 >= want + inside) & (lanes24 < want + 24), part, tile)
        patches[c2 * per_tile : (c2 + 1) * per_tile, :] = tile.astype(BF16)

    def stem_of(c0):
        n = ch * 2 * rows
        pre = mm(patches[pl.ds(c0 * 2 * rows, n), :], pix_d[0])
        s = (pre * sigmoid(pre)).astype(BF16)
        stem[pl.ds(c0, ch)] = s.reshape(ch, 2, rows, 256)

    loop(pairs, ch, stem_of)

    def top_in(c0):
        for cq in range(2):
            pieces = [stem[2 * (c0 + c) + cq, rp] for c in range(ch_t) for rp in range(2)]
            taps = jnp.concatenate(
                [jnp.concatenate(pieces[2 * c : 2 * c + 2], axis=1) for c in range(ch_t)], axis=0
            )
            x = mm(taps, down_b[...]).reshape(ch_t, rows, 128)
            grad_hi[pl.ds(c0, ch_t), 0, :, pl.ds(cq * 128, 128)] = x
            xs_top[pl.ds(c0, ch_t), 0, :, pl.ds(cq * 128, 128)] = shift_rows(x, 1).astype(BF16)
            xs_top[pl.ds(c0, ch_t), 1, :, pl.ds(cq * 128, 128)] = x.astype(BF16)
            xs_top[pl.ds(c0, ch_t), 2, :, pl.ds(cq * 128, 128)] = shift_rows(x, -1).astype(BF16)

    loop(pairs_t, ch_t, top_in)

    wide[pairs_t + 1, 0] = jnp.zeros((rows, 256), F32)

    def top_conv(c0):
        taps = jnp.concatenate([flat(xs_top[pl.ds(c0, ch_t), t]) for t in range(3)], axis=1)
        wide[pl.ds(c0 + 1, ch_t), 0] = mm_t(taps, b_fwd[0]).reshape(ch_t, rows, 256)

    loop(pairs_t, ch_t, top_conv)

    def add_num(x):
        acc_num[...] += jnp.sum(x.reshape(x.shape[0] // 8, 8, 128), axis=0)

    def add_sums(level, latent, hot_ref, here):
        hi = latent.astype(BF16).astype(F32)
        lo = latent - hi
        half = low_half(hi.shape)
        even = jnp.where(half, hi, swap_halves(lo)).astype(BF16)
        odd = jnp.where(half, swap_halves(hi), lo).astype(BF16)
        acc_sums[level] += mm_w(even, hot_ref[here, pl.ds(0, 512)]) + mm_w(
            odd, hot_ref[here, pl.ds(512, 512)]
        )

    def top_out(c0):
        n = ch_t * rows
        here = pl.ds(c0 * rows, n)
        a = flat(gather_wide(c0, ch_t, 0))
        act_top[here, :] = a
        hidden = (a * sigmoid(a)).astype(BF16)
        y = flat(grad_hi[pl.ds(c0, ch_t), 0]) + mm(hidden, wo_d[0])
        low = y.astype(BF16)
        low_top[here, :] = low
        latent = mm_t(low, to_d[0])
        lat_t[here, :] = latent
        add_sums(0, latent, hot_t, here)
        diff = latent - near_t[here, :]
        add_num(COMMIT_WEIGHT * diff * diff)

    loop(pairs_t, ch_t, top_out)

    def bottom_in(c0):
        x = stem[pl.ds(c0, ch)].astype(F32) + up[pl.ds(c0, ch)]
        res[pl.ds(c0, ch)] = x
        put_slots(xs_bot, c0, ch, x[:, 0], x[:, 1])

    loop(pairs, ch, bottom_in)
    conv_wide(xs_bot, 1)

    def bottom_out(c0):
        n = ch * 2 * rows
        here = pl.ds(c0 * 2 * rows, n)
        a = jnp.stack([gather_wide(c0, ch, rp) for rp in range(2)], axis=1).reshape(n, 128)
        act_bot[here, :] = a
        hidden = (a * sigmoid(a)).astype(BF16)
        y = res[pl.ds(c0, ch)].reshape(n, 256) + mm(hidden, wo_d[1])
        low = y.astype(BF16)
        low_bot[here, :] = low
        latent = mm_t(low, to_d[1])
        lat[here, :] = latent
        add_sums(1, latent, hot_b, here)
        diff = latent - near[here, :]
        add_num(COMMIT_WEIGHT * diff * diff)

    loop(pairs, ch, bottom_out)

    micro = place[0] + step
    image = place[1]
    images = valid_s.shape[1]
    for level, lat_ref in ((0, lat_t), (1, lat)):
        side = pairs * (level + 1)
        for r in range(8):
            pos = dead_source[level, r]
            col = lax.rem(pos, side)
            row_all = lax.div(pos, side)
            row = lax.rem(row_all, side)
            img_all = lax.div(row_all, side)
            mine = (lax.rem(img_all, images) == image) & (lax.div(img_all, images) == micro)
            if level == 0:
                local = lax.div(col, 2) * rows + row
            else:
                local = lax.div(col, 2) * (2 * rows) + lax.rem(row, 2) * rows + lax.div(row, 2)
            line = lat_ref[pl.ds(local, 1), :]
            odd = lax.rem(col, 2)
            line = jnp.where(low_half(line.shape) == (odd == 0), line, 0.0)
            line = line + swap_halves(line)
            line = jnp.where(low_half(line.shape) == (level == 0), line, 0.0)
            acc_dead[pl.ds(r, 1), :] += line * mine.astype(F32)

    limit = valid_s[micro, image]

    def decode_back(c0):
        n = ch * 2 * rows
        here = pl.ds(c0 * 2 * rows, n)
        lane = lane_iota((ch, 2, rows, 128))
        pixel_row = (
            8 * lax.broadcasted_iota(jnp.int32, lane.shape, 2)
            + 4 * lax.broadcasted_iota(jnp.int32, lane.shape, 1)
            + lane // 24
        )
        keep = ((pixel_row < limit) & (lane < 96)).astype(F32).reshape(n, 128)
        p = patches[here, :]
        diff = keep * (resid[here, :] - p.astype(F32))
        add_num(diff * diff)
        g_re = (loss_slope * diff).astype(BF16)
        acc_pix[1] += mm_w(g_re, low_dec[here, :])
        g = mm(g_re, pix_d[1])
        grad_hi[pl.ds(c0, ch)] = g.reshape(ch, 2, rows, 256)
        res_back(g, act_dec[here, :], 2, c0)

    def res_back(g, a, k, c0):
        n = ch * 2 * rows
        g_low = g.astype(BF16)
        s = sigmoid(a)
        hidden = (a * s).astype(BF16)
        acc_res[k] += mm_w(hidden, g_low)
        d = (mm_t(g_low, wo_d[k]) * (s * (1.0 + a * (1.0 - s)))).astype(BF16)
        d_two[pl.ds(c0 + 1, ch)] = d.astype(F32).reshape(ch, 2, rows, 128)

    def conv_back(k, xs, c0):
        outs = []
        total = None
        here = d_two[pl.ds(c0 + 1, ch)]
        before = d_two[pl.ds(c0, ch)]
        after = d_two[pl.ds(c0 + 2, ch)]
        d = jnp.concatenate([here, jnp.where(low_half(here.shape), after, before)], axis=3)
        put_slots(d_slots, c0, ch, d[:, 0], d[:, 1])
        for rp in range(2):
            taps = jnp.concatenate(
                [flat(d_slots[pl.ds(c0, ch), rp + t]) for t in range(3)], axis=1
            )
            outs.append(mm(taps, b_bwd[k]).reshape(ch, rows, 256))
            part = mm_w(flat(xs[pl.ds(c0, ch), rp + 1]), taps)
            total = part if total is None else total + part
        acc_conv[k] += total
        return jnp.stack(outs, axis=1)

    loop(pairs, ch, decode_back)

    def decode_in_back(c0):
        n = ch * 2 * rows
        here = pl.ds(c0 * 2 * rows, n)
        g = grad_hi[pl.ds(c0, ch)] + conv_back(2, xs_dec, c0)
        gup[pl.ds(c0, ch)] = g
        g_low = g.reshape(n, 256).astype(BF16)
        full = near[here, :]
        acc_from[...] += mm_w(full.astype(BF16), g_low)
        g_lat = mm_t(g_low, from_d[...]) + commit_slope * (lat[here, :] - full)
        g_lat = g_lat.astype(BF16)
        acc_to[1] += mm_w(g_lat, low_bot[here, :])
        grad_hi[pl.ds(c0, ch)] = mm(g_lat, to_d[1]).reshape(ch, 2, rows, 256)

    loop(pairs, ch, decode_in_back)

    def bottom_back(c0):
        n = ch * 2 * rows
        res_back(
            grad_hi[pl.ds(c0, ch)].reshape(n, 256), act_bot[pl.ds(c0 * 2 * rows, n), :], 1, c0
        )

    loop(pairs, ch, bottom_back)

    def bottom_in_back(c0):
        g = grad_hi[pl.ds(c0, ch)] + conv_back(1, xs_bot, c0)
        gstem[pl.ds(c0, ch)] = g.astype(BF16)
        total = (g + gup[pl.ds(c0, ch)]).astype(BF16)
        half = ch // 2
        total = total.reshape(half, 2, 2, rows, 256)
        wide_g = jnp.concatenate(
            [total[:, cq, rp].reshape(half * rows, 256) for cq in range(2) for rp in range(2)],
            axis=1,
        )
        t0 = pl.multiple_of(lax.div(c0, 2) * rows, half * rows)
        here = pl.ds(t0, half * rows)
        full = near_t[here, :]
        acc_up[...] += mm_w(full.astype(BF16), wide_g)
        g_q = mm_t(wide_g, up_d[...]).astype(BF16).astype(F32)
        g_lat = (g_q + commit_slope * (lat_t[here, :] - full)).astype(BF16)
        acc_to[0] += mm_w(g_lat, low_top[here, :])
        g_top = mm(g_lat, to_d[0])
        grad_lo[here, :] = g_top
        g_low = g_top.astype(BF16)
        a = act_top[here, :]
        s = sigmoid(a)
        acc_res[0] += mm_w((a * s).astype(BF16), g_low)
        d = (mm_t(g_low, wo_d[0]) * (s * (1.0 + a * (1.0 - s)))).astype(BF16)
        d_two_t[pl.ds(lax.div(c0, 2) + 1, half)] = d.astype(F32).reshape(half, rows, 128)

    loop(pairs, ch, bottom_in_back)

    def top_back(c0):
        n = ch_t * rows
        here = d_two_t[pl.ds(c0 + 1, ch_t)]
        before = d_two_t[pl.ds(c0, ch_t)]
        after = d_two_t[pl.ds(c0 + 2, ch_t)]
        d = jnp.concatenate([here, jnp.where(low_half(here.shape), after, before)], axis=2)
        taps = jnp.concatenate(
            [
                flat(shift_rows(d, 1)).astype(BF16),
                flat(d).astype(BF16),
                flat(shift_rows(d, -1)).astype(BF16),
            ],
            axis=1,
        )
        acc_conv[0] += mm_w(flat(xs_top[pl.ds(c0, ch_t), 1]), taps)
        g = grad_lo[pl.ds(c0 * rows, n), :] + mm(taps, b_bwd[0])
        g_low = g.astype(BF16).reshape(ch_t, rows, 256)
        for cq in range(2):
            g_cq = flat(g_low[:, :, cq * 128 : cq * 128 + 128])
            pieces = [stem[2 * (c0 + c) + cq, rp] for c in range(ch_t) for rp in range(2)]
            taps_s = jnp.concatenate(
                [jnp.concatenate(pieces[2 * c : 2 * c + 2], axis=1) for c in range(ch_t)], axis=0
            )
            acc_down[...] += mm_w(taps_s, g_cq)
            g_st = mm_t(g_cq, down_b[...]).reshape(ch_t, rows, 512)
            for c in range(ch_t):
                col = 2 * (c0 + c) + cq
                p = patches[pl.ds(pl.multiple_of(col * 2 * rows, 2 * rows), 2 * rows), :]
                sl = slope(mm(p, pix_d[0]))
                g_t = jnp.concatenate([g_st[c, :, :256], g_st[c, :, 256:]], axis=0)
                g_b = gstem[col].reshape(2 * rows, 256).astype(F32)
                both = jnp.concatenate([(g_t * sl).astype(BF16), (g_b * sl).astype(BF16)], axis=0)
                acc_pix[0] += mm_w(jnp.concatenate([p, p], axis=0), both)

    loop(pairs_t, ch_t, top_back)

    @pl.when(step == last)
    def _():
        for k in range(3):
            for i in range(3):
                lanes = (2 - i) * 256
                t = jnp.transpose(acc_conv[k, :, lanes : lanes + 256])
                taps = (
                    t[64:128, :128] + t[128:192, 128:],
                    t[:64, :128] + t[64:128, 128:],
                    t[:64, 128:] + t[192:, :128],
                )
                for j in range(3):
                    at = k * CONV_ROWS + (i * 3 + j) * TAP_ROWS
                    out[at : at + 64, :] = taps[j]
            out[ROW_RES + k * 64 : ROW_RES + k * 64 + 64, :] = (
                acc_res[k, :64, :128] + acc_res[k, 64:, 128:]
            )
        out[ROW_FROM : ROW_FROM + 64, :] = acc_from[:64, :128] + acc_from[64:, 128:]
        for k in range(4):
            out[ROW_FROM + (k + 1) * 64 : ROW_FROM + (k + 2) * 64, :] = (
                acc_up[:64, k * 128 : k * 128 + 128] + acc_up[64:, 512 + k * 128 : 640 + k * 128]
            )
        for k in range(2):
            at = ROW_TO + k * 64
            out[at : at + 64, :] = acc_to[k, :64, :128] + acc_to[k, 64:, 128:]
            for i in range(4):
                even = acc_pix[k, 24 * i : 24 * i + 12, :128]
                odd = acc_pix[k, 24 * i + 12 : 24 * i + 24, 128:]
                at = ROW_PIXEL + k * 48 + i * 12
                out[at : at + 12, :] = even + odd
        out[ROW_DOWN : ROW_DOWN + 512, :] = acc_down[...]
        for level in range(2):
            sums = acc_sums[level, :64, :] + acc_sums[level, 64:, :]
            used = jnp.sum(acc_count[level], axis=0, keepdims=True)
            for b in range(4):
                at = ROW_SUMS + (level * 4 + b) * 64
                out[at : at + 64, :] = sums[:, b * 128 : b * 128 + 128]
                at = ROW_COUNT + level * 4 + b
                out[at : at + 1, :] = used[:, b * 128 : b * 128 + 128]
        out[ROW_DEAD : ROW_DEAD + 8, :] = acc_dead[...]
        out[ROW_NUMER : ROW_NUMER + 8, :] = acc_num[...]
        if out.shape[0] > ROW_END:
            out[ROW_END:, :] = jnp.zeros((out.shape[0] - ROW_END, 128), F32)


def compute(place, valid_rows, dead_source, pix, ct, cb, weights, book, total_rows):
    share, part_rows, _ = pix[1].shape
    height = 2 * part_rows
    pairs = height // 8
    rows = height // 8
    pairs_t = pairs // 2
    n = pairs * 2 * rows
    n_t = pairs_t * rows
    smem = pl.BlockSpec(memory_space=pltpu.SMEM)

    def whole(x):
        zeros = (0,) * len(x.shape)
        return pl.BlockSpec(x.shape, lambda i, place: zeros)

    def near(x):
        return pl.BlockSpec((1,) + x.shape[1:], lambda i, place: (place[0] + i, 0, 0))

    def far(x):
        return pl.BlockSpec((1,) + x.shape[1:], lambda i, place: (i, 0, 0))

    v = pltpu.VMEM
    scratch = [
        v((3, 256, 768), BF16),
        v((3, 768, 256), BF16),
        v((3, 128, 256), BF16),
        v((128, 256), BF16),
        v((2, 128, 256), BF16),
        v((128, 1024), BF16),
        v((2, 128, 256), BF16),
        v((512, 128), BF16),
        v((2, 256, 512), BF16),
        v((2, 256, 512), BF16),
        v((height, height), BF16),
        v((n_t, 1024), BF16),
        v((n, 1024), BF16),
        v((n, 128), BF16),
        v((pairs, 2, rows, 256), BF16),
        v((pairs, 2, rows, 256), F32),
        v((n, 128), F32),
        v((n_t, 128), F32),
        v((pairs, 4, rows, 256), BF16),
        v((pairs, 4, rows, 256), BF16),
        v((pairs_t, 3, rows, 256), BF16),
        v((pairs + 2, 2, rows, 256), F32),
        v((pairs, 2, rows, 256), F32),
        v((n, 128), F32),
        v((n, 128), F32),
        v((n_t, 128), F32),
        v((n, 256), BF16),
        v((n, 256), BF16),
        v((n_t, 256), BF16),
        v((n, 128), F32),
        v((n_t, 128), F32),
        v((n, 128), F32),
        v((pairs, 2, rows, 256), F32),
        v((n_t, 256), F32),
        v((pairs + 2, 2, rows, 128), F32),
        v((pairs, 4, rows, 256), BF16),
        v((pairs_t + 2, rows, 128), F32),
        v((8, 128), BF16),
        v((pairs, 2, rows, 256), BF16),
        v((pairs, 2, rows, 256), F32),
        v((3, 256, 768), F32),
        v((3, 128, 256), F32),
        v((128, 256), F32),
        v((128, 1024), F32),
        v((2, 128, 256), F32),
        v((2, 128, 256), F32),
        v((512, 128), F32),
        v((2, 128, 512), F32),
        v((2, 8, 512), F32),
        v((8, 128), F32),
        v((8, 128), F32),
    ]
    return pl.pallas_call(
        compute_kernel,
        grid_spec=pltpu.PrefetchScalarGridSpec(
            num_scalar_prefetch=1,
            grid=(share,),
            in_specs=[smem, smem, whole(valid_rows)]
            + [spec(x) for pair in (pix, ct, cb) for spec, x in zip((near, far), pair)]
            + [whole(w) for w in weights]
            + [whole(book)],
            out_specs=pl.BlockSpec((total_rows, 128), lambda i, place: (0, 0)),
            scratch_shapes=scratch,
        ),
        out_shape=jax.ShapeDtypeStruct((total_rows, 128), F32),
        compiler_params=pltpu.CompilerParams(
            dimension_semantics=("arbitrary",), vmem_limit_bytes=VMEM_LIMIT
        ),
        name="step_compute",
    )(place, valid_rows, dead_source, valid_rows, *pix, *ct, *cb, *weights, book)


MESH = pl.DeviceIdType.MESH
Z_SIZE = 4


def reduce_kernel(plane, x, out, one, two, sums, three, acc, s1, r1, s2, r2, s3, r3, a3s, a3r, a2s, a2r, a1s, a1r):
    total = x.shape[0]
    half, part = total // 2, total // 2 // plane
    chunk = part // Z_SIZE
    s = lax.axis_index("section")
    d = lax.axis_index("dp")
    z, q = d // plane, d % plane
    peer = (1 - s, d)
    mates = [lax.rem(q + k, plane) for k in range(plane)]
    levels = [lax.rem(z + k, Z_SIZE) for k in range(Z_SIZE)]

    def rows(ref, sec, q_at, z_at=None):
        start = sec * half + q_at * part
        size = part
        if z_at is not None:
            start = start + z_at * chunk
            size = chunk
        return ref.at[pl.ds(pl.multiple_of(start, 8), size)]

    def piece(ref, index, size):
        return ref.at[pl.ds(pl.multiple_of(index * size, 8), size)]

    partners = [peer] + [(s, z * plane + m) for m in mates[1:]] + [(s, l * plane + q) for l in levels[1:]]
    barrier = pltpu.get_barrier_semaphore()
    for p in partners:
        pl.semaphore_signal(barrier, inc=1, device_id=p, device_id_type=MESH)
    pl.semaphore_wait(barrier, len(partners))

    def send(src, dst, ssem, rsem, to):
        c = pltpu.make_async_remote_copy(src, dst, ssem, rsem, device_id=to, device_id_type=MESH)
        c.start()
        return c

    order = list(range(1, plane)) + [0]
    first = {}
    for k in order:
        first[k] = send(rows(x, 1 - s, mates[k]), one.at[k], s1.at[k], r1.at[k], peer)
    second = {}
    for k in order:
        first[k].wait_recv()
        mine = rows(x, s, mates[k])[...] + one[k]
        if k == 0:
            acc[...] = mine
        else:
            sums[k - 1] = mine
            second[k] = send(
                sums.at[k - 1], two.at[k - 1], s2.at[k - 1], r2.at[k - 1], (s, z * plane + mates[k])
            )
    for k in range(1, plane):
        second[k].wait_recv()
    third = {}
    for k in [1, 2, 3, 0]:
        at = pl.ds(pl.multiple_of(levels[k] * chunk, 8), chunk)
        value = acc[at, :]
        for j in range(plane - 1):
            value = value + two[j, at, :]
        acc[at, :] = value
        if k > 0:
            third[k] = send(
                acc.at[at], three.at[k - 1], s3.at[k - 1], r3.at[k - 1], (s, levels[k] * plane + q)
            )
    value = acc[pl.ds(pl.multiple_of(z * chunk, 8), chunk), :]
    for k in range(1, Z_SIZE):
        third[k].wait_recv()
        value = value + three[k - 1]
    own = rows(out, s, q, z)
    own[...] = value
    up = {}
    for k in range(1, Z_SIZE):
        up[k] = send(own, own, a3s.at[k - 1], a3r.at[k - 1], (s, levels[k] * plane + q))
    across, over = {}, {}

    def spread(k):
        src = rows(out, s, q, lax.rem(z + Z_SIZE - k, Z_SIZE))
        for j in range(1, plane):
            at = (j - 1) * Z_SIZE + k
            across[j, k] = send(src, src, a2s.at[at], a2r.at[at], (s, z * plane + mates[j]))
        over[0, k] = send(src, src, a1s.at[k], a1r.at[k], peer)

    spread(0)
    for k in range(1, Z_SIZE):
        up[k].wait_recv()
        spread(k)
    for k in range(Z_SIZE):
        for j in range(1, plane):
            across[j, k].wait_recv()
            src = rows(out, s, lax.rem(q + plane - j, plane), lax.rem(z + Z_SIZE - k, Z_SIZE))
            at = j * Z_SIZE + k
            over[j, k] = send(src, src, a1s.at[at], a1r.at[at], peer)
    for c in over.values():
        c.wait_recv()
    for group in (first, second, third, up, across, over):
        for c in group.values():
            c.wait_send()


def all_sum(x, devices):
    total = x.shape[0]
    plane = devices // Z_SIZE
    part = total // 2 // plane
    chunk = part // Z_SIZE
    dma = pltpu.SemaphoreType.DMA
    v = pltpu.VMEM
    vm = pl.BlockSpec(memory_space=pltpu.VMEM)
    pairs = [plane, plane - 1, Z_SIZE - 1, Z_SIZE - 1, (plane - 1) * Z_SIZE, plane * Z_SIZE]
    return pl.pallas_call(
        functools.partial(reduce_kernel, plane),
        out_shape=jax.ShapeDtypeStruct(x.shape, F32),
        in_specs=[vm],
        out_specs=vm,
        scratch_shapes=[
            v((plane, part, 128), F32),
            v((plane - 1, part, 128), F32),
            v((plane - 1, part, 128), F32),
            v((Z_SIZE - 1, chunk, 128), F32),
            v((part, 128), F32),
        ]
        + [dma((n,)) for n in pairs for _ in range(2)],
        compiler_params=pltpu.CompilerParams(collective_id=0, has_side_effects=True, vmem_limit_bytes=VMEM_LIMIT),
        name="step_reduce",
    )(x)


def update_kernel(dead_codes, valid_v, total, *refs):
    w, m, v = refs[0:6], refs[6:12], refs[12:18]
    ema_count, ema_sum = refs[18:20]
    norm_o, pair_o = refs[20:22]
    new_o, mom_o, sec_o, low_o = refs[22:28], refs[28:34], refs[34:40], refs[40:46]
    book_o, count_o, sum_o = refs[46:49]
    grads = total[0:ROW_SUMS, :]
    squares = jnp.sum(jnp.sum((grads * grads).reshape(ROW_SUMS // 8, 8, 128), axis=0))
    norm = jnp.sqrt(jnp.full((8, 128), squares, F32))
    norm_o[0] = norm[0, 0]
    factor = (CLIP_NORM / jnp.maximum(norm, CLIP_NORM))[0, 0]
    pair_o[0] = jnp.sum(total[ROW_NUMER : ROW_NUMER + 8, :])
    pair_o[1] = 3.0 * 256.0 * jnp.sum(valid_v[...].astype(F32))

    def apply(t, index, grad):
        g = grad * factor
        first = MOMENT_ONE * m[t][index] + (1.0 - MOMENT_ONE) * g
        second = MOMENT_TWO * v[t][index] + (1.0 - MOMENT_TWO) * g * g
        step = first / (1.0 - MOMENT_ONE**STEP) / (
            jnp.sqrt(second / (1.0 - MOMENT_TWO**STEP)) + ADAM_EPSILON
        )
        weight = w[t][index]
        fresh = weight - LEARN_RATE * (step + WEIGHT_DECAY * weight)
        new_o[t][index] = fresh
        mom_o[t][index] = first
        sec_o[t][index] = second
        low_o[t][index] = fresh.astype(BF16)

    for k in range(3):
        for t in range(9):
            at = k * CONV_ROWS + t * TAP_ROWS
            apply(0, (k, slice(None), pl.ds(t * 128, 128)), total[at : at + 64, :])
        apply(1, (k,), total[ROW_RES + k * 64 : ROW_RES + k * 64 + 64, :])
    for k in range(5):
        apply(2, (k,), total[ROW_FROM + k * 64 : ROW_FROM + k * 64 + 64, :])
    for k in range(2):
        apply(3, (k,), total[ROW_TO + k * 64 : ROW_TO + k * 64 + 64, :])
        apply(4, (k,), total[ROW_PIXEL + k * 48 : ROW_PIXEL + k * 48 + 48, :])
    for k in range(4):
        apply(5, (k,), total[ROW_DOWN + k * 128 : ROW_DOWN + k * 128 + 128, :])

    dead = jnp.concatenate(
        [total[ROW_DEAD : ROW_DEAD + 8, :], jnp.zeros((120, 128), F32)], axis=0
    )
    dead = jnp.transpose(dead)
    for level in range(2):
        for b in range(4):
            lanes = pl.ds(b * 128, 128)
            at = ROW_COUNT + level * 4 + b
            ids = lane_iota((64, 128)) + b * 128
            count = CODE_DECAY * ema_count[level : level + 1, b * 128 : b * 128 + 128] + (
                1.0 - CODE_DECAY
            ) * total[at : at + 1, :]
            at = ROW_SUMS + (level * 4 + b) * 64
            sums = CODE_DECAY * ema_sum[level, :, lanes] + (1.0 - CODE_DECAY) * total[at : at + 64, :]
            for r in range(8):
                taken = ids == dead_codes[level, r]
                count = jnp.where(taken[:1], 1.0, count)
                sums = jnp.where(taken, dead[level * 64 : level * 64 + 64, r : r + 1], sums)
            count_o[level : level + 1, b * 128 : b * 128 + 128] = count
            sum_o[level, :, lanes] = sums
            book_o[level, :, lanes] = sums / count


def update(dead_codes, valid_rows, total, weights, firsts, seconds, ema_count, ema_sum):
    sds = jax.ShapeDtypeStruct
    shapes = [sds((1,), F32), sds((2,), F32)]
    for _ in range(3):
        shapes += [sds(w.shape, F32) for w in weights]
    shapes += [sds(w.shape, BF16) for w in weights]
    shapes += [sds(ema_sum.shape, F32), sds(ema_count.shape, F32), sds(ema_sum.shape, F32)]
    vm = pl.BlockSpec(memory_space=pltpu.VMEM)
    sm = pl.BlockSpec(memory_space=pltpu.SMEM)
    return pl.pallas_call(
        update_kernel,
        out_shape=shapes,
        in_specs=[sm] + [vm] * 22,
        out_specs=[sm, sm] + [vm] * 27,
        compiler_params=pltpu.CompilerParams(vmem_limit_bytes=VMEM_LIMIT),
        name="step_update",
    )(dead_codes, valid_rows, total, *weights, *firsts, *seconds, ema_count, ema_sum)


def body(sections, devices, *args):
    pixels, codes_top, codes_bottom, valid_rows, dead_codes, dead_source = args[:6]
    weights, firsts, seconds = args[6:12], args[12:18], args[18:24]
    codebook, ema_count, ema_sum = args[24:27]
    batches, part_rows, lanes = pixels.shape
    height = lanes // 3
    parts = height // part_rows
    share = batches // (sections * parts)
    section = lax.axis_index("section")
    device = lax.axis_index("dp")
    part = device % parts
    image = device // parts

    assert parts == 2 and sections == 2
    first = (section * parts + part) * share
    pairs = [(base + p, base + 1 - p) for base in range(0, devices, 2) for p in range(2)]

    def swapped(x):
        theirs = (section * parts + 1 - part) * share
        return (x, lax.ppermute(lax.dynamic_slice_in_dim(x, theirs, share, 0), "dp", pairs))

    def turn(arrays):
        return [x.transpose(0, 2, 1) if x.shape[2] == 64 else x for x in arrays]

    ct, cb, pix = swapped(codes_top), swapped(codes_bottom), swapped(pixels)
    place = jnp.stack([first, image, part]).astype(jnp.int32)
    multiple = 8 * sections * devices
    total_rows = -(-ROW_END // multiple) * multiple
    weights, firsts, seconds = turn(weights), turn(firsts), turn(seconds)
    codebook, ema_sum = turn([codebook, ema_sum])
    packed = compute(place, valid_rows, dead_source, pix, ct, cb, weights, codebook, total_rows)
    total = all_sum(packed, devices)
    outs = update(dead_codes, valid_rows, total, weights, firsts, seconds, ema_count, ema_sum)
    outs = [x.transpose(0, 2, 1) if len(x.shape) == 3 and x.shape[1] == 64 and turned else x for x, turned in zip(outs, TURNED)]
    return (outs[0].reshape(()),) + tuple(outs[1:])


TURNED = (False, False) + (True, False, False, True, False, False) * 4 + (True, False, True)


def solution(mesh):
    return jax.shard_map(
        functools.partial(body, mesh.shape["section"], mesh.shape["dp"]),
        mesh=mesh,
        in_specs=(P(None, "dp", None),) * 3 + (P(),) * 24,
        out_specs=(P(),) * 29,
        check_vma=False,
    )
```

```python
import functools

import jax
import jax.numpy as jnp
from jax import lax
from jax.experimental import pallas as pl
from jax.experimental.pallas import tpu as pltpu
from jax.sharding import PartitionSpec as P

STEP = 10
COMMIT_WEIGHT = 0.25
CODE_DECAY = 0.9
CLIP_NORM = 0.001
LEARN_RATE = 0.03
MOMENT_ONE = 0.9
MOMENT_TWO = 0.999
WEIGHT_DECAY = 0.01
ADAM_EPSILON = 1e-08

F32 = jnp.float32
BF16 = jnp.bfloat16
VMEM_LIMIT = 56 * 1024 * 1024

TAP_ROWS = 64
CONV_ROWS = 9 * TAP_ROWS
ROW_RES = 3 * CONV_ROWS
ROW_FROM = ROW_RES + 3 * 64
ROW_TO = ROW_FROM + 5 * 64
ROW_PIXEL = ROW_TO + 2 * 64
ROW_DOWN = ROW_PIXEL + 2 * 48
ROW_SUMS = ROW_DOWN + 512
ROW_COUNT = ROW_SUMS + 512
ROW_DEAD = ROW_COUNT + 8
ROW_NUMER = ROW_DEAD + 8
ROW_END = ROW_NUMER + 8


def mm(x, w):
    return lax.dot_general(x, w, (((1,), (0,)), ((), ())), preferred_element_type=F32)


def mm_t(x, w):
    return lax.dot_general(x, w, (((1,), (1,)), ((), ())), preferred_element_type=F32)


def mm_w(x, g):
    return lax.dot_general(x, g, (((0,), (0,)), ((), ())), preferred_element_type=F32)


def lane_iota(shape):
    return lax.broadcasted_iota(jnp.int32, shape, len(shape) - 1)


def low_half(shape):
    return lane_iota(shape) % 128 < 64


def sigmoid(x):
    return 0.5 * jnp.tanh(0.5 * x) + 0.5


def slope(a):
    s = sigmoid(a)
    return s * (1.0 + a * (1.0 - s))


def shift_rows(x, by):
    rows = x.shape[1]
    moved = pltpu.roll(x, by % rows, 1)
    ids = lax.broadcasted_iota(jnp.int32, x.shape, 1)
    edge = 0 if by == 1 else rows - 1
    return jnp.where(ids == edge, 0.0, moved)


def flat(x):
    return x.reshape(x.shape[0] * x.shape[1], x.shape[2])


def pair_diag(w):
    zero = jnp.zeros_like(w)
    return jnp.concatenate(
        [jnp.concatenate([w, zero], axis=1), jnp.concatenate([zero, w], axis=1)], axis=0
    )


def swap_halves(x):
    return pltpu.roll(x, 64, len(x.shape) - 1)


def compute_kernel(
    place,
    valid_s,
    dead_source,
    valid_v,
    pix,
    pix_far,
    ct_near,
    ct_far,
    cb_near,
    cb_far,
    w_conv,
    w_res,
    w_from,
    w_to,
    w_pix,
    w_down,
    book,
    out,
    b_fwd,
    b_bwd,
    wo_d,
    from_d,
    to_d,
    up_d,
    pix_d,
    down_b,
    book_a,
    book_b,
    sel,
    hot_t,
    hot_b,
    patches,
    stem,
    up,
    near,
    near_t,
    xs_dec,
    xs_bot,
    xs_top,
    wide,
    res,
    act_dec,
    act_bot,
    act_top,
    low_dec,
    low_bot,
    low_top,
    lat,
    lat_t,
    resid,
    grad_hi,
    grad_lo,
    d_two,
    d_slots,
    d_two_t,
    gpre,
    gstem,
    gup,
    acc_conv,
    acc_res,
    acc_from,
    acc_up,
    acc_to,
    acc_pix,
    acc_down,
    acc_sums,
    acc_count,
    acc_dead,
    acc_num,
):
    step = pl.program_id(0)
    last = pl.num_programs(0) - 1
    pairs, rows = xs_bot.shape[0], xs_bot.shape[2]
    pairs_t = xs_top.shape[0]
    ch, ch_t = pairs, pairs_t
    height = 2 * pix.shape[1]
    valid_count = 3.0 * height * jnp.sum(valid_v[...].astype(F32))
    loss_slope = 2.0 / valid_count
    commit_slope = loss_slope * COMMIT_WEIGHT

    def picker(src, start):
        size = src.shape[0]
        at = lax.broadcasted_iota(jnp.int32, src.shape, 1) + start
        at = jnp.where(at >= size, at - size, at)
        return (at == src).astype(F32).astype(BF16)

    @pl.when(step == 0)
    def _():
        for ref in (acc_conv, acc_res, acc_from, acc_up, acc_to, acc_pix, acc_down, acc_sums, acc_count, acc_dead, acc_num):
            ref[...] = jnp.zeros(ref.shape, F32)
        wide[...] = jnp.zeros(wide.shape, F32)
        d_two[...] = jnp.zeros(d_two.shape, F32)
        d_two_t[...] = jnp.zeros(d_two_t.shape, F32)
        zero = jnp.zeros((64, 128), F32)
        for k in range(3):
            for i in range(3):
                t = [w_conv[k, :, pl.ds((i * 3 + j) * 128, 128)] for j in range(3)]
                even = jnp.concatenate([t[1], t[0], zero, t[2]], axis=0).astype(BF16)
                odd = jnp.concatenate([t[2], t[1], t[0], zero], axis=0).astype(BF16)
                both = jnp.concatenate([even, odd], axis=1)
                b_fwd[k, :, pl.ds(i * 256, 256)] = both
                b_bwd[k, pl.ds((2 - i) * 256, 256), :] = both
            wo_d[k] = pair_diag(w_res[k]).astype(BF16)
        from_d[...] = pair_diag(w_from[0]).astype(BF16)
        for k in range(2):
            to_d[k] = pair_diag(w_to[k]).astype(BF16)
        up_d[...] = pair_diag(
            jnp.concatenate([w_from[k] for k in range(1, 5)], axis=1)
        ).astype(BF16)
        lane = lax.broadcasted_iota(jnp.int32, (128, 48), 0)
        tap = lax.broadcasted_iota(jnp.int32, (128, 48), 1)
        for k in range(2):
            low = w_pix[k].astype(BF16)
            for cp in range(2):
                pick = (lane == (tap // 12) * 24 + cp * 12 + tap % 12).astype(F32).astype(BF16)
                pix_d[k, :, pl.ds(cp * 128, 128)] = mm(pick, low).astype(BF16)
        for k in range(4):
            down_b[pl.ds(k * 128, 128), :] = w_down[k].astype(BF16)
        for k in range(2):
            full = book[k]
            hi = full.astype(BF16).astype(F32)
            mid = (full - hi).astype(BF16).astype(F32)
            lo = full - hi - mid
            empty = jnp.zeros_like(full)
            book_a[k] = jnp.concatenate([hi, mid, lo, empty], axis=0).astype(BF16)
            book_b[k] = jnp.concatenate([mid, hi, empty, lo], axis=0).astype(BF16)
        o = lax.broadcasted_iota(jnp.int32, (height, height), 0)
        quarter = height // 4
        src = 8 * (o % rows) + 4 * ((o % quarter) // rows) + o // quarter
        sel[...] = picker(src, place[2] * (height // 2))

    def codes_of(near_ref, far_ref, split):
        both = jnp.concatenate([near_ref[0], far_ref[0]], axis=0).astype(F32)
        size = both.shape[0]
        o = lax.broadcasted_iota(jnp.int32, (size, size), 0)
        src = 2 * (o % rows) + o // rows if split else o
        pick = picker(src, place[2] * (size // 2))
        high = jnp.floor(both * (1.0 / 256.0))
        low = both - 256.0 * high
        codes = 256.0 * mm(pick, high.astype(BF16)) + mm(pick, low.astype(BF16))
        pad = jnp.zeros((size, 128 - size), F32)
        return jnp.concatenate([codes, pad], axis=1)

    codes_t = codes_of(ct_near, ct_far, False)
    codes_b = codes_of(cb_near, cb_far, True)

    def near_of(codes, level, c0, n, hot_ref):
        size = codes.shape[0]
        here = pl.ds(c0 * size, n * size)
        moved = codes
        ids = lax.broadcasted_iota(jnp.int32, (size, 512), 1).astype(F32)
        v = []
        used = jnp.zeros((8, 512), F32)
        for cp, table in ((0, book_a), (1, book_b)):
            for j in range(n):
                hot = (moved[:, 2 * j + cp : 2 * j + cp + 1] == ids).astype(F32)
                used = used + jnp.sum(hot.reshape(size // 8, 8, 512), axis=0)
                at = pl.ds((c0 + j) * size, size)
                hot_ref[at, pl.ds(cp * 512, 512)] = hot.astype(BF16)
            v.append(mm_t(hot_ref[here, pl.ds(cp * 512, 512)], table[level]))
        acc_count[level] += used
        half = low_half((n * size, 128))
        hi = jnp.where(half, v[0][:, :128], v[1][:, :128])
        mid = swap_halves(jnp.where(half, v[1][:, :128], v[0][:, :128]))
        lo = jnp.where(half, v[0][:, 128:], v[1][:, 128:])
        return hi, hi + mid + lo

    def top_codes(c0):
        hi, full = near_of(codes_t, 0, c0, ch_t, hot_t)
        near_t[pl.ds(c0 * rows, ch_t * rows), :] = full
        u = mm(hi.astype(BF16), up_d[...]).reshape(ch_t, rows, 1024)
        for cq in range(2):
            for rp in range(2):
                for c in range(ch_t):
                    at = (cq * 2 + rp) * 256
                    up[2 * (c0 + c) + cq, rp] = u[c, :, at : at + 256]

    top_codes(0)

    def put_slots(ref, c0, n, even, odd):
        ref[pl.ds(c0, n), 0] = shift_rows(odd, 1).astype(BF16)
        ref[pl.ds(c0, n), 1] = even.astype(BF16)
        ref[pl.ds(c0, n), 2] = odd.astype(BF16)
        ref[pl.ds(c0, n), 3] = shift_rows(even, -1).astype(BF16)

    def bottom_codes(c0):
        n = ch * 2 * rows
        hi, full = near_of(codes_b, 1, c0, ch, hot_b)
        near[pl.ds(c0 * 2 * rows, n), :] = full
        x = mm(hi.astype(BF16), from_d[...]).reshape(ch, 2, rows, 256) + up[pl.ds(c0, ch)]
        res[pl.ds(c0, ch)] = x
        put_slots(xs_dec, c0, ch, x[:, 0], x[:, 1])

    bottom_codes(0)

    def conv_wide(xs, k):
        def run(c0):
            for rp in range(2):
                taps = jnp.concatenate(
                    [flat(xs[pl.ds(c0, ch), rp + t]) for t in range(3)], axis=1
                )
                y = mm_t(taps, b_fwd[k])
                wide[pl.ds(c0 + 1, ch), rp] = y.reshape(ch, rows, 256)

        run(0)

    def gather_wide(c0, n, rp):
        before = wide[pl.ds(c0, n), rp, :, 128:]
        after = wide[pl.ds(c0 + 2, n), rp, :, 128:]
        return wide[pl.ds(c0 + 1, n), rp, :, :128] + jnp.where(low_half(before.shape), before, after)

    conv_wide(xs_dec, 2)

    def decode_out(c0):
        a = jnp.stack([gather_wide(c0, ch, rp) for rp in range(2)], axis=1)
        n = ch * 2 * rows
        a = a.reshape(n, 128)
        act_dec[pl.ds(c0 * 2 * rows, n), :] = a
        hidden = (a * sigmoid(a)).astype(BF16)
        y = res[pl.ds(c0, ch)].reshape(n, 256) + mm(hidden, wo_d[2])
        low = y.astype(BF16)
        low_dec[pl.ds(c0 * 2 * rows, n), :] = low
        resid[pl.ds(c0 * 2 * rows, n), :] = mm_t(low, pix_d[1])

    decode_out(0)

    per_tile = 2 * rows
    picked = mm(sel[...], jnp.concatenate([pix[0], pix_far[0]], axis=0))
    lanes24 = lane_iota((per_tile, 128))
    for c2 in range(pairs):
        tile = jnp.zeros((per_tile, 128), F32)
        for i in range(4):
            start = 24 * c2
            want = 24 * i
            block = start // 128
            row = picked[i * per_tile : (i + 1) * per_tile]
            part = row[:, block * 128 : block * 128 + 128]
            part = pltpu.roll(part, (want - start % 128) % 128, 1)
            inside = min(24, 128 - start % 128)
            tile = jnp.where((lanes24 >= want) & (lanes24 < want + inside), part, tile)
            if inside < 24:
                part = row[:, block * 128 + 128 : block * 128 + 256]
                part = pltpu.roll(part, want + inside, 1)
                tile = jnp.where((lanes24 >= want + inside) & (lanes24 < want + 24), part, tile)
        patches[c2 * per_tile : (c2 + 1) * per_tile, :] = tile.astype(BF16)

    def stem_of(c0):
        n = ch * 2 * rows
        pre = mm(patches[pl.ds(c0 * 2 * rows, n), :], pix_d[0])
        s = (pre * sigmoid(pre)).astype(BF16)
        stem[pl.ds(c0, ch)] = s.reshape(ch, 2, rows, 256)

    stem_of(0)

    def top_in(c0):
        for cq in range(2):
            pieces = [stem[2 * (c0 + c) + cq, rp] for c in range(ch_t) for rp in range(2)]
            taps = jnp.concatenate(
                [jnp.concatenate(pieces[2 * c : 2 * c + 2], axis=1) for c in range(ch_t)], axis=0
            )
            x = mm(taps, down_b[...]).reshape(ch_t, rows, 128)
            grad_hi[pl.ds(c0, ch_t), 0, :, pl.ds(cq * 128, 128)] = x
            xs_top[pl.ds(c0, ch_t), 0, :, pl.ds(cq * 128, 128)] = shift_rows(x, 1).astype(BF16)
            xs_top[pl.ds(c0, ch_t), 1, :, pl.ds(cq * 128, 128)] = x.astype(BF16)
            xs_top[pl.ds(c0, ch_t), 2, :, pl.ds(cq * 128, 128)] = shift_rows(x, -1).astype(BF16)

    top_in(0)

    wide[pairs_t + 1, 0] = jnp.zeros((rows, 256), F32)

    def top_conv(c0):
        taps = jnp.concatenate([flat(xs_top[pl.ds(c0, ch_t), t]) for t in range(3)], axis=1)
        wide[pl.ds(c0 + 1, ch_t), 0] = mm_t(taps, b_fwd[0]).reshape(ch_t, rows, 256)

    top_conv(0)

    def add_num(x):
        acc_num[...] += jnp.sum(x.reshape(x.shape[0] // 8, 8, 128), axis=0)

    def add_sums(level, latent, hot_ref, here):
        hi = latent.astype(BF16).astype(F32)
        lo = latent - hi
        half = low_half(hi.shape)
        even = jnp.where(half, hi, swap_halves(lo)).astype(BF16)
        odd = jnp.where(half, swap_halves(hi), lo).astype(BF16)
        acc_sums[level] += mm_w(even, hot_ref[here, pl.ds(0, 512)]) + mm_w(
            odd, hot_ref[here, pl.ds(512, 512)]
        )

    def top_out(c0):
        n = ch_t * rows
        here = pl.ds(c0 * rows, n)
        a = flat(gather_wide(c0, ch_t, 0))
        act_top[here, :] = a
        hidden = (a * sigmoid(a)).astype(BF16)
        y = flat(grad_hi[pl.ds(c0, ch_t), 0]) + mm(hidden, wo_d[0])
        low = y.astype(BF16)
        low_top[here, :] = low
        latent = mm_t(low, to_d[0])
        lat_t[here, :] = latent
        add_sums(0, latent, hot_t, here)
        diff = latent - near_t[here, :]
        add_num(COMMIT_WEIGHT * diff * diff)

    top_out(0)

    def bottom_in(c0):
        x = stem[pl.ds(c0, ch)].astype(F32) + up[pl.ds(c0, ch)]
        res[pl.ds(c0, ch)] = x
        put_slots(xs_bot, c0, ch, x[:, 0], x[:, 1])

    bottom_in(0)
    conv_wide(xs_bot, 1)

    def bottom_out(c0):
        n = ch * 2 * rows
        here = pl.ds(c0 * 2 * rows, n)
        a = jnp.stack([gather_wide(c0, ch, rp) for rp in range(2)], axis=1).reshape(n, 128)
        act_bot[here, :] = a
        hidden = (a * sigmoid(a)).astype(BF16)
        y = res[pl.ds(c0, ch)].reshape(n, 256) + mm(hidden, wo_d[1])
        low = y.astype(BF16)
        low_bot[here, :] = low
        latent = mm_t(low, to_d[1])
        lat[here, :] = latent
        add_sums(1, latent, hot_b, here)
        diff = latent - near[here, :]
        add_num(COMMIT_WEIGHT * diff * diff)

    bottom_out(0)

    micro = place[0] + step
    image = place[1]
    images = valid_s.shape[1]
    for level, lat_ref in ((0, lat_t), (1, lat)):
        side = pairs * (level + 1)
        for r in range(8):
            pos = dead_source[level, r]
            col = lax.rem(pos, side)
            row_all = lax.div(pos, side)
            row = lax.rem(row_all, side)
            img_all = lax.div(row_all, side)
            mine = (lax.rem(img_all, images) == image) & (lax.div(img_all, images) == micro)
            if level == 0:
                local = lax.div(col, 2) * rows + row
            else:
                local = lax.div(col, 2) * (2 * rows) + lax.rem(row, 2) * rows + lax.div(row, 2)
            line = lat_ref[pl.ds(local, 1), :]
            odd = lax.rem(col, 2)
            line = jnp.where(low_half(line.shape) == (odd == 0), line, 0.0)
            line = line + swap_halves(line)
            line = jnp.where(low_half(line.shape) == (level == 0), line, 0.0)
            acc_dead[pl.ds(r, 1), :] += line * mine.astype(F32)

    limit = valid_s[micro, image]

    def decode_back(c0):
        n = ch * 2 * rows
        here = pl.ds(c0 * 2 * rows, n)
        lane = lane_iota((ch, 2, rows, 128))
        pixel_row = (
            8 * lax.broadcasted_iota(jnp.int32, lane.shape, 2)
            + 4 * lax.broadcasted_iota(jnp.int32, lane.shape, 1)
            + lane // 24
        )
        keep = ((pixel_row < limit) & (lane < 96)).astype(F32).reshape(n, 128)
        p = patches[here, :]
        diff = keep * (resid[here, :] - p.astype(F32))
        add_num(diff * diff)
        g_re = (loss_slope * diff).astype(BF16)
        acc_pix[1] += mm_w(g_re, low_dec[here, :])
        g = mm(g_re, pix_d[1])
        grad_hi[pl.ds(c0, ch)] = g.reshape(ch, 2, rows, 256)
        res_back(g, act_dec[here, :], 2, c0)

    def res_back(g, a, k, c0):
        n = ch * 2 * rows
        g_low = g.astype(BF16)
        s = sigmoid(a)
        hidden = (a * s).astype(BF16)
        acc_res[k] += mm_w(hidden, g_low)
        d = (mm_t(g_low, wo_d[k]) * (s * (1.0 + a * (1.0 - s)))).astype(BF16)
        d_two[pl.ds(c0 + 1, ch)] = d.astype(F32).reshape(ch, 2, rows, 128)

    def conv_back(k, xs, c0):
        outs = []
        total = None
        here = d_two[pl.ds(c0 + 1, ch)]
        before = d_two[pl.ds(c0, ch)]
        after = d_two[pl.ds(c0 + 2, ch)]
        d = jnp.concatenate([here, jnp.where(low_half(here.shape), after, before)], axis=3)
        put_slots(d_slots, c0, ch, d[:, 0], d[:, 1])
        for rp in range(2):
            taps = jnp.concatenate(
                [flat(d_slots[pl.ds(c0, ch), rp + t]) for t in range(3)], axis=1
            )
            outs.append(mm(taps, b_bwd[k]).reshape(ch, rows, 256))
            part = mm_w(flat(xs[pl.ds(c0, ch), rp + 1]), taps)
            total = part if total is None else total + part
        acc_conv[k] += total
        return jnp.stack(outs, axis=1)

    decode_back(0)

    def decode_in_back(c0):
        n = ch * 2 * rows
        here = pl.ds(c0 * 2 * rows, n)
        g = grad_hi[pl.ds(c0, ch)] + conv_back(2, xs_dec, c0)
        gup[pl.ds(c0, ch)] = g
        g_low = g.reshape(n, 256).astype(BF16)
        full = near[here, :]
        acc_from[...] += mm_w(full.astype(BF16), g_low)
        g_lat = mm_t(g_low, from_d[...]) + commit_slope * (lat[here, :] - full)
        g_lat = g_lat.astype(BF16)
        acc_to[1] += mm_w(g_lat, low_bot[here, :])
        grad_hi[pl.ds(c0, ch)] = mm(g_lat, to_d[1]).reshape(ch, 2, rows, 256)

    decode_in_back(0)

    def bottom_back(c0):
        n = ch * 2 * rows
        res_back(
            grad_hi[pl.ds(c0, ch)].reshape(n, 256), act_bot[pl.ds(c0 * 2 * rows, n), :], 1, c0
        )

    bottom_back(0)

    def bottom_in_back(c0):
        g = grad_hi[pl.ds(c0, ch)] + conv_back(1, xs_bot, c0)
        gstem[pl.ds(c0, ch)] = g.astype(BF16)
        total = (g + gup[pl.ds(c0, ch)]).astype(BF16)
        half = ch // 2
        total = total.reshape(half, 2, 2, rows, 256)
        wide_g = jnp.concatenate(
            [total[:, cq, rp].reshape(half * rows, 256) for cq in range(2) for rp in range(2)],
            axis=1,
        )
        t0 = c0 // 2 * rows
        here = pl.ds(t0, half * rows)
        full = near_t[here, :]
        acc_up[...] += mm_w(full.astype(BF16), wide_g)
        g_q = mm_t(wide_g, up_d[...]).astype(BF16).astype(F32)
        g_lat = (g_q + commit_slope * (lat_t[here, :] - full)).astype(BF16)
        acc_to[0] += mm_w(g_lat, low_top[here, :])
        g_top = mm(g_lat, to_d[0])
        grad_lo[here, :] = g_top
        g_low = g_top.astype(BF16)
        a = act_top[here, :]
        s = sigmoid(a)
        acc_res[0] += mm_w((a * s).astype(BF16), g_low)
        d = (mm_t(g_low, wo_d[0]) * (s * (1.0 + a * (1.0 - s)))).astype(BF16)
        d_two_t[pl.ds(c0 // 2 + 1, half)] = d.astype(F32).reshape(half, rows, 128)

    bottom_in_back(0)

    def top_back(c0):
        n = ch_t * rows
        here = d_two_t[pl.ds(c0 + 1, ch_t)]
        before = d_two_t[pl.ds(c0, ch_t)]
        after = d_two_t[pl.ds(c0 + 2, ch_t)]
        d = jnp.concatenate([here, jnp.where(low_half(here.shape), after, before)], axis=2)
        taps = jnp.concatenate(
            [
                flat(shift_rows(d, 1)).astype(BF16),
                flat(d).astype(BF16),
                flat(shift_rows(d, -1)).astype(BF16),
            ],
            axis=1,
        )
        acc_conv[0] += mm_w(flat(xs_top[pl.ds(c0, ch_t), 1]), taps)
        g = grad_lo[pl.ds(c0 * rows, n), :] + mm(taps, b_bwd[0])
        g_low = g.astype(BF16).reshape(ch_t, rows, 256)
        for cq in range(2):
            g_cq = flat(g_low[:, :, cq * 128 : cq * 128 + 128])
            pieces = [stem[2 * (c0 + c) + cq, rp] for c in range(ch_t) for rp in range(2)]
            taps_s = jnp.concatenate(
                [jnp.concatenate(pieces[2 * c : 2 * c + 2], axis=1) for c in range(ch_t)], axis=0
            )
            acc_down[...] += mm_w(taps_s, g_cq)
            g_st = mm_t(g_cq, down_b[...]).reshape(ch_t, rows, 512)
            for c in range(ch_t):
                col = 2 * (c0 + c) + cq
                at = pl.ds(col * 2 * rows, 2 * rows)
                sl = slope(mm(patches[at, :], pix_d[0]))
                g_t = jnp.concatenate([g_st[c, :, :256], g_st[c, :, 256:]], axis=0)
                g_b = gstem[col].reshape(2 * rows, 256).astype(F32)
                gpre[0, at, :] = (g_t * sl).astype(BF16)
                gpre[1, at, :] = (g_b * sl).astype(BF16)
        acc_pix[0] += mm_w(patches[...], gpre[0]) + mm_w(patches[...], gpre[1])

    top_back(0)

    @pl.when(step == last)
    def _():
        for k in range(3):
            for i in range(3):
                lanes = (2 - i) * 256
                t = jnp.transpose(acc_conv[k, :, lanes : lanes + 256])
                taps = (
                    t[64:128, :128] + t[128:192, 128:],
                    t[:64, :128] + t[64:128, 128:],
                    t[:64, 128:] + t[192:, :128],
                )
                for j in range(3):
                    at = k * CONV_ROWS + (i * 3 + j) * TAP_ROWS
                    out[at : at + 64, :] = taps[j]
            out[ROW_RES + k * 64 : ROW_RES + k * 64 + 64, :] = (
                acc_res[k, :64, :128] + acc_res[k, 64:, 128:]
            )
        out[ROW_FROM : ROW_FROM + 64, :] = acc_from[:64, :128] + acc_from[64:, 128:]
        for k in range(4):
            out[ROW_FROM + (k + 1) * 64 : ROW_FROM + (k + 2) * 64, :] = (
                acc_up[:64, k * 128 : k * 128 + 128] + acc_up[64:, 512 + k * 128 : 640 + k * 128]
            )
        for k in range(2):
            at = ROW_TO + k * 64
            out[at : at + 64, :] = acc_to[k, :64, :128] + acc_to[k, 64:, 128:]
            for i in range(4):
                even = acc_pix[k, 24 * i : 24 * i + 12, :128]
                odd = acc_pix[k, 24 * i + 12 : 24 * i + 24, 128:]
                at = ROW_PIXEL + k * 48 + i * 12
                out[at : at + 12, :] = even + odd
        out[ROW_DOWN : ROW_DOWN + 512, :] = acc_down[...]
        for level in range(2):
            sums = acc_sums[level, :64, :] + acc_sums[level, 64:, :]
            used = jnp.sum(acc_count[level], axis=0, keepdims=True)
            for b in range(4):
                at = ROW_SUMS + (level * 4 + b) * 64
                out[at : at + 64, :] = sums[:, b * 128 : b * 128 + 128]
                at = ROW_COUNT + level * 4 + b
                out[at : at + 1, :] = used[:, b * 128 : b * 128 + 128]
        out[ROW_DEAD : ROW_DEAD + 8, :] = acc_dead[...]
        out[ROW_NUMER : ROW_NUMER + 8, :] = acc_num[...]
        if out.shape[0] > ROW_END:
            out[ROW_END:, :] = jnp.zeros((out.shape[0] - ROW_END, 128), F32)


def compute(place, valid_rows, dead_source, pix, ct, cb, weights, book, total_rows):
    share, part_rows, _ = pix[1].shape
    height = 2 * part_rows
    pairs = height // 8
    rows = height // 8
    pairs_t = pairs // 2
    n = pairs * 2 * rows
    n_t = pairs_t * rows
    smem = pl.BlockSpec(memory_space=pltpu.SMEM)

    def whole(x):
        zeros = (0,) * len(x.shape)
        return pl.BlockSpec(x.shape, lambda i, place: zeros)

    def near(x):
        return pl.BlockSpec((1,) + x.shape[1:], lambda i, place: (place[0] + i, 0, 0))

    def far(x):
        return pl.BlockSpec((1,) + x.shape[1:], lambda i, place: (i, 0, 0))

    v = pltpu.VMEM
    scratch = [
        v((3, 256, 768), BF16),
        v((3, 768, 256), BF16),
        v((3, 128, 256), BF16),
        v((128, 256), BF16),
        v((2, 128, 256), BF16),
        v((128, 1024), BF16),
        v((2, 128, 256), BF16),
        v((512, 128), BF16),
        v((2, 256, 512), BF16),
        v((2, 256, 512), BF16),
        v((height, height), BF16),
        v((n_t, 1024), BF16),
        v((n, 1024), BF16),
        v((n, 128), BF16),
        v((pairs, 2, rows, 256), BF16),
        v((pairs, 2, rows, 256), F32),
        v((n, 128), F32),
        v((n_t, 128), F32),
        v((pairs, 4, rows, 256), BF16),
        v((pairs, 4, rows, 256), BF16),
        v((pairs_t, 3, rows, 256), BF16),
        v((pairs + 2, 2, rows, 256), F32),
        v((pairs, 2, rows, 256), F32),
        v((n, 128), F32),
        v((n, 128), F32),
        v((n_t, 128), F32),
        v((n, 256), BF16),
        v((n, 256), BF16),
        v((n_t, 256), BF16),
        v((n, 128), F32),
        v((n_t, 128), F32),
        v((n, 128), F32),
        v((pairs, 2, rows, 256), F32),
        v((n_t, 256), F32),
        v((pairs + 2, 2, rows, 128), F32),
        v((pairs, 4, rows, 256), BF16),
        v((pairs_t + 2, rows, 128), F32),
        v((2, n, 256), BF16),
        v((pairs, 2, rows, 256), BF16),
        v((pairs, 2, rows, 256), F32),
        v((3, 256, 768), F32),
        v((3, 128, 256), F32),
        v((128, 256), F32),
        v((128, 1024), F32),
        v((2, 128, 256), F32),
        v((2, 128, 256), F32),
        v((512, 128), F32),
        v((2, 128, 512), F32),
        v((2, 8, 512), F32),
        v((8, 128), F32),
        v((8, 128), F32),
    ]
    return pl.pallas_call(
        compute_kernel,
        grid_spec=pltpu.PrefetchScalarGridSpec(
            num_scalar_prefetch=1,
            grid=(share,),
            in_specs=[smem, smem, whole(valid_rows)]
            + [spec(x) for pair in (pix, ct, cb) for spec, x in zip((near, far), pair)]
            + [whole(w) for w in weights]
            + [whole(book)],
            out_specs=pl.BlockSpec((total_rows, 128), lambda i, place: (0, 0)),
            scratch_shapes=scratch,
        ),
        out_shape=jax.ShapeDtypeStruct((total_rows, 128), F32),
        compiler_params=pltpu.CompilerParams(
            dimension_semantics=("arbitrary",), vmem_limit_bytes=VMEM_LIMIT
        ),
        name="step_compute",
    )(place, valid_rows, dead_source, valid_rows, *pix, *ct, *cb, *weights, book)


MESH = pl.DeviceIdType.MESH
Z_SIZE = 4


def reduce_kernel(plane, x, out, one, two, sums, three, acc, s1, r1, s2, r2, s3, r3, a3s, a3r, a2s, a2r, a1s, a1r):
    total = x.shape[0]
    half, part = total // 2, total // 2 // plane
    chunk = part // Z_SIZE
    s = lax.axis_index("section")
    d = lax.axis_index("dp")
    z, q = d // plane, d % plane
    peer = (1 - s, d)
    mates = [lax.rem(q + k, plane) for k in range(plane)]
    levels = [lax.rem(z + k, Z_SIZE) for k in range(Z_SIZE)]

    def rows(ref, sec, q_at, z_at=None):
        start = sec * half + q_at * part
        size = part
        if z_at is not None:
            start = start + z_at * chunk
            size = chunk
        return ref.at[pl.ds(pl.multiple_of(start, 8), size)]

    def piece(ref, index, size):
        return ref.at[pl.ds(pl.multiple_of(index * size, 8), size)]

    partners = [peer] + [(s, z * plane + m) for m in mates[1:]] + [(s, l * plane + q) for l in levels[1:]]
    barrier = pltpu.get_barrier_semaphore()
    for p in partners:
        pl.semaphore_signal(barrier, inc=1, device_id=p, device_id_type=MESH)
    pl.semaphore_wait(barrier, len(partners))

    def send(src, dst, ssem, rsem, to):
        c = pltpu.make_async_remote_copy(src, dst, ssem, rsem, device_id=to, device_id_type=MESH)
        c.start()
        return c

    order = list(range(1, plane)) + [0]
    first = {}
    for k in order:
        first[k] = send(rows(x, 1 - s, mates[k]), one.at[k], s1.at[k], r1.at[k], peer)
    second = {}
    for k in order:
        first[k].wait_recv()
        mine = rows(x, s, mates[k])[...] + one[k]
        if k == 0:
            acc[...] = mine
        else:
            sums[k - 1] = mine
            second[k] = send(
                sums.at[k - 1], two.at[k - 1], s2.at[k - 1], r2.at[k - 1], (s, z * plane + mates[k])
            )
    for k in range(1, plane):
        second[k].wait_recv()
    third = {}
    for k in [1, 2, 3, 0]:
        at = pl.ds(pl.multiple_of(levels[k] * chunk, 8), chunk)
        value = acc[at, :]
        for j in range(plane - 1):
            value = value + two[j, at, :]
        acc[at, :] = value
        if k > 0:
            third[k] = send(
                acc.at[at], three.at[k - 1], s3.at[k - 1], r3.at[k - 1], (s, levels[k] * plane + q)
            )
    value = acc[pl.ds(pl.multiple_of(z * chunk, 8), chunk), :]
    for k in range(1, Z_SIZE):
        third[k].wait_recv()
        value = value + three[k - 1]
    own = rows(out, s, q, z)
    own[...] = value
    up = {}
    for k in range(1, Z_SIZE):
        up[k] = send(own, own, a3s.at[k - 1], a3r.at[k - 1], (s, levels[k] * plane + q))
    across, over = {}, {}

    def spread(k):
        src = rows(out, s, q, lax.rem(z + Z_SIZE - k, Z_SIZE))
        for j in range(1, plane):
            at = (j - 1) * Z_SIZE + k
            across[j, k] = send(src, src, a2s.at[at], a2r.at[at], (s, z * plane + mates[j]))
        over[0, k] = send(src, src, a1s.at[k], a1r.at[k], peer)

    spread(0)
    for k in range(1, Z_SIZE):
        up[k].wait_recv()
        spread(k)
    for k in range(Z_SIZE):
        for j in range(1, plane):
            across[j, k].wait_recv()
            src = rows(out, s, lax.rem(q + plane - j, plane), lax.rem(z + Z_SIZE - k, Z_SIZE))
            at = j * Z_SIZE + k
            over[j, k] = send(src, src, a1s.at[at], a1r.at[at], peer)
    for c in over.values():
        c.wait_recv()
    for group in (first, second, third, up, across, over):
        for c in group.values():
            c.wait_send()


def all_sum(x, devices):
    total = x.shape[0]
    plane = devices // Z_SIZE
    part = total // 2 // plane
    chunk = part // Z_SIZE
    dma = pltpu.SemaphoreType.DMA
    v = pltpu.VMEM
    vm = pl.BlockSpec(memory_space=pltpu.VMEM)
    pairs = [plane, plane - 1, Z_SIZE - 1, Z_SIZE - 1, (plane - 1) * Z_SIZE, plane * Z_SIZE]
    return pl.pallas_call(
        functools.partial(reduce_kernel, plane),
        out_shape=jax.ShapeDtypeStruct(x.shape, F32),
        in_specs=[vm],
        out_specs=vm,
        scratch_shapes=[
            v((plane, part, 128), F32),
            v((plane - 1, part, 128), F32),
            v((plane - 1, part, 128), F32),
            v((Z_SIZE - 1, chunk, 128), F32),
            v((part, 128), F32),
        ]
        + [dma((n,)) for n in pairs for _ in range(2)],
        compiler_params=pltpu.CompilerParams(collective_id=0, has_side_effects=True, vmem_limit_bytes=VMEM_LIMIT),
        name="step_reduce",
    )(x)


def update_kernel(dead_codes, valid_v, total, *refs):
    w, m, v = refs[0:6], refs[6:12], refs[12:18]
    ema_count, ema_sum = refs[18:20]
    norm_o, pair_o = refs[20:22]
    new_o, mom_o, sec_o, low_o = refs[22:28], refs[28:34], refs[34:40], refs[40:46]
    book_o, count_o, sum_o = refs[46:49]
    grads = total[0:ROW_SUMS, :]
    squares = jnp.sum(jnp.sum((grads * grads).reshape(ROW_SUMS // 8, 8, 128), axis=0))
    norm = jnp.sqrt(jnp.full((8, 128), squares, F32))
    norm_o[0] = norm[0, 0]
    factor = (CLIP_NORM / jnp.maximum(norm, CLIP_NORM))[0, 0]
    pair_o[0] = jnp.sum(total[ROW_NUMER : ROW_NUMER + 8, :])
    pair_o[1] = 3.0 * 256.0 * jnp.sum(valid_v[...].astype(F32))

    def apply(t, index, grad):
        g = grad * factor
        first = MOMENT_ONE * m[t][index] + (1.0 - MOMENT_ONE) * g
        second = MOMENT_TWO * v[t][index] + (1.0 - MOMENT_TWO) * g * g
        step = first / (1.0 - MOMENT_ONE**STEP) / (
            jnp.sqrt(second / (1.0 - MOMENT_TWO**STEP)) + ADAM_EPSILON
        )
        weight = w[t][index]
        fresh = weight - LEARN_RATE * (step + WEIGHT_DECAY * weight)
        new_o[t][index] = fresh
        mom_o[t][index] = first
        sec_o[t][index] = second
        low_o[t][index] = fresh.astype(BF16)

    for k in range(3):
        for t in range(9):
            at = k * CONV_ROWS + t * TAP_ROWS
            apply(0, (k, slice(None), pl.ds(t * 128, 128)), total[at : at + 64, :])
        apply(1, (k,), total[ROW_RES + k * 64 : ROW_RES + k * 64 + 64, :])
    for k in range(5):
        apply(2, (k,), total[ROW_FROM + k * 64 : ROW_FROM + k * 64 + 64, :])
    for k in range(2):
        apply(3, (k,), total[ROW_TO + k * 64 : ROW_TO + k * 64 + 64, :])
        apply(4, (k,), total[ROW_PIXEL + k * 48 : ROW_PIXEL + k * 48 + 48, :])
    for k in range(4):
        apply(5, (k,), total[ROW_DOWN + k * 128 : ROW_DOWN + k * 128 + 128, :])

    dead = jnp.concatenate(
        [total[ROW_DEAD : ROW_DEAD + 8, :], jnp.zeros((120, 128), F32)], axis=0
    )
    dead = jnp.transpose(dead)
    for level in range(2):
        for b in range(4):
            lanes = pl.ds(b * 128, 128)
            at = ROW_COUNT + level * 4 + b
            ids = lane_iota((64, 128)) + b * 128
            count = CODE_DECAY * ema_count[level : level + 1, b * 128 : b * 128 + 128] + (
                1.0 - CODE_DECAY
            ) * total[at : at + 1, :]
            at = ROW_SUMS + (level * 4 + b) * 64
            sums = CODE_DECAY * ema_sum[level, :, lanes] + (1.0 - CODE_DECAY) * total[at : at + 64, :]
            for r in range(8):
                taken = ids == dead_codes[level, r]
                count = jnp.where(taken[:1], 1.0, count)
                sums = jnp.where(taken, dead[level * 64 : level * 64 + 64, r : r + 1], sums)
            count_o[level : level + 1, b * 128 : b * 128 + 128] = count
            sum_o[level, :, lanes] = sums
            book_o[level, :, lanes] = sums / count


def update(dead_codes, valid_rows, total, weights, firsts, seconds, ema_count, ema_sum):
    sds = jax.ShapeDtypeStruct
    shapes = [sds((1,), F32), sds((2,), F32)]
    for _ in range(3):
        shapes += [sds(w.shape, F32) for w in weights]
    shapes += [sds(w.shape, BF16) for w in weights]
    shapes += [sds(ema_sum.shape, F32), sds(ema_count.shape, F32), sds(ema_sum.shape, F32)]
    vm = pl.BlockSpec(memory_space=pltpu.VMEM)
    sm = pl.BlockSpec(memory_space=pltpu.SMEM)
    return pl.pallas_call(
        update_kernel,
        out_shape=shapes,
        in_specs=[sm] + [vm] * 22,
        out_specs=[sm, sm] + [vm] * 27,
        compiler_params=pltpu.CompilerParams(vmem_limit_bytes=VMEM_LIMIT),
        name="step_update",
    )(dead_codes, valid_rows, total, *weights, *firsts, *seconds, ema_count, ema_sum)


def body(sections, devices, *args):
    pixels, codes_top, codes_bottom, valid_rows, dead_codes, dead_source = args[:6]
    weights, firsts, seconds = args[6:12], args[12:18], args[18:24]
    codebook, ema_count, ema_sum = args[24:27]
    batches, part_rows, lanes = pixels.shape
    height = lanes // 3
    parts = height // part_rows
    share = batches // (sections * parts)
    section = lax.axis_index("section")
    device = lax.axis_index("dp")
    part = device % parts
    image = device // parts

    assert parts == 2 and sections == 2
    first = (section * parts + part) * share
    pairs = [(base + p, base + 1 - p) for base in range(0, devices, 2) for p in range(2)]

    def swapped(x):
        theirs = (section * parts + 1 - part) * share
        return (x, lax.ppermute(lax.dynamic_slice_in_dim(x, theirs, share, 0), "dp", pairs))

    def turn(arrays):
        return [x.transpose(0, 2, 1) if x.shape[2] == 64 else x for x in arrays]

    ct, cb, pix = swapped(codes_top), swapped(codes_bottom), swapped(pixels)
    place = jnp.stack([first, image, part]).astype(jnp.int32)
    multiple = 8 * sections * devices
    total_rows = -(-ROW_END // multiple) * multiple
    weights, firsts, seconds = turn(weights), turn(firsts), turn(seconds)
    codebook, ema_sum = turn([codebook, ema_sum])
    packed = compute(place, valid_rows, dead_source, pix, ct, cb, weights, codebook, total_rows)
    total = all_sum(packed, devices)
    outs = update(dead_codes, valid_rows, total, weights, firsts, seconds, ema_count, ema_sum)
    outs = [x.transpose(0, 2, 1) if len(x.shape) == 3 and x.shape[1] == 64 and turned else x for x, turned in zip(outs, TURNED)]
    return (outs[0].reshape(()),) + tuple(outs[1:])


TURNED = (False, False) + (True, False, False, True, False, False) * 4 + (True, False, True)


def solution(mesh):
    return jax.shard_map(
        functools.partial(body, mesh.shape["section"], mesh.shape["dp"]),
        mesh=mesh,
        in_specs=(P(None, "dp", None),) * 3 + (P(),) * 24,
        out_specs=(P(),) * 29,
        check_vma=False,
    )
```

```python
import functools

import jax
import jax.numpy as jnp
from jax import lax
from jax.experimental import pallas as pl
from jax.experimental.pallas import tpu as pltpu
from jax.sharding import PartitionSpec as P

STEP = 10
COMMIT_WEIGHT = 0.25
CODE_DECAY = 0.9
CLIP_NORM = 0.001
LEARN_RATE = 0.03
MOMENT_ONE = 0.9
MOMENT_TWO = 0.999
WEIGHT_DECAY = 0.01
ADAM_EPSILON = 1e-08

F32 = jnp.float32
BF16 = jnp.bfloat16
VMEM_LIMIT = 62 * 1024 * 1024
PARTS = 2

MESH = pl.DeviceIdType.MESH
Z_SIZE = 4
DEAD = 8
GROUPS = (
    (("conv2", 576), ("res2", 64), ("from0", 64), ("pixel1", 48)),
    (("sums", 512), ("count", 8), ("dead", 8), ("numer", 8)),
    (("conv1", 576), ("res1", 64), ("from1", 64), ("from2", 64), ("from3", 64), ("from4", 64), ("to1", 64), ("to0", 64)),
    (("conv0", 576), ("res0", 64), ("pixel0", 48), ("down", 512)),
)


def row_layout(devices):
    multiple = 16 * devices
    at, groups, row = {}, [], 0
    for group in GROUPS:
        start = row
        for name, size in group:
            at[name] = row
            row += size
        row = start + -(-(row - start) // multiple) * multiple
        groups.append((start, row - start))
    return at, groups, row


def mm(x, w):
    return lax.dot_general(x, w, (((1,), (0,)), ((), ())), preferred_element_type=F32)


def mm_t(x, w):
    return lax.dot_general(x, w, (((1,), (1,)), ((), ())), preferred_element_type=F32)


def mm_w(x, g):
    return lax.dot_general(x, g, (((0,), (0,)), ((), ())), preferred_element_type=F32)


def lane_iota(shape):
    return lax.broadcasted_iota(jnp.int32, shape, len(shape) - 1)


def low_half(shape):
    return lane_iota(shape) % 128 < 64


def sigmoid(x):
    return 0.5 * jnp.tanh(0.5 * x) + 0.5


def slope(a):
    s = sigmoid(a)
    return s * (1.0 + a * (1.0 - s))


def shift_rows(x, by):
    rows = x.shape[1]
    moved = pltpu.roll(x, by % rows, 1)
    ids = lax.broadcasted_iota(jnp.int32, x.shape, 1)
    edge = 0 if by == 1 else rows - 1
    return jnp.where(ids == edge, 0.0, moved)


def flat(x):
    return x.reshape(x.shape[0] * x.shape[1], x.shape[2])


def pair_diag(w):
    zero = jnp.zeros_like(w)
    return jnp.concatenate(
        [jnp.concatenate([w, zero], axis=1), jnp.concatenate([zero, w], axis=1)], axis=0
    )


def swap_halves(x):
    return pltpu.roll(x, 64, len(x.shape) - 1)


def partners_of(plane):
    s = lax.axis_index("section")
    d = lax.axis_index("dp")
    z, q = lax.div(d, plane), lax.rem(d, plane)
    peer = (1 - s, d)
    mates = [lax.rem(q + k, plane) for k in range(plane)]
    levels = [lax.rem(z + k, Z_SIZE) for k in range(Z_SIZE)]
    partners = [peer] + [(s, z * plane + m) for m in mates[1:]] + [(s, l * plane + q) for l in levels[1:]]
    return s, z, q, peer, mates, levels, partners


class Reduction:
    def __init__(self, plane, base, total, x, out, one, two, sums, three, acc, ssem, rsem):
        half, part = total // 2, total // 2 // plane
        chunk = part // Z_SIZE
        s, z, q, peer, mates, levels, _ = partners_of(plane)
        mine = base + s * half
        self.x, self.out, self.one, self.two, self.sums, self.three, self.acc = x, out, one, two, sums, three, acc
        self.plane, self.part, self.chunk = plane, part, chunk
        self.own = mine + q * part + z * chunk
        self.z_row = z * chunk
        self.mates, self.mine = mates, mine
        to_mates = [(s, z * plane + m) for m in mates[1:]]
        to_levels = [(s, l * plane + q) for l in levels[1:]]
        moves = [(self.rows(x, base + (1 - s) * half, half), one, peer)]
        moves += [(sums.at[k], two.at[k], to) for k, to in enumerate(to_mates)]
        moves += [
            (self.rows(acc, l * chunk, chunk), three.at[k], to)
            for k, (l, to) in enumerate(zip(levels[1:], to_levels))
        ]
        own = self.rows(out, self.own, chunk)
        moves += [(own, own, to) for to in to_levels]
        own = self.rows(out, mine + q * part, part)
        moves += [(own, own, to) for to in to_mates]
        own = self.rows(out, mine, half)
        moves += [(own, own, peer)]
        self.moves, self.ssem, self.rsem = moves, ssem, rsem
        a, b = plane - 1, Z_SIZE - 1
        stops = [0, 1, 1 + a, 1 + a + b, 1 + a + 2 * b, 1 + 2 * a + 2 * b, 2 + 2 * a + 2 * b]
        self.stage = [range(lo, hi) for lo, hi in zip(stops, stops[1:])]

    def rows(self, ref, start, size):
        return ref.at[pl.ds(pl.multiple_of(start, 8), size)]

    def copy(self, k):
        src, dst, to = self.moves[k]
        return pltpu.make_async_remote_copy(
            src, dst, self.ssem.at[k], self.rsem.at[k], device_id=to, device_id_type=MESH
        )

    def step(self, number):
        if number > 0:
            for k in self.stage[number - 1]:
                self.copy(k).wait_recv()
        part, chunk = self.part, self.chunk
        if number == 1:
            for k in list(range(1, self.plane)) + [0]:
                at = self.mates[k] * part
                value = self.rows(self.x, self.mine + at, part)[...] + self.rows(self.one, at, part)[...]
                if k == 0:
                    self.acc[...] = value
                else:
                    self.sums[k - 1] = value
                    self.copy(k).start()
            return
        if number == 2:
            value = self.acc[...]
            for j in range(self.plane - 1):
                value = value + self.two[j]
            self.acc[...] = value
        if number == 3:
            value = self.rows(self.acc, self.z_row, chunk)[...]
            for k in range(1, Z_SIZE):
                value = value + self.three[k - 1]
            self.rows(self.out, self.own, chunk)[...] = value
        if number < 6:
            for k in self.stage[number]:
                self.copy(k).start()
        else:
            for k in range(len(self.moves)):
                self.copy(k).wait_send()


def reduce_scratch(plane, total):
    part = total // 2 // plane
    chunk = part // Z_SIZE
    v = pltpu.VMEM
    count = 2 + 2 * (plane - 1) + 2 * (Z_SIZE - 1)
    return [
        v((total // 2, 128), F32),
        v((plane - 1, part, 128), F32),
        v((plane - 1, part, 128), F32),
        v((Z_SIZE - 1, chunk, 128), F32),
        v((part, 128), F32),
        pltpu.SemaphoreType.DMA((count,)),
        pltpu.SemaphoreType.DMA((count,)),
    ]


REDUCE_REFS = 7
SCRATCH = (
    "b_fwd", "b_bwd", "wo_d", "from_d", "to_d", "up_d", "pix_d", "down_b", "book_a", "book_b", "sel", "hot",
    "near", "near_t", "quant_t", "patches", "stem", "xs", "xs_top", "wide", "res", "act", "act_t", "low",
    "low_t", "lat_t", "resid", "gup", "gquant", "gtop", "d_two", "d_two_t", "d_slots", "acc_conv",
    "acc_res", "acc_from", "acc_up", "acc_to", "acc_pix", "acc_down", "acc_sums", "acc_count", "acc_dead",
    "acc_num", "pix", "pix_far", "ct_near", "ct_far", "cb_near", "cb_far", "in_sems", "weight_sems",
    "packed", "valid_s", "valid_v", "dead_source", "codes_t", "codes_b", "w_conv", "w_res", "w_from", "w_to",
    "w_pix", "w_down", "book",
)


def scratch_of(share, height, valid, dead, pixels, ct, cb, weights, total_rows, plane, groups):
    pairs, rows = height // 8, height // 8
    pairs_t = pairs // 2
    n, n_t = pairs * 2 * rows, pairs_t * rows
    v = pltpu.VMEM
    shapes = dict(
        b_fwd=v((3, 256, 768), BF16),
        b_bwd=v((3, 768, 256), BF16),
        wo_d=v((3, 128, 256), BF16),
        from_d=v((128, 256), BF16),
        to_d=v((2, 128, 256), BF16),
        up_d=v((128, 1024), BF16),
        pix_d=v((2, 128, 256), BF16),
        down_b=v((512, 128), BF16),
        book_a=v((2, 256, 512), BF16),
        book_b=v((2, 256, 512), BF16),
        sel=v((height, height), BF16),
        hot=v((n, 512), BF16),
        near=v((share, n, 128), F32),
        near_t=v((share, n_t, 128), F32),
        quant_t=v((share, n_t, 128), BF16),
        patches=v((share, n, 128), BF16),
        stem=v((share, pairs, 2, rows, 256), BF16),
        xs=v((share, pairs, 4, rows, 256), BF16),
        xs_top=v((share, pairs_t, 3, rows, 256), BF16),
        wide=v((pairs + 2, 2, rows, 256), F32),
        res=v((pairs, 2, rows, 256), F32),
        act=v((share, n, 128), F32),
        act_t=v((share, n_t, 128), F32),
        low=v((share, n, 256), BF16),
        low_t=v((share, n_t, 256), BF16),
        lat_t=v((n_t, 128), F32),
        resid=v((share, n, 128), F32),
        gup=v((share, pairs, 2, rows, 256), F32),
        gquant=v((share, n, 128), F32),
        gtop=v((share, n_t, 256), F32),
        d_two=v((pairs + 2, 2, rows, 128), F32),
        d_two_t=v((share, pairs_t + 2, rows, 128), F32),
        d_slots=v((pairs, 4, rows, 256), BF16),
        acc_conv=v((3, 256, 768), F32),
        acc_res=v((3, 128, 256), F32),
        acc_from=v((128, 256), F32),
        acc_up=v((128, 1024), F32),
        acc_to=v((2, 128, 256), F32),
        acc_pix=v((2, 128, 256), F32),
        acc_down=v((512, 128), F32),
        acc_sums=v((2, 128, 512), F32),
        acc_count=v((2, 8, 512), F32),
        acc_dead=v((DEAD, 128), F32),
        acc_num=v((8, 128), F32),
        pix=v((share,) + pixels.shape[1:], pixels.dtype),
        pix_far=v((share,) + pixels.shape[1:], pixels.dtype),
        ct_near=v((share,) + ct.shape[1:], ct.dtype),
        ct_far=v((share,) + ct.shape[1:], ct.dtype),
        cb_near=v((share,) + cb.shape[1:], cb.dtype),
        cb_far=v((share,) + cb.shape[1:], cb.dtype),
        in_sems=pltpu.SemaphoreType.DMA((9,)),
        codes_t=v((share, height // 8, height // 8), F32),
        codes_b=v((share, height // 4, height // 4), F32),
        weight_sems=pltpu.SemaphoreType.DMA((10,)),
        valid_s=pltpu.SMEM(valid.shape, valid.dtype),
        valid_v=v(valid.shape, valid.dtype),
        dead_source=pltpu.SMEM(dead.shape, dead.dtype),
        packed=v((total_rows, 128), F32),
    )
    for name, w in zip(SCRATCH[-7:], weights):
        shapes[name] = v(w.shape, w.dtype)
    scratch = [shapes[name] for name in SCRATCH]
    for _, size in groups:
        scratch += reduce_scratch(plane, size)
    return scratch


class Refs:
    def __init__(self, names, refs):
        for name, ref in zip(names, refs):
            setattr(self, name, ref)


def compute_kernel(devices, valid_rows, dead_rows, pixels, codes_top, codes_bottom, *refs):
    weights_hbm, out, scratch = refs[:7], refs[7], refs[8:]
    r = Refs(SCRATCH, scratch)
    reduce_refs = scratch[len(SCRATCH) :]
    plane = devices // Z_SIZE
    at, groups, _ = row_layout(devices)
    packed = r.packed
    section, _, _, _, _, _, partners = partners_of(plane)
    device = lax.axis_index("dp")
    part, image = lax.rem(device, 2), lax.div(device, 2)
    share = r.pix.shape[0]
    first = (section * 2 + part) * share
    theirs = (section * 2 + 1 - part) * share
    mate = (section, device + 1 - 2 * part)
    height = 2 * r.pix.shape[1]
    pairs, rows = r.res.shape[0], r.res.shape[2]
    pairs_t = r.xs_top.shape[1]
    n, n_t = pairs * 2 * rows, pairs_t * rows
    ch = pairs // PARTS
    starts = range(0, pairs, ch)
    size = ch * 2 * rows

    def span(c0):
        return pl.ds(c0 * 2 * rows, size)

    inputs = (
        (pixels, r.pix, r.pix_far),
        (codes_top, r.ct_near, r.ct_far),
        (codes_bottom, r.cb_near, r.cb_far),
    )
    barrier = pltpu.get_barrier_semaphore()
    for p in partners:
        pl.semaphore_signal(barrier, inc=1, device_id=p, device_id_type=MESH)
    local, remote, loads = {}, {}, {}
    for k in (1, 2):
        src, near_ref, _ = inputs[k]
        local[k] = pltpu.make_async_copy(src.at[pl.ds(first, share)], near_ref, r.in_sems.at[k])
        local[k].start()
    w_conv, w_res, w_from, w_to, w_pix, w_down, book = [getattr(r, name) for name in SCRATCH[-7:]]
    for k in (6, 2, 0, 1, 3, 4, 5):
        loads[k] = pltpu.make_async_copy(weights_hbm[k], getattr(r, SCRATCH[k - 7]), r.weight_sems.at[k])
        loads[k].start()
    valid_s, valid_v, dead_source = r.valid_s, r.valid_v, r.dead_source
    for k, src, dst in ((7, valid_rows, valid_s), (8, valid_rows, valid_v), (9, dead_rows, dead_source)):
        loads[k] = pltpu.make_async_copy(src, dst, r.weight_sems.at[k])
        loads[k].start()
    local[0] = pltpu.make_async_copy(pixels.at[pl.ds(first, share)], r.pix, r.in_sems.at[0])
    local[0].start()
    pl.semaphore_wait(barrier, len(partners))
    for k in (1, 2, 0):
        src, near_ref, far_ref = inputs[k]
        remote[k] = pltpu.make_async_remote_copy(
            src.at[pl.ds(theirs, share)],
            far_ref,
            r.in_sems.at[3 + k],
            r.in_sems.at[6 + k],
            device_id=mate,
            device_id_type=MESH,
        )
        remote[k].start()

    reductions = []
    for group, (base, count) in enumerate(groups):
        refs = reduce_refs[group * REDUCE_REFS : (group + 1) * REDUCE_REFS]
        reductions.append(Reduction(plane, base, count, packed, out, *refs))

    def begin(group):
        start, size = groups[group]
        used = sum(size for _, size in GROUPS[group])
        if size > used:
            packed[start + used : start + size, :] = jnp.zeros((size - used, 128), F32)
        reductions[group].step(0)

    def steps(*which):
        for group, number in which:
            reductions[group].step(number)

    def between(*per_image):
        def run(img):
            for want, which in enumerate(per_image):
                if which:
                    pl.when(img == want)(functools.partial(steps, *which))

        return run

    def accum(ref, index, value, img):
        ref[index] += value

    def picker(src, start):
        size = src.shape[0]
        ids = lax.broadcasted_iota(jnp.int32, src.shape, 1) + start
        ids = jnp.where(ids >= size, ids - size, ids)
        return (ids == src).astype(F32).astype(BF16)

    for name in SCRATCH:
        if name[:4] == "acc_":
            ref = getattr(r, name)
            ref[...] = jnp.zeros(ref.shape, F32)
    for edge in (0, pairs + 1):
        r.wide[edge] = jnp.zeros(r.wide.shape[1:], F32)
        r.d_two[edge] = jnp.zeros(r.d_two.shape[1:], F32)
    for img in range(share):
        for edge in (0, pairs_t + 1):
            r.d_two_t[img, edge] = jnp.zeros(r.d_two_t.shape[2:], F32)
    for c in loads.values():
        c.wait()
    valid_count = 3.0 * height * jnp.sum(valid_v[...].astype(F32))
    loss_slope = 2.0 / valid_count
    commit_slope = loss_slope * COMMIT_WEIGHT

    zero = jnp.zeros((64, 128), F32)
    for k in range(3):
        for i in range(3):
            t = [w_conv[k, :, pl.ds((i * 3 + j) * 128, 128)] for j in range(3)]
            even = jnp.concatenate([t[1], t[0], zero, t[2]], axis=0).astype(BF16)
            odd = jnp.concatenate([t[2], t[1], t[0], zero], axis=0).astype(BF16)
            both = jnp.concatenate([even, odd], axis=1)
            r.b_fwd[k, :, pl.ds(i * 256, 256)] = both
            r.b_bwd[k, pl.ds((2 - i) * 256, 256), :] = both
        r.wo_d[k] = pair_diag(w_res[k]).astype(BF16)
    r.from_d[...] = pair_diag(w_from[0]).astype(BF16)
    for k in range(2):
        r.to_d[k] = pair_diag(w_to[k]).astype(BF16)
    r.up_d[...] = pair_diag(jnp.concatenate([w_from[k] for k in range(1, 5)], axis=1)).astype(BF16)
    lane = lax.broadcasted_iota(jnp.int32, (128, 48), 0)
    tap = lax.broadcasted_iota(jnp.int32, (128, 48), 1)
    for k in range(2):
        w_low = w_pix[k].astype(BF16)
        for cp in range(2):
            pick = (lane == (tap // 12) * 24 + cp * 12 + tap % 12).astype(F32).astype(BF16)
            r.pix_d[k, :, pl.ds(cp * 128, 128)] = mm(pick, w_low).astype(BF16)
    for k in range(4):
        r.down_b[pl.ds(k * 128, 128), :] = w_down[k].astype(BF16)
    for k in range(2):
        full = book[k]
        hi = full.astype(BF16).astype(F32)
        mid = (full - hi).astype(BF16).astype(F32)
        lo = full - hi - mid
        empty = jnp.zeros_like(full)
        r.book_a[k] = jnp.concatenate([hi, mid, lo, empty], axis=0).astype(BF16)
        r.book_b[k] = jnp.concatenate([mid, hi, empty, lo], axis=0).astype(BF16)
    o = lax.broadcasted_iota(jnp.int32, (height, height), 0)
    quarter = height // 4
    r.sel[...] = picker(8 * (o % rows) + 4 * ((o % quarter) // rows) + o // quarter, part * (height // 2))

    for k in (1, 2):
        local[k].wait()
        remote[k].wait()

    def codes_of(near_ref, far_ref, img, split):
        both = jnp.concatenate([near_ref[img], far_ref[img]], axis=0).astype(F32)
        size = both.shape[0]
        o = lax.broadcasted_iota(jnp.int32, (size, size), 0)
        pick = picker(2 * (o % rows) + o // rows if split else o, part * (size // 2))
        high = jnp.floor(both * (1.0 / 256.0))
        rest = both - 256.0 * high
        return 256.0 * mm(pick, high.astype(BF16)) + mm(pick, rest.astype(BF16))

    for img in range(share):
        r.codes_t[img] = codes_of(r.ct_near, r.ct_far, img, False)
        r.codes_b[img] = codes_of(r.cb_near, r.cb_far, img, True)

    def make_hot(level, img, cp, count, j0, j1):
        c = (r.codes_b if level else r.codes_t)[img]
        side = c.shape[0]
        ids = lax.broadcasted_iota(jnp.int32, (side, 512), 1).astype(F32)
        used = jnp.zeros((8, 512), F32)
        for j in range(j0, j1):
            hot = (c[:, 2 * j + cp : 2 * j + cp + 1] == ids).astype(F32)
            if count:
                used = used + jnp.sum(hot.reshape(side // 8, 8, 512), axis=0)
            r.hot[j * side : (j + 1) * side, :] = hot.astype(BF16)
        return r.hot[j0 * side : j1 * side, :], used

    def near_of(level, img, j0, j1):
        v = []
        used = jnp.zeros((8, 512), F32)
        for cp, table in ((0, r.book_a), (1, r.book_b)):
            hot, more = make_hot(level, img, cp, True, j0, j1)
            used = used + more
            v.append(mm_t(hot, table[level]))
        accum(r.acc_count, level, used, img)
        half = low_half(v[0][:, :128].shape)
        hi = jnp.where(half, v[0][:, :128], v[1][:, :128])
        mid = swap_halves(jnp.where(half, v[1][:, :128], v[0][:, :128]))
        lo = jnp.where(half, v[0][:, 128:], v[1][:, 128:])
        return hi, hi + mid + lo

    def add_sums(level, img, latent, j0, j1):
        hi = latent.astype(BF16).astype(F32)
        lo = latent - hi
        half = low_half(hi.shape)
        even = jnp.where(half, hi, swap_halves(lo)).astype(BF16)
        odd = jnp.where(half, swap_halves(hi), lo).astype(BF16)
        total = mm_w(even, make_hot(level, img, 0, False, j0, j1)[0])
        total = total + mm_w(odd, make_hot(level, img, 1, False, j0, j1)[0])
        accum(r.acc_sums, level, total, img)

    def put_up(img):
        u = mm(r.quant_t[img], r.up_d[...]).reshape(pairs_t, rows, 1024)
        for c in range(pairs_t):
            for cq in range(2):
                for rp in range(2):
                    lanes = (cq * 2 + rp) * 256
                    r.res[2 * c + cq, rp] = u[c, :, lanes : lanes + 256]

    def put_slots(ref, c0, even, odd):
        ref[c0 : c0 + ch, 0] = shift_rows(odd, 1).astype(BF16)
        ref[c0 : c0 + ch, 1] = even.astype(BF16)
        ref[c0 : c0 + ch, 2] = odd.astype(BF16)
        ref[c0 : c0 + ch, 3] = shift_rows(even, -1).astype(BF16)

    def taps_of(ref, c0, c1, rp):
        return jnp.concatenate([flat(ref[c0:c1, rp + t]) for t in range(3)], axis=1)

    def gather_wide(c0, c1, rp):
        before = r.wide[c0:c1, rp, :, 128:]
        after = r.wide[c0 + 2 : c1 + 2, rp, :, 128:]
        return r.wide[c0 + 1 : c1 + 1, rp, :, :128] + jnp.where(low_half(before.shape), before, after)

    def conv(img, k, then):
        for c0 in starts:
            for rp in range(2):
                y = mm_t(taps_of(r.xs.at[img], c0, c0 + ch, rp), r.b_fwd[k])
                r.wide[c0 + 1 : c0 + 1 + ch, rp] = y.reshape(ch, rows, 256)
        for c0 in starts:
            a = jnp.stack([gather_wide(c0, c0 + ch, rp) for rp in range(2)], axis=1).reshape(size, 128)
            r.act[img, span(c0), :] = a
            hidden = (a * sigmoid(a)).astype(BF16)
            y = r.res[c0 : c0 + ch].reshape(size, 256) + mm(hidden, r.wo_d[k])
            y = y.astype(BF16)
            r.low[img, span(c0), :] = y
            then(img, c0, y)

    def add_num(x):
        r.acc_num[...] += jnp.sum(x.reshape(x.shape[0] // 8, 8, 128), axis=0)

    def decode_forward(img):
        hi, full = near_of(0, img, 0, pairs_t)
        r.near_t[img] = full
        r.quant_t[img] = hi.astype(BF16)
        put_up(img)
        for c0 in starts:
            hi, full = near_of(1, img, c0, c0 + ch)
            r.near[img, span(c0), :] = full
            x = mm(hi.astype(BF16), r.from_d[...]).reshape(ch, 2, rows, 256) + r.res[c0 : c0 + ch]
            r.res[c0 : c0 + ch] = x
            put_slots(r.xs.at[img], c0, x[:, 0], x[:, 1])
        conv(img, 2, rebuild)

    def rebuild(img, c0, low):
        r.resid[img, span(c0), :] = mm_t(low, r.pix_d[1])

    def make_patches(img):
        size = 2 * rows
        picked = mm(r.sel[...], jnp.concatenate([r.pix[img], r.pix_far[img]], axis=0))
        lanes24 = lane_iota((size, 128))
        for c2 in range(pairs):
            tile = jnp.zeros((size, 128), F32)
            for i in range(4):
                start, want = 24 * c2, 24 * i
                block = start // 128 * 128
                row = picked[i * size : (i + 1) * size]
                piece = pltpu.roll(row[:, block : block + 128], (want - start % 128) % 128, 1)
                inside = min(24, 128 - start % 128)
                tile = jnp.where((lanes24 >= want) & (lanes24 < want + inside), piece, tile)
                if inside < 24:
                    piece = pltpu.roll(row[:, block + 128 : block + 256], want + inside, 1)
                    tile = jnp.where((lanes24 >= want + inside) & (lanes24 < want + 24), piece, tile)
            r.patches[img, c2 * size : (c2 + 1) * size, :] = tile.astype(BF16)

    def hidden_back(img, g, a, k):
        g_low = g.astype(BF16)
        s = sigmoid(a)
        accum(r.acc_res, k, mm_w((a * s).astype(BF16), g_low), img)
        return (mm_t(g_low, r.wo_d[k]) * (s * (1.0 + a * (1.0 - s)))).astype(BF16).astype(F32)

    def conv_back(img, k, c0):
        here, before, after = r.d_two[c0 + 1 : c0 + 1 + ch], r.d_two[c0 : c0 + ch], r.d_two[c0 + 2 : c0 + 2 + ch]
        d = jnp.concatenate([here, jnp.where(low_half(here.shape), after, before)], axis=3)
        put_slots(r.d_slots, c0, d[:, 0], d[:, 1])
        outs, total = [], None
        for rp in range(2):
            taps = taps_of(r.d_slots, c0, c0 + ch, rp)
            outs.append(mm(taps, r.b_bwd[k]).reshape(ch, rows, 256))
            more = mm_w(flat(r.xs[img, c0 : c0 + ch, rp + 1]), taps)
            total = more if total is None else total + more
        accum(r.acc_conv, k, total, img)
        return jnp.stack(outs, axis=1)

    def decode_back(img):
        limit = valid_s[first + img, image]
        lane = lane_iota((ch, 2, rows, 128))
        pixel_row = (
            8 * lax.broadcasted_iota(jnp.int32, lane.shape, 2)
            + 4 * lax.broadcasted_iota(jnp.int32, lane.shape, 1)
            + lane // 24
        )
        keep = ((pixel_row < limit) & (lane < 96)).astype(F32).reshape(size, 128)
        for c0 in starts:
            at_rows = span(c0)
            diff = keep * (r.resid[img, at_rows, :] - r.patches[img, at_rows, :].astype(F32))
            add_num(diff * diff)
            g_re = (loss_slope * diff).astype(BF16)
            accum(r.acc_pix, 1, mm_w(g_re, r.low[img, at_rows, :]), img)
            g = mm(g_re, r.pix_d[1])
            r.res[c0 : c0 + ch] = g.reshape(ch, 2, rows, 256)
            d = hidden_back(img, g, r.act[img, at_rows, :], 2)
            r.d_two[c0 + 1 : c0 + 1 + ch] = d.reshape(ch, 2, rows, 128)

    def decode_in_back(img):
        for c0 in starts:
            g = r.res[c0 : c0 + ch] + conv_back(img, 2, c0)
            r.gup[img, c0 : c0 + ch] = g
            g_low = g.reshape(size, 256).astype(BF16)
            accum(r.acc_from, Ellipsis, mm_w(r.near[img, span(c0), :].astype(BF16), g_low), img)
            r.gquant[img, span(c0), :] = mm_t(g_low, r.from_d[...])

    def dead_lines(level, img, lat_ref):
        side = pairs * (level + 1)
        images = valid_s.shape[1]
        for k in range(DEAD):
            pos = dead_source[level, k]
            col, row_all = lax.rem(pos, side), lax.div(pos, side)
            row, img_all = lax.rem(row_all, side), lax.div(row_all, side)
            mine = (lax.rem(img_all, images) == image) & (lax.div(img_all, images) == first + img)
            if level == 0:
                place = lax.div(col, 2) * rows + row
            else:
                place = lax.div(col, 2) * (2 * rows) + lax.rem(row, 2) * rows + lax.div(row, 2)
            line = lat_ref[pl.ds(place, 1), :]
            line = jnp.where(low_half(line.shape) == (lax.rem(col, 2) == 0), line, 0.0)
            line = line + swap_halves(line)
            line = jnp.where(low_half(line.shape) == (level == 0), line, 0.0)
            r.acc_dead[k : k + 1, :] += line * mine.astype(F32)

    def top_forward(img):
        for c0 in starts:
            pre = mm(r.patches[img, span(c0), :], r.pix_d[0])
            r.stem[img, c0 : c0 + ch] = (pre * sigmoid(pre)).astype(BF16).reshape(ch, 2, rows, 256)
        xs = r.xs_top.at[img]
        inputs = []
        for cq in range(2):
            x = mm(stem_blocks(img, cq), r.down_b[...])
            inputs.append(x)
            x = x.reshape(pairs_t, rows, 128)
            lanes = pl.ds(cq * 128, 128)
            xs[:, 0, :, lanes] = shift_rows(x, 1).astype(BF16)
            xs[:, 1, :, lanes] = x.astype(BF16)
            xs[:, 2, :, lanes] = shift_rows(x, -1).astype(BF16)
        r.wide[pairs_t + 1, 0] = jnp.zeros((rows, 256), F32)
        r.wide[1 : pairs_t + 1, 0] = mm_t(taps_of(xs, 0, pairs_t, 0), r.b_fwd[0]).reshape(pairs_t, rows, 256)
        a = flat(gather_wide(0, pairs_t, 0))
        r.act_t[img] = a
        hidden = (a * sigmoid(a)).astype(BF16)
        y = (jnp.concatenate(inputs, axis=1) + mm(hidden, r.wo_d[0])).astype(BF16)
        r.low_t[img] = y
        latent = mm_t(y, r.to_d[0])
        r.lat_t[...] = latent
        diff = latent - r.near_t[img]
        r.near_t[img] = diff
        add_num(COMMIT_WEIGHT * diff * diff)
        add_sums(0, img, latent, 0, pairs_t)
        dead_lines(0, img, r.lat_t)

    def stem_blocks(img, cq):
        return jnp.concatenate(
            [
                jnp.concatenate([r.stem[img, 2 * c + cq, rp] for rp in range(2)], axis=1)
                for c in range(pairs_t)
            ],
            axis=0,
        )

    def bottom_forward(img):
        put_up(img)
        for c0 in starts:
            x = r.stem[img, c0 : c0 + ch].astype(F32) + r.res[c0 : c0 + ch]
            r.res[c0 : c0 + ch] = x
            put_slots(r.xs.at[img], c0, x[:, 0], x[:, 1])
        conv(img, 1, bottom_latent)
        dead_lines(1, img, r.resid.at[0])

    def bottom_latent(img, c0, low):
        latent = mm_t(low, r.to_d[1])
        r.resid[0, span(c0), :] = latent
        diff = latent - r.near[img, span(c0), :]
        r.near[img, span(c0), :] = diff
        add_num(COMMIT_WEIGHT * diff * diff)
        add_sums(1, img, latent, c0, c0 + ch)

    def bottom_back(img):
        for c0 in starts:
            at_rows = span(c0)
            g_lat = (r.gquant[img, at_rows, :] + commit_slope * r.near[img, at_rows, :]).astype(BF16)
            accum(r.acc_to, 1, mm_w(g_lat, r.low[img, at_rows, :]), img)
            g = mm(g_lat, r.to_d[1])
            r.res[c0 : c0 + ch] = g.reshape(ch, 2, rows, 256)
            d = hidden_back(img, g, r.act[img, at_rows, :], 1)
            r.d_two[c0 + 1 : c0 + 1 + ch] = d.reshape(ch, 2, rows, 128)

    def bottom_in_back(img):
        half, size_t = ch // 2, ch // 2 * rows
        for c0 in starts:
            g = r.res[c0 : c0 + ch] + conv_back(img, 1, c0)
            r.xs[img, c0 : c0 + ch, 0] = g[:, 0].astype(BF16)
            r.xs[img, c0 : c0 + ch, 3] = g[:, 1].astype(BF16)
            total = (g + r.gup[img, c0 : c0 + ch]).astype(BF16).reshape(half, 2, 2, rows, 256)
            wide_g = jnp.concatenate(
                [total[:, cq, rp].reshape(size_t, 256) for cq in range(2) for rp in range(2)], axis=1
            )
            here = pl.ds(c0 // 2 * rows, size_t)
            accum(r.acc_up, Ellipsis, mm_w(r.quant_t[img, here, :], wide_g), img)
            g_q = mm_t(wide_g, r.up_d[...]).astype(BF16).astype(F32)
            g_lat = (g_q + commit_slope * r.near_t[img, here, :]).astype(BF16)
            accum(r.acc_to, 0, mm_w(g_lat, r.low_t[img, here, :]), img)
            r.gtop[img, here, :] = mm(g_lat, r.to_d[0])

    def top_back(img):
        g = r.gtop[img]
        d = hidden_back(img, g, r.act_t[img], 0)
        r.d_two_t[img, 1 : pairs_t + 1] = d.reshape(pairs_t, rows, 128)
        here, before, after = (
            r.d_two_t[img, 1 : pairs_t + 1],
            r.d_two_t[img, :pairs_t],
            r.d_two_t[img, 2:],
        )
        d = jnp.concatenate([here, jnp.where(low_half(here.shape), after, before)], axis=2)
        taps = jnp.concatenate(
            [flat(x).astype(BF16) for x in (shift_rows(d, 1), d, shift_rows(d, -1))], axis=1
        )
        accum(r.acc_conv, 0, mm_w(flat(r.xs_top[img, :, 1]), taps), img)
        g_low = (g + mm(taps, r.b_bwd[0])).astype(BF16)
        total = None
        sl = slope(mm(r.patches[img], r.pix_d[0])).reshape(pairs, 2, rows, 256)
        g_b = jnp.stack([r.xs[img, :, 0], r.xs[img, :, 3]], axis=1).astype(F32) * sl
        r.d_slots[:, 2:4] = g_b.astype(BF16)
        for cq in range(2):
            g_cq = g_low[:, cq * 128 : cq * 128 + 128]
            more = mm_w(stem_blocks(img, cq), g_cq)
            total = more if total is None else total + more
            g_st = mm_t(g_cq, r.down_b[...]).reshape(pairs_t, rows, 512)
            for c in range(pairs_t):
                for rp in range(2):
                    g_t = g_st[c, :, rp * 256 : rp * 256 + 256] * sl[2 * c + cq, rp]
                    r.d_slots[2 * c + cq, rp] = g_t.astype(BF16)
        accum(r.acc_down, Ellipsis, total, img)
        p = r.patches[img]
        more = mm_w(p, r.d_slots[:, 0:2].reshape(n, 256)) + mm_w(p, r.d_slots[:, 2:4].reshape(n, 256))
        accum(r.acc_pix, 0, more, img)

    def put(name, value):
        packed[at[name] : at[name] + value.shape[0], :] = value

    def pack_conv(k):
        for i in range(3):
            lanes = (2 - i) * 256
            t = jnp.transpose(r.acc_conv[k, :, lanes : lanes + 256])
            taps = (
                t[64:128, :128] + t[128:192, 128:],
                t[:64, :128] + t[64:128, 128:],
                t[:64, 128:] + t[192:, :128],
            )
            for j in range(3):
                row = at[f"conv{k}"] + (i * 3 + j) * 64
                packed[row : row + 64, :] = taps[j]
        put(f"res{k}", r.acc_res[k, :64, :128] + r.acc_res[k, 64:, 128:])

    def pack_pixel(k):
        for i in range(4):
            even = r.acc_pix[k, 24 * i : 24 * i + 12, :128]
            odd = r.acc_pix[k, 24 * i + 12 : 24 * i + 24, 128:]
            row = at[f"pixel{k}"] + i * 12
            packed[row : row + 12, :] = even + odd

    def each_image(*stages):
        def run(img, _):
            for stage in stages:
                stage(img)
            return 0

        lax.fori_loop(0, share, run, 0)

    each_image(decode_forward)
    local[0].wait()
    remote[0].wait()
    each_image(make_patches, decode_back, decode_in_back)
    pack_conv(2)
    pack_pixel(1)
    put("from0", r.acc_from[:64, :128] + r.acc_from[64:, 128:])
    begin(0)
    each_image(top_forward, between([(0, 1)], [(0, 2)]), bottom_forward)
    for level in range(2):
        sums = r.acc_sums[level, :64, :] + r.acc_sums[level, 64:, :]
        used = jnp.sum(r.acc_count[level], axis=0, keepdims=True)
        for b in range(4):
            row = at["sums"] + (level * 4 + b) * 64
            packed[row : row + 64, :] = sums[:, b * 128 : b * 128 + 128]
            row = at["count"] + level * 4 + b
            packed[row : row + 1, :] = used[:, b * 128 : b * 128 + 128]
    put("dead", r.acc_dead[...])
    put("numer", r.acc_num[...])
    steps((0, 3))
    begin(1)
    each_image(
        bottom_back,
        between([(1, 1)], [(1, 2)]),
        bottom_in_back,
        between([(0, 4)], [(0, 5)]),
    )
    pack_conv(1)
    for k in range(4):
        put(
            f"from{k + 1}",
            r.acc_up[:64, k * 128 : k * 128 + 128] + r.acc_up[64:, 512 + k * 128 : 640 + k * 128],
        )
    for k in range(2):
        put(f"to{k}", r.acc_to[k, :64, :128] + r.acc_to[k, 64:, 128:])
    begin(2)
    steps((1, 3))
    each_image(top_back, between([(2, 1), (0, 6)], []))
    pack_conv(0)
    pack_pixel(0)
    put("down", r.acc_down[...])
    begin(3)
    steps(
        (1, 4), (3, 1), (2, 2), (1, 5), (3, 2), (2, 3), (1, 6),
        (3, 3), (2, 4), (3, 4), (2, 5), (3, 5), (2, 6), (3, 6),
    )


def compute(devices, valid_rows, dead_source, pixels, ct, cb, weights, book):
    plane = devices // Z_SIZE
    _, groups, total_rows = row_layout(devices)
    share = pixels.shape[0] // 4
    vm = pl.BlockSpec(memory_space=pltpu.VMEM)
    anywhere = pl.BlockSpec(memory_space=pl.ANY)
    return pl.pallas_call(
        functools.partial(compute_kernel, devices),
        in_specs=[anywhere] * 12,
        out_specs=vm,
        scratch_shapes=scratch_of(
            share, 2 * pixels.shape[1], valid_rows, dead_source, pixels, ct, cb, [*weights, book], total_rows, plane, groups
        ),
        out_shape=jax.ShapeDtypeStruct((total_rows, 128), F32),
        compiler_params=pltpu.CompilerParams(
            collective_id=0, has_side_effects=True, vmem_limit_bytes=VMEM_LIMIT
        ),
        name="step_compute",
    )(valid_rows, dead_source, pixels, ct, cb, *weights, book)


def update_kernel(devices, dead_codes, valid_v, total, *refs):
    w, m, v = refs[0:6], refs[6:12], refs[12:18]
    ema_count, ema_sum = refs[18:20]
    norm_o, pair_o = refs[20:22]
    new_o, mom_o, sec_o, low_o = refs[22:28], refs[28:34], refs[34:40], refs[40:46]
    book_o, count_o, sum_o = refs[46:49]
    at, groups, _ = row_layout(devices)
    squares = jnp.zeros((8, 128), F32)
    for group in (0, 2, 3):
        start, size = groups[group]
        grads = total[start : start + size, :]
        squares = squares + jnp.sum((grads * grads).reshape(size // 8, 8, 128), axis=0)
    squares = jnp.sum(squares)
    norm = jnp.sqrt(jnp.full((8, 128), squares, F32))
    norm_o[0] = norm[0, 0]
    factor = (CLIP_NORM / jnp.maximum(norm, CLIP_NORM))[0, 0]
    pair_o[0] = jnp.sum(total[at["numer"] : at["numer"] + 8, :])
    pair_o[1] = 3.0 * 256.0 * jnp.sum(valid_v[...].astype(F32))

    def apply(t, index, grad):
        g = grad * factor
        first = MOMENT_ONE * m[t][index] + (1.0 - MOMENT_ONE) * g
        second = MOMENT_TWO * v[t][index] + (1.0 - MOMENT_TWO) * g * g
        step = first / (1.0 - MOMENT_ONE**STEP) / (
            jnp.sqrt(second / (1.0 - MOMENT_TWO**STEP)) + ADAM_EPSILON
        )
        weight = w[t][index]
        fresh = weight - LEARN_RATE * (step + WEIGHT_DECAY * weight)
        new_o[t][index] = fresh
        mom_o[t][index] = first
        sec_o[t][index] = second
        low_o[t][index] = fresh.astype(BF16)

    def piece(name, size, offset=0):
        return total[at[name] + offset : at[name] + offset + size, :]

    for k in range(3):
        for t in range(9):
            apply(0, (k, slice(None), pl.ds(t * 128, 128)), piece(f"conv{k}", 64, t * 64))
        apply(1, (k,), piece(f"res{k}", 64))
    for k in range(5):
        apply(2, (k,), piece(f"from{k}", 64))
    for k in range(2):
        apply(3, (k,), piece(f"to{k}", 64))
        apply(4, (k,), piece(f"pixel{k}", 48))
    for k in range(4):
        apply(5, (k,), piece("down", 128, k * 128))

    dead = jnp.concatenate(
        [piece("dead", DEAD), jnp.zeros((128 - DEAD, 128), F32)], axis=0
    )
    dead = jnp.transpose(dead)
    for level in range(2):
        for b in range(4):
            lanes = pl.ds(b * 128, 128)
            ids = lane_iota((64, 128)) + b * 128
            count = CODE_DECAY * ema_count[level : level + 1, b * 128 : b * 128 + 128] + (
                1.0 - CODE_DECAY
            ) * piece("count", 1, level * 4 + b)
            sums = CODE_DECAY * ema_sum[level, :, lanes] + (
                1.0 - CODE_DECAY
            ) * piece("sums", 64, (level * 4 + b) * 64)
            for r in range(8):
                taken = ids == dead_codes[level, r]
                count = jnp.where(taken[:1], 1.0, count)
                sums = jnp.where(taken, dead[level * 64 : level * 64 + 64, r : r + 1], sums)
            count_o[level : level + 1, b * 128 : b * 128 + 128] = count
            sum_o[level, :, lanes] = sums
            book_o[level, :, lanes] = sums / count


def update(devices, dead_codes, valid_rows, total, weights, firsts, seconds, ema_count, ema_sum):
    sds = jax.ShapeDtypeStruct
    shapes = [sds((1,), F32), sds((2,), F32)]
    for _ in range(3):
        shapes += [sds(w.shape, F32) for w in weights]
    shapes += [sds(w.shape, BF16) for w in weights]
    shapes += [sds(ema_sum.shape, F32), sds(ema_count.shape, F32), sds(ema_sum.shape, F32)]
    vm = pl.BlockSpec(memory_space=pltpu.VMEM)
    sm = pl.BlockSpec(memory_space=pltpu.SMEM)
    return pl.pallas_call(
        functools.partial(update_kernel, devices),
        out_shape=shapes,
        in_specs=[sm] + [vm] * 22,
        out_specs=[sm, sm] + [vm] * 27,
        compiler_params=pltpu.CompilerParams(vmem_limit_bytes=VMEM_LIMIT),
        name="step_update",
    )(dead_codes, valid_rows, total, *weights, *firsts, *seconds, ema_count, ema_sum)


def body(sections, devices, *args):
    pixels, codes_top, codes_bottom, valid_rows, dead_codes, dead_source = args[:6]
    weights, firsts, seconds = args[6:12], args[12:18], args[18:24]
    codebook, ema_count, ema_sum = args[24:27]
    batches, part_rows, lanes = pixels.shape
    height = lanes // 3
    parts = height // part_rows
    assert parts == 2 and sections == 2

    def turn(arrays):
        return [x.transpose(0, 2, 1) if x.shape[2] == 64 else x for x in arrays]

    weights, firsts, seconds = turn(weights), turn(firsts), turn(seconds)
    codebook, ema_sum = turn([codebook, ema_sum])
    total = compute(
        devices, valid_rows, dead_source, pixels, codes_top, codes_bottom, weights, codebook
    )
    outs = update(devices, dead_codes, valid_rows, total, weights, firsts, seconds, ema_count, ema_sum)
    outs = [x.transpose(0, 2, 1) if len(x.shape) == 3 and x.shape[1] == 64 and turned else x for x, turned in zip(outs, TURNED)]
    return (outs[0].reshape(()),) + tuple(outs[1:])


TURNED = (False, False) + (True, False, False, True, False, False) * 4 + (True, False, True)


def solution(mesh):
    return jax.shard_map(
        functools.partial(body, mesh.shape["section"], mesh.shape["dp"]),
        mesh=mesh,
        in_specs=(P(None, "dp", None),) * 3 + (P(),) * 24,
        out_specs=(P(),) * 29,
        check_vma=False,
    )
```

```python
import functools

import jax
import jax.numpy as jnp
from jax import lax
from jax.experimental import pallas as pl
from jax.experimental.pallas import tpu as pltpu
from jax.sharding import PartitionSpec as P

STEP = 10
COMMIT_WEIGHT = 0.25
CODE_DECAY = 0.9
CLIP_NORM = 0.001
LEARN_RATE = 0.03
MOMENT_ONE = 0.9
MOMENT_TWO = 0.999
WEIGHT_DECAY = 0.01
ADAM_EPSILON = 1e-08

F32 = jnp.float32
BF16 = jnp.bfloat16
VMEM_LIMIT = 62 * 1024 * 1024
PARTS = 2

MESH = pl.DeviceIdType.MESH
Z_SIZE = 4
DEAD = 8
GROUPS = (
    (("conv2", 576), ("res2", 64), ("from0", 64), ("pixel1", 48)),
    (("sums", 512), ("count", 8), ("dead", 8), ("numer", 8)),
    (("conv1", 576), ("res1", 64), ("from1", 64), ("from2", 64), ("from3", 64), ("from4", 64), ("to1", 64), ("to0", 64)),
    (("conv0", 576), ("res0", 64), ("pixel0", 48)),
    (("down", 512),),
)


def groups_of(devices):
    if devices > 16:
        return GROUPS[:-2] + (GROUPS[-2] + GROUPS[-1],)
    return GROUPS


def row_layout(devices):
    multiple = 16 * devices
    at, groups, row = {}, [], 0
    for group in groups_of(devices):
        start = row
        for name, size in group:
            at[name] = row
            row += size
        row = start + -(-(row - start) // multiple) * multiple
        groups.append((start, row - start))
    return at, groups, row


def mm(x, w):
    return lax.dot_general(x, w, (((1,), (0,)), ((), ())), preferred_element_type=F32)


def mm_t(x, w):
    return lax.dot_general(x, w, (((1,), (1,)), ((), ())), preferred_element_type=F32)


def mm_w(x, g):
    return lax.dot_general(x, g, (((0,), (0,)), ((), ())), preferred_element_type=F32)


def lane_iota(shape):
    return lax.broadcasted_iota(jnp.int32, shape, len(shape) - 1)


def low_half(shape):
    return lane_iota(shape) % 128 < 64


def sigmoid(x):
    return 0.5 * jnp.tanh(0.5 * x) + 0.5


def slope(a):
    s = sigmoid(a)
    return s * (1.0 + a * (1.0 - s))


def shift_rows(x, by):
    rows = x.shape[1]
    moved = pltpu.roll(x, by % rows, 1)
    ids = lax.broadcasted_iota(jnp.int32, x.shape, 1)
    edge = 0 if by == 1 else rows - 1
    return jnp.where(ids == edge, 0.0, moved)


def flat(x):
    return x.reshape(x.shape[0] * x.shape[1], x.shape[2])


def pair_diag(w):
    zero = jnp.zeros_like(w)
    return jnp.concatenate(
        [jnp.concatenate([w, zero], axis=1), jnp.concatenate([zero, w], axis=1)], axis=0
    )


def swap_halves(x):
    return pltpu.roll(x, 64, len(x.shape) - 1)


def exchange_stages(plane):
    s = lax.axis_index("section")
    d = lax.axis_index("dp")
    z, q = lax.div(d, plane), lax.rem(d, plane)
    mates = [(s, z * plane + lax.rem(q + k, plane)) for k in range(1, plane)]
    levels = [(s, lax.rem(z + k, Z_SIZE) * plane + q) for k in range(1, Z_SIZE)]
    return [(s, [(1 - s, d)]), (q, mates), (z, levels)]


class Reduction:
    def __init__(self, plane, base, total, x, out, *refs):
        stages = exchange_stages(plane)
        landed, (ssem, rsem) = refs[: len(stages)], refs[len(stages) :]
        self.x, self.out, self.landed, self.ssem, self.rsem = x, out, landed, ssem, rsem
        self.moves, self.stage, self.block = [], [], []
        start, size = base, total
        back = []
        for (place, members), buffer in zip(stages, landed):
            count = len(members) + 1
            back.append((start, size, place, members))
            size = size // count
            first = len(self.moves)
            for k, to in enumerate(members):
                theirs = lax.rem(place + k + 1, count)
                self.moves.append((self.rows(x, start + theirs * size, size), buffer.at[k], to))
            self.stage.append(range(first, len(self.moves)))
            start = start + place * size
            self.block.append((start, size, len(members)))
        for _, _, _, members in reversed(back):
            first = len(self.moves)
            own = self.rows(out, start, size)
            self.moves += [(own, own, to) for to in members]
            self.stage.append(range(first, len(self.moves)))
            start, size = back[len(stages) - 1 - (len(self.stage) - len(stages) - 1)][:2]

    def rows(self, ref, start, size):
        return ref.at[pl.ds(pl.multiple_of(start, 8), size)]

    def copy(self, k):
        src, dst, to = self.moves[k]
        return pltpu.make_async_remote_copy(
            src, dst, self.ssem.at[k], self.rsem.at[k], device_id=to, device_id_type=MESH
        )

    def step(self, number):
        stages = len(self.landed)
        if number > 0:
            for k in self.stage[number - 1]:
                self.copy(k).wait_recv()
        if 0 < number <= stages:
            start, size, others = self.block[number - 1]
            value = self.rows(self.x, start, size)[...]
            for k in range(others):
                value = value + self.landed[number - 1][k]
            self.rows(self.out if number == stages else self.x, start, size)[...] = value
        if number < 2 * stages:
            for k in self.stage[number]:
                self.copy(k).start()
        else:
            for k in range(len(self.moves)):
                self.copy(k).wait_send()


def reduce_scratch(plane, total):
    scratch, size, moves = [], total, 0
    for count in (2, plane, Z_SIZE):
        size = size // count
        moves += 2 * (count - 1)
        scratch.append(pltpu.VMEM((count - 1, size, 128), F32))
    return scratch + [pltpu.SemaphoreType.DMA((moves,)), pltpu.SemaphoreType.DMA((moves,))]


REDUCE_REFS = 5
SCRATCH = (
    "b_fwd", "b_bwd", "wo_d", "from_d", "to_d", "up_d", "pix_d", "down_b", "book_a", "book_b", "sel", "hot",
    "near", "near_t", "quant_t", "patches", "stem", "xs", "xs_top", "wide", "res", "act", "act_t", "low",
    "low_t", "lat_t", "resid", "gup", "gquant", "gtop", "d_two", "d_two_t", "d_slots", "acc_conv",
    "acc_res", "acc_from", "acc_up", "acc_to", "acc_pix", "acc_down", "acc_sums", "acc_count", "acc_dead",
    "acc_num", "pix", "pix_far", "ct_near", "ct_far", "cb_near", "cb_far", "in_sems", "weight_sems",
    "packed", "valid_s", "valid_v", "dead_source", "codes_t", "codes_b", "w_conv", "w_res", "w_from", "w_to",
    "w_pix", "w_down", "book",
)


def scratch_of(share, height, valid, dead, pixels, ct, cb, weights, total_rows, plane, groups):
    pairs, rows = height // 8, height // 8
    pairs_t = pairs // 2
    n, n_t = pairs * 2 * rows, pairs_t * rows
    v = pltpu.VMEM
    shapes = dict(
        b_fwd=v((3, 256, 768), BF16),
        b_bwd=v((3, 768, 256), BF16),
        wo_d=v((3, 128, 256), BF16),
        from_d=v((128, 256), BF16),
        to_d=v((2, 128, 256), BF16),
        up_d=v((128, 1024), BF16),
        pix_d=v((2, 128, 256), BF16),
        down_b=v((512, 128), BF16),
        book_a=v((2, 256, 512), BF16),
        book_b=v((2, 256, 512), BF16),
        sel=v((height, height), BF16),
        hot=v((n, 512), BF16),
        near=v((share, n, 128), F32),
        near_t=v((share, n_t, 128), F32),
        quant_t=v((share, n_t, 128), BF16),
        patches=v((share, n, 128), BF16),
        stem=v((share, pairs, 2, rows, 256), BF16),
        xs=v((share, pairs, 4, rows, 256), BF16),
        xs_top=v((share, pairs_t, 3, rows, 256), BF16),
        wide=v((pairs + 2, 2, rows, 256), F32),
        res=v((pairs, 2, rows, 256), F32),
        act=v((share, n, 128), F32),
        act_t=v((share, n_t, 128), F32),
        low=v((share, n, 256), BF16),
        low_t=v((share, n_t, 256), BF16),
        lat_t=v((n_t, 128), F32),
        resid=v((share, n, 128), F32),
        gup=v((share, pairs, 2, rows, 256), F32),
        gquant=v((share, n, 128), F32),
        gtop=v((share, n_t, 256), F32),
        d_two=v((pairs + 2, 2, rows, 128), F32),
        d_two_t=v((share, pairs_t + 2, rows, 128), F32),
        d_slots=v((pairs, 4, rows, 256), BF16),
        acc_conv=v((3, 256, 768), F32),
        acc_res=v((3, 128, 256), F32),
        acc_from=v((128, 256), F32),
        acc_up=v((128, 1024), F32),
        acc_to=v((2, 128, 256), F32),
        acc_pix=v((2, 128, 256), F32),
        acc_down=v((512, 128), F32),
        acc_sums=v((2, 128, 512), F32),
        acc_count=v((2, 8, 512), F32),
        acc_dead=v((DEAD, 128), F32),
        acc_num=v((8, 128), F32),
        pix=v((share,) + pixels.shape[1:], pixels.dtype),
        pix_far=v((share,) + pixels.shape[1:], pixels.dtype),
        ct_near=v((share,) + ct.shape[1:], ct.dtype),
        ct_far=v((share,) + ct.shape[1:], ct.dtype),
        cb_near=v((share,) + cb.shape[1:], cb.dtype),
        cb_far=v((share,) + cb.shape[1:], cb.dtype),
        in_sems=pltpu.SemaphoreType.DMA((9,)),
        codes_t=v((share, height // 8, height // 8), F32),
        codes_b=v((share, height // 4, height // 4), F32),
        weight_sems=pltpu.SemaphoreType.DMA((10,)),
        valid_s=pltpu.SMEM(valid.shape, valid.dtype),
        valid_v=v(valid.shape, valid.dtype),
        dead_source=pltpu.SMEM(dead.shape, dead.dtype),
        packed=v((total_rows, 128), F32),
    )
    for name, w in zip(SCRATCH[-7:], weights):
        shapes[name] = v(w.shape, w.dtype)
    scratch = [shapes[name] for name in SCRATCH]
    for _, size in groups:
        scratch += reduce_scratch(plane, size)
    return scratch


class Refs:
    def __init__(self, names, refs):
        for name, ref in zip(names, refs):
            setattr(self, name, ref)


def compute_kernel(devices, valid_rows, dead_rows, pixels, codes_top, codes_bottom, *refs):
    weights_hbm, out, scratch = refs[:7], refs[7], refs[8:]
    r = Refs(SCRATCH, scratch)
    reduce_refs = scratch[len(SCRATCH) :]
    plane = devices // Z_SIZE
    at, groups, _ = row_layout(devices)
    packed = r.packed
    section = lax.axis_index("section")
    partners = [to for _, members in exchange_stages(plane) for to in members]
    device = lax.axis_index("dp")
    part, image = lax.rem(device, 2), lax.div(device, 2)
    share = r.pix.shape[0]
    first = (section * 2 + part) * share
    theirs = (section * 2 + 1 - part) * share
    mate = (section, device + 1 - 2 * part)
    height = 2 * r.pix.shape[1]
    pairs, rows = r.res.shape[0], r.res.shape[2]
    pairs_t = r.xs_top.shape[1]
    n, n_t = pairs * 2 * rows, pairs_t * rows
    ch = pairs // PARTS
    starts = range(0, pairs, ch)
    size = ch * 2 * rows

    def span(c0):
        return pl.ds(c0 * 2 * rows, size)

    inputs = (
        (pixels, r.pix, r.pix_far),
        (codes_top, r.ct_near, r.ct_far),
        (codes_bottom, r.cb_near, r.cb_far),
    )
    barrier = pltpu.get_barrier_semaphore()
    for p in partners:
        pl.semaphore_signal(barrier, inc=1, device_id=p, device_id_type=MESH)
    local, remote, loads = {}, {}, {}
    for k in (1, 2):
        src, near_ref, _ = inputs[k]
        local[k] = pltpu.make_async_copy(src.at[pl.ds(first, share)], near_ref, r.in_sems.at[k])
        local[k].start()
    w_conv, w_res, w_from, w_to, w_pix, w_down, book = [getattr(r, name) for name in SCRATCH[-7:]]
    for k in (6, 2, 0, 1, 3, 4, 5):
        loads[k] = pltpu.make_async_copy(weights_hbm[k], getattr(r, SCRATCH[k - 7]), r.weight_sems.at[k])
        loads[k].start()
    valid_s, valid_v, dead_source = r.valid_s, r.valid_v, r.dead_source
    for k, src, dst in ((7, valid_rows, valid_s), (8, valid_rows, valid_v), (9, dead_rows, dead_source)):
        loads[k] = pltpu.make_async_copy(src, dst, r.weight_sems.at[k])
        loads[k].start()
    local[0] = pltpu.make_async_copy(pixels.at[pl.ds(first, share)], r.pix, r.in_sems.at[0])
    local[0].start()
    pl.semaphore_wait(barrier, len(partners))
    for k in (1, 2, 0):
        src, near_ref, far_ref = inputs[k]
        remote[k] = pltpu.make_async_remote_copy(
            src.at[pl.ds(theirs, share)],
            far_ref,
            r.in_sems.at[3 + k],
            r.in_sems.at[6 + k],
            device_id=mate,
            device_id_type=MESH,
        )
        remote[k].start()

    reductions = []
    for group, (base, count) in enumerate(groups):
        refs = reduce_refs[group * REDUCE_REFS : (group + 1) * REDUCE_REFS]
        reductions.append(Reduction(plane, base, count, packed, out, *refs))

    def begin(group):
        start, size = groups[group]
        used = sum(size for _, size in groups_of(devices)[group])
        if size > used:
            packed[start + used : start + size, :] = jnp.zeros((size - used, 128), F32)
        reductions[group].step(0)

    def steps(*which):
        for group, number in which:
            reductions[group].step(number)

    def between(*per_image):
        def run(img):
            for want, which in enumerate(per_image):
                if which:
                    pl.when(img == want)(functools.partial(steps, *which))

        return run

    def accum(ref, index, value, img):
        ref[index] += value

    def picker(src, start):
        size = src.shape[0]
        ids = lax.broadcasted_iota(jnp.int32, src.shape, 1) + start
        ids = jnp.where(ids >= size, ids - size, ids)
        return (ids == src).astype(F32).astype(BF16)

    for name in SCRATCH:
        if name[:4] == "acc_":
            ref = getattr(r, name)
            ref[...] = jnp.zeros(ref.shape, F32)
    for edge in (0, pairs + 1):
        r.wide[edge] = jnp.zeros(r.wide.shape[1:], F32)
        r.d_two[edge] = jnp.zeros(r.d_two.shape[1:], F32)
    for img in range(share):
        for edge in (0, pairs_t + 1):
            r.d_two_t[img, edge] = jnp.zeros(r.d_two_t.shape[2:], F32)
    for c in loads.values():
        c.wait()
    valid_count = 3.0 * height * jnp.sum(valid_v[...].astype(F32))
    loss_slope = 2.0 / valid_count
    commit_slope = loss_slope * COMMIT_WEIGHT

    zero = jnp.zeros((64, 128), F32)
    for k in range(3):
        for i in range(3):
            t = [w_conv[k, :, pl.ds((i * 3 + j) * 128, 128)] for j in range(3)]
            even = jnp.concatenate([t[1], t[0], zero, t[2]], axis=0).astype(BF16)
            odd = jnp.concatenate([t[2], t[1], t[0], zero], axis=0).astype(BF16)
            both = jnp.concatenate([even, odd], axis=1)
            r.b_fwd[k, :, pl.ds(i * 256, 256)] = both
            r.b_bwd[k, pl.ds((2 - i) * 256, 256), :] = both
        r.wo_d[k] = pair_diag(w_res[k]).astype(BF16)
    r.from_d[...] = pair_diag(w_from[0]).astype(BF16)
    for k in range(2):
        r.to_d[k] = pair_diag(w_to[k]).astype(BF16)
    r.up_d[...] = pair_diag(jnp.concatenate([w_from[k] for k in range(1, 5)], axis=1)).astype(BF16)
    lane = lax.broadcasted_iota(jnp.int32, (128, 48), 0)
    tap = lax.broadcasted_iota(jnp.int32, (128, 48), 1)
    for k in range(2):
        w_low = w_pix[k].astype(BF16)
        for cp in range(2):
            pick = (lane == (tap // 12) * 24 + cp * 12 + tap % 12).astype(F32).astype(BF16)
            r.pix_d[k, :, pl.ds(cp * 128, 128)] = mm(pick, w_low).astype(BF16)
    for k in range(4):
        r.down_b[pl.ds(k * 128, 128), :] = w_down[k].astype(BF16)
    for k in range(2):
        full = book[k]
        hi = full.astype(BF16).astype(F32)
        mid = (full - hi).astype(BF16).astype(F32)
        lo = full - hi - mid
        empty = jnp.zeros_like(full)
        r.book_a[k] = jnp.concatenate([hi, mid, lo, empty], axis=0).astype(BF16)
        r.book_b[k] = jnp.concatenate([mid, hi, empty, lo], axis=0).astype(BF16)
    o = lax.broadcasted_iota(jnp.int32, (height, height), 0)
    quarter = height // 4
    r.sel[...] = picker(8 * (o % rows) + 4 * ((o % quarter) // rows) + o // quarter, part * (height // 2))

    for k in (1, 2):
        local[k].wait()
        remote[k].wait()

    def codes_of(near_ref, far_ref, img, split):
        both = jnp.concatenate([near_ref[img], far_ref[img]], axis=0).astype(F32)
        size = both.shape[0]
        o = lax.broadcasted_iota(jnp.int32, (size, size), 0)
        pick = picker(2 * (o % rows) + o // rows if split else o, part * (size // 2))
        high = jnp.floor(both * (1.0 / 256.0))
        rest = both - 256.0 * high
        return 256.0 * mm(pick, high.astype(BF16)) + mm(pick, rest.astype(BF16))

    for img in range(share):
        r.codes_t[img] = codes_of(r.ct_near, r.ct_far, img, False)
        r.codes_b[img] = codes_of(r.cb_near, r.cb_far, img, True)

    def make_hot(level, img, cp, count, j0, j1):
        c = (r.codes_b if level else r.codes_t)[img]
        side = c.shape[0]
        ids = lax.broadcasted_iota(jnp.int32, (side, 512), 1).astype(F32)
        used = jnp.zeros((8, 512), F32)
        for j in range(j0, j1):
            hot = (c[:, 2 * j + cp : 2 * j + cp + 1] == ids).astype(F32)
            if count:
                used = used + jnp.sum(hot.reshape(side // 8, 8, 512), axis=0)
            r.hot[j * side : (j + 1) * side, :] = hot.astype(BF16)
        return r.hot[j0 * side : j1 * side, :], used

    def near_of(level, img, j0, j1):
        v = []
        used = jnp.zeros((8, 512), F32)
        for cp, table in ((0, r.book_a), (1, r.book_b)):
            hot, more = make_hot(level, img, cp, True, j0, j1)
            used = used + more
            v.append(mm_t(hot, table[level]))
        accum(r.acc_count, level, used, img)
        half = low_half(v[0][:, :128].shape)
        hi = jnp.where(half, v[0][:, :128], v[1][:, :128])
        mid = swap_halves(jnp.where(half, v[1][:, :128], v[0][:, :128]))
        lo = jnp.where(half, v[0][:, 128:], v[1][:, 128:])
        return hi, hi + mid + lo

    def add_sums(level, img, latent, j0, j1):
        hi = latent.astype(BF16).astype(F32)
        lo = latent - hi
        half = low_half(hi.shape)
        even = jnp.where(half, hi, swap_halves(lo)).astype(BF16)
        odd = jnp.where(half, swap_halves(hi), lo).astype(BF16)
        total = mm_w(even, make_hot(level, img, 0, False, j0, j1)[0])
        total = total + mm_w(odd, make_hot(level, img, 1, False, j0, j1)[0])
        accum(r.acc_sums, level, total, img)

    def put_up(img):
        u = mm(r.quant_t[img], r.up_d[...]).reshape(pairs_t, rows, 1024)
        for c in range(pairs_t):
            for cq in range(2):
                for rp in range(2):
                    lanes = (cq * 2 + rp) * 256
                    r.res[2 * c + cq, rp] = u[c, :, lanes : lanes + 256]

    def put_slots(ref, c0, even, odd):
        ref[c0 : c0 + ch, 0] = shift_rows(odd, 1).astype(BF16)
        ref[c0 : c0 + ch, 1] = even.astype(BF16)
        ref[c0 : c0 + ch, 2] = odd.astype(BF16)
        ref[c0 : c0 + ch, 3] = shift_rows(even, -1).astype(BF16)

    def taps_of(ref, c0, c1, rp):
        return jnp.concatenate([flat(ref[c0:c1, rp + t]) for t in range(3)], axis=1)

    def gather_wide(c0, c1, rp):
        before = r.wide[c0:c1, rp, :, 128:]
        after = r.wide[c0 + 2 : c1 + 2, rp, :, 128:]
        return r.wide[c0 + 1 : c1 + 1, rp, :, :128] + jnp.where(low_half(before.shape), before, after)

    def conv(img, k, then):
        for c0 in starts:
            for rp in range(2):
                y = mm_t(taps_of(r.xs.at[img], c0, c0 + ch, rp), r.b_fwd[k])
                r.wide[c0 + 1 : c0 + 1 + ch, rp] = y.reshape(ch, rows, 256)
        for c0 in starts:
            a = jnp.stack([gather_wide(c0, c0 + ch, rp) for rp in range(2)], axis=1).reshape(size, 128)
            r.act[img, span(c0), :] = a
            hidden = (a * sigmoid(a)).astype(BF16)
            y = r.res[c0 : c0 + ch].reshape(size, 256) + mm(hidden, r.wo_d[k])
            y = y.astype(BF16)
            r.low[img, span(c0), :] = y
            then(img, c0, y)

    def add_num(x):
        r.acc_num[...] += jnp.sum(x.reshape(x.shape[0] // 8, 8, 128), axis=0)

    def decode_forward(img):
        hi, full = near_of(0, img, 0, pairs_t)
        r.near_t[img] = full
        r.quant_t[img] = hi.astype(BF16)
        put_up(img)
        for c0 in starts:
            hi, full = near_of(1, img, c0, c0 + ch)
            r.near[img, span(c0), :] = full
            x = mm(hi.astype(BF16), r.from_d[...]).reshape(ch, 2, rows, 256) + r.res[c0 : c0 + ch]
            r.res[c0 : c0 + ch] = x
            put_slots(r.xs.at[img], c0, x[:, 0], x[:, 1])
        conv(img, 2, rebuild)

    def rebuild(img, c0, low):
        r.resid[img, span(c0), :] = mm_t(low, r.pix_d[1])

    def make_patches(img):
        size = 2 * rows
        picked = mm(r.sel[...], jnp.concatenate([r.pix[img], r.pix_far[img]], axis=0))
        lanes24 = lane_iota((size, 128))
        for c2 in range(pairs):
            tile = jnp.zeros((size, 128), F32)
            for i in range(4):
                start, want = 24 * c2, 24 * i
                block = start // 128 * 128
                row = picked[i * size : (i + 1) * size]
                piece = pltpu.roll(row[:, block : block + 128], (want - start % 128) % 128, 1)
                inside = min(24, 128 - start % 128)
                tile = jnp.where((lanes24 >= want) & (lanes24 < want + inside), piece, tile)
                if inside < 24:
                    piece = pltpu.roll(row[:, block + 128 : block + 256], want + inside, 1)
                    tile = jnp.where((lanes24 >= want + inside) & (lanes24 < want + 24), piece, tile)
            r.patches[img, c2 * size : (c2 + 1) * size, :] = tile.astype(BF16)

    def hidden_back(img, g, a, k):
        g_low = g.astype(BF16)
        s = sigmoid(a)
        accum(r.acc_res, k, mm_w((a * s).astype(BF16), g_low), img)
        return (mm_t(g_low, r.wo_d[k]) * (s * (1.0 + a * (1.0 - s)))).astype(BF16).astype(F32)

    def conv_back(img, k, c0):
        here, before, after = r.d_two[c0 + 1 : c0 + 1 + ch], r.d_two[c0 : c0 + ch], r.d_two[c0 + 2 : c0 + 2 + ch]
        d = jnp.concatenate([here, jnp.where(low_half(here.shape), after, before)], axis=3)
        put_slots(r.d_slots, c0, d[:, 0], d[:, 1])
        outs, total = [], None
        for rp in range(2):
            taps = taps_of(r.d_slots, c0, c0 + ch, rp)
            outs.append(mm(taps, r.b_bwd[k]).reshape(ch, rows, 256))
            more = mm_w(flat(r.xs[img, c0 : c0 + ch, rp + 1]), taps)
            total = more if total is None else total + more
        accum(r.acc_conv, k, total, img)
        return jnp.stack(outs, axis=1)

    def decode_back(img):
        limit = valid_s[first + img, image]
        lane = lane_iota((ch, 2, rows, 128))
        pixel_row = (
            8 * lax.broadcasted_iota(jnp.int32, lane.shape, 2)
            + 4 * lax.broadcasted_iota(jnp.int32, lane.shape, 1)
            + lane // 24
        )
        keep = ((pixel_row < limit) & (lane < 96)).astype(F32).reshape(size, 128)
        for c0 in starts:
            at_rows = span(c0)
            diff = keep * (r.resid[img, at_rows, :] - r.patches[img, at_rows, :].astype(F32))
            add_num(diff * diff)
            g_re = (loss_slope * diff).astype(BF16)
            accum(r.acc_pix, 1, mm_w(g_re, r.low[img, at_rows, :]), img)
            g = mm(g_re, r.pix_d[1])
            r.res[c0 : c0 + ch] = g.reshape(ch, 2, rows, 256)
            d = hidden_back(img, g, r.act[img, at_rows, :], 2)
            r.d_two[c0 + 1 : c0 + 1 + ch] = d.reshape(ch, 2, rows, 128)

    def decode_in_back(img):
        for c0 in starts:
            g = r.res[c0 : c0 + ch] + conv_back(img, 2, c0)
            r.gup[img, c0 : c0 + ch] = g
            g_low = g.reshape(size, 256).astype(BF16)
            accum(r.acc_from, Ellipsis, mm_w(r.near[img, span(c0), :].astype(BF16), g_low), img)
            r.gquant[img, span(c0), :] = mm_t(g_low, r.from_d[...])

    def dead_lines(level, img, lat_ref):
        side = pairs * (level + 1)
        images = valid_s.shape[1]
        for k in range(DEAD):
            pos = dead_source[level, k]
            col, row_all = lax.rem(pos, side), lax.div(pos, side)
            row, img_all = lax.rem(row_all, side), lax.div(row_all, side)
            mine = (lax.rem(img_all, images) == image) & (lax.div(img_all, images) == first + img)
            if level == 0:
                place = lax.div(col, 2) * rows + row
            else:
                place = lax.div(col, 2) * (2 * rows) + lax.rem(row, 2) * rows + lax.div(row, 2)
            line = lat_ref[pl.ds(place, 1), :]
            line = jnp.where(low_half(line.shape) == (lax.rem(col, 2) == 0), line, 0.0)
            line = line + swap_halves(line)
            line = jnp.where(low_half(line.shape) == (level == 0), line, 0.0)
            r.acc_dead[k : k + 1, :] += line * mine.astype(F32)

    def top_forward(img):
        for c0 in starts:
            pre = mm(r.patches[img, span(c0), :], r.pix_d[0])
            r.stem[img, c0 : c0 + ch] = (pre * sigmoid(pre)).astype(BF16).reshape(ch, 2, rows, 256)
        xs = r.xs_top.at[img]
        inputs = []
        for cq in range(2):
            x = mm(stem_blocks(img, cq), r.down_b[...])
            inputs.append(x)
            x = x.reshape(pairs_t, rows, 128)
            lanes = pl.ds(cq * 128, 128)
            xs[:, 0, :, lanes] = shift_rows(x, 1).astype(BF16)
            xs[:, 1, :, lanes] = x.astype(BF16)
            xs[:, 2, :, lanes] = shift_rows(x, -1).astype(BF16)
        r.wide[pairs_t + 1, 0] = jnp.zeros((rows, 256), F32)
        r.wide[1 : pairs_t + 1, 0] = mm_t(taps_of(xs, 0, pairs_t, 0), r.b_fwd[0]).reshape(pairs_t, rows, 256)
        a = flat(gather_wide(0, pairs_t, 0))
        r.act_t[img] = a
        hidden = (a * sigmoid(a)).astype(BF16)
        y = (jnp.concatenate(inputs, axis=1) + mm(hidden, r.wo_d[0])).astype(BF16)
        r.low_t[img] = y
        latent = mm_t(y, r.to_d[0])
        r.lat_t[...] = latent
        diff = latent - r.near_t[img]
        r.near_t[img] = diff
        add_num(COMMIT_WEIGHT * diff * diff)
        add_sums(0, img, latent, 0, pairs_t)
        dead_lines(0, img, r.lat_t)

    def stem_blocks(img, cq):
        return jnp.concatenate(
            [
                jnp.concatenate([r.stem[img, 2 * c + cq, rp] for rp in range(2)], axis=1)
                for c in range(pairs_t)
            ],
            axis=0,
        )

    def bottom_forward(img):
        put_up(img)
        for c0 in starts:
            x = r.stem[img, c0 : c0 + ch].astype(F32) + r.res[c0 : c0 + ch]
            r.res[c0 : c0 + ch] = x
            put_slots(r.xs.at[img], c0, x[:, 0], x[:, 1])
        conv(img, 1, bottom_latent)
        dead_lines(1, img, r.resid.at[0])

    def bottom_latent(img, c0, low):
        latent = mm_t(low, r.to_d[1])
        r.resid[0, span(c0), :] = latent
        diff = latent - r.near[img, span(c0), :]
        r.near[img, span(c0), :] = diff
        add_num(COMMIT_WEIGHT * diff * diff)
        add_sums(1, img, latent, c0, c0 + ch)

    def bottom_back(img):
        for c0 in starts:
            at_rows = span(c0)
            g_lat = (r.gquant[img, at_rows, :] + commit_slope * r.near[img, at_rows, :]).astype(BF16)
            accum(r.acc_to, 1, mm_w(g_lat, r.low[img, at_rows, :]), img)
            g = mm(g_lat, r.to_d[1])
            r.res[c0 : c0 + ch] = g.reshape(ch, 2, rows, 256)
            d = hidden_back(img, g, r.act[img, at_rows, :], 1)
            r.d_two[c0 + 1 : c0 + 1 + ch] = d.reshape(ch, 2, rows, 128)

    def bottom_in_back(img):
        half, size_t = ch // 2, ch // 2 * rows
        for c0 in starts:
            g = r.res[c0 : c0 + ch] + conv_back(img, 1, c0)
            r.xs[img, c0 : c0 + ch, 0] = g[:, 0].astype(BF16)
            r.xs[img, c0 : c0 + ch, 3] = g[:, 1].astype(BF16)
            total = (g + r.gup[img, c0 : c0 + ch]).astype(BF16).reshape(half, 2, 2, rows, 256)
            wide_g = jnp.concatenate(
                [total[:, cq, rp].reshape(size_t, 256) for cq in range(2) for rp in range(2)], axis=1
            )
            here = pl.ds(c0 // 2 * rows, size_t)
            accum(r.acc_up, Ellipsis, mm_w(r.quant_t[img, here, :], wide_g), img)
            g_q = mm_t(wide_g, r.up_d[...]).astype(BF16).astype(F32)
            g_lat = (g_q + commit_slope * r.near_t[img, here, :]).astype(BF16)
            accum(r.acc_to, 0, mm_w(g_lat, r.low_t[img, here, :]), img)
            r.gtop[img, here, :] = mm(g_lat, r.to_d[0])

    def top_back(img):
        g = r.gtop[img]
        d = hidden_back(img, g, r.act_t[img], 0)
        r.d_two_t[img, 1 : pairs_t + 1] = d.reshape(pairs_t, rows, 128)
        here, before, after = (
            r.d_two_t[img, 1 : pairs_t + 1],
            r.d_two_t[img, :pairs_t],
            r.d_two_t[img, 2:],
        )
        d = jnp.concatenate([here, jnp.where(low_half(here.shape), after, before)], axis=2)
        taps = jnp.concatenate(
            [flat(x).astype(BF16) for x in (shift_rows(d, 1), d, shift_rows(d, -1))], axis=1
        )
        accum(r.acc_conv, 0, mm_w(flat(r.xs_top[img, :, 1]), taps), img)
        g_low = (g + mm(taps, r.b_bwd[0])).astype(BF16)
        total = None
        sl = slope(mm(r.patches[img], r.pix_d[0])).reshape(pairs, 2, rows, 256)
        g_b = jnp.stack([r.xs[img, :, 0], r.xs[img, :, 3]], axis=1).astype(F32) * sl
        r.d_slots[:, 2:4] = g_b.astype(BF16)
        for cq in range(2):
            g_cq = g_low[:, cq * 128 : cq * 128 + 128]
            more = mm_w(stem_blocks(img, cq), g_cq)
            total = more if total is None else total + more
            g_st = mm_t(g_cq, r.down_b[...]).reshape(pairs_t, rows, 512)
            for c in range(pairs_t):
                for rp in range(2):
                    g_t = g_st[c, :, rp * 256 : rp * 256 + 256] * sl[2 * c + cq, rp]
                    r.d_slots[2 * c + cq, rp] = g_t.astype(BF16)
        accum(r.acc_down, Ellipsis, total, img)
        p = r.patches[img]
        more = mm_w(p, r.d_slots[:, 0:2].reshape(n, 256)) + mm_w(p, r.d_slots[:, 2:4].reshape(n, 256))
        accum(r.acc_pix, 0, more, img)

    def put(name, value):
        packed[at[name] : at[name] + value.shape[0], :] = value

    def pack_conv(k):
        for i in range(3):
            lanes = (2 - i) * 256
            t = jnp.transpose(r.acc_conv[k, :, lanes : lanes + 256])
            taps = (
                t[64:128, :128] + t[128:192, 128:],
                t[:64, :128] + t[64:128, 128:],
                t[:64, 128:] + t[192:, :128],
            )
            for j in range(3):
                row = at[f"conv{k}"] + (i * 3 + j) * 64
                packed[row : row + 64, :] = taps[j]
        put(f"res{k}", r.acc_res[k, :64, :128] + r.acc_res[k, 64:, 128:])

    def pack_pixel(k):
        for i in range(4):
            even = r.acc_pix[k, 24 * i : 24 * i + 12, :128]
            odd = r.acc_pix[k, 24 * i + 12 : 24 * i + 24, 128:]
            row = at[f"pixel{k}"] + i * 12
            packed[row : row + 12, :] = even + odd

    def each_image(*stages):
        def run(img, _):
            for stage in stages:
                stage(img)
            return 0

        lax.fori_loop(0, share, run, 0)

    each_image(decode_forward)
    local[0].wait()
    remote[0].wait()
    each_image(make_patches, decode_back, decode_in_back)
    pack_conv(2)
    pack_pixel(1)
    put("from0", r.acc_from[:64, :128] + r.acc_from[64:, 128:])
    begin(0)
    each_image(top_forward, between([(0, 1)], [(0, 2)]), bottom_forward)
    for level in range(2):
        sums = r.acc_sums[level, :64, :] + r.acc_sums[level, 64:, :]
        used = jnp.sum(r.acc_count[level], axis=0, keepdims=True)
        for b in range(4):
            row = at["sums"] + (level * 4 + b) * 64
            packed[row : row + 64, :] = sums[:, b * 128 : b * 128 + 128]
            row = at["count"] + level * 4 + b
            packed[row : row + 1, :] = used[:, b * 128 : b * 128 + 128]
    put("dead", r.acc_dead[...])
    put("numer", r.acc_num[...])
    steps((0, 3))
    begin(1)
    each_image(
        bottom_back,
        between([(1, 1)], [(1, 2)]),
        bottom_in_back,
        between([(0, 4)], [(0, 5)]),
    )
    pack_conv(1)
    for k in range(4):
        put(
            f"from{k + 1}",
            r.acc_up[:64, k * 128 : k * 128 + 128] + r.acc_up[64:, 512 + k * 128 : 640 + k * 128],
        )
    for k in range(2):
        put(f"to{k}", r.acc_to[k, :64, :128] + r.acc_to[k, 64:, 128:])
    begin(2)
    steps((1, 3))
    each_image(top_back, between([(2, 1), (0, 6)], []))
    pack_conv(0)
    pack_pixel(0)
    put("down", r.acc_down[...])
    begin(3)
    if len(groups) > 4:
        begin(4)
        steps(
            (1, 4), (3, 1), (4, 1), (2, 2), (3, 2), (1, 5), (4, 2), (2, 3), (3, 3), (1, 6), (4, 3), (2, 4),
            (3, 4), (4, 4), (2, 5), (3, 5), (4, 5), (2, 6), (3, 6), (4, 6),
        )
    else:
        steps(
            (1, 4), (3, 1), (2, 2), (1, 5), (3, 2), (2, 3), (1, 6),
            (3, 3), (2, 4), (3, 4), (2, 5), (3, 5), (2, 6), (3, 6),
        )


def compute(devices, valid_rows, dead_source, pixels, ct, cb, weights, book):
    plane = devices // Z_SIZE
    _, groups, total_rows = row_layout(devices)
    share = pixels.shape[0] // 4
    vm = pl.BlockSpec(memory_space=pltpu.VMEM)
    anywhere = pl.BlockSpec(memory_space=pl.ANY)
    return pl.pallas_call(
        functools.partial(compute_kernel, devices),
        in_specs=[anywhere] * 12,
        out_specs=vm,
        scratch_shapes=scratch_of(
            share, 2 * pixels.shape[1], valid_rows, dead_source, pixels, ct, cb, [*weights, book], total_rows, plane, groups
        ),
        out_shape=jax.ShapeDtypeStruct((total_rows, 128), F32),
        compiler_params=pltpu.CompilerParams(
            collective_id=0, has_side_effects=True, vmem_limit_bytes=VMEM_LIMIT
        ),
        name="step_compute",
    )(valid_rows, dead_source, pixels, ct, cb, *weights, book)


def update_kernel(devices, dead_codes, valid_v, total, *refs):
    w, m, v = refs[0:6], refs[6:12], refs[12:18]
    ema_count, ema_sum = refs[18:20]
    norm_o, pair_o = refs[20:22]
    new_o, mom_o, sec_o, low_o = refs[22:28], refs[28:34], refs[34:40], refs[40:46]
    book_o, count_o, sum_o = refs[46:49]
    at, groups, _ = row_layout(devices)
    squares = jnp.zeros((8, 128), F32)
    for start, size in groups[:1] + groups[2:]:
        grads = total[start : start + size, :]
        squares = squares + jnp.sum((grads * grads).reshape(size // 8, 8, 128), axis=0)
    squares = jnp.sum(squares)
    norm = jnp.sqrt(jnp.full((8, 128), squares, F32))
    norm_o[0] = norm[0, 0]
    factor = (CLIP_NORM / jnp.maximum(norm, CLIP_NORM))[0, 0]
    pair_o[0] = jnp.sum(total[at["numer"] : at["numer"] + 8, :])
    pair_o[1] = 3.0 * 256.0 * jnp.sum(valid_v[...].astype(F32))

    def apply(t, index, grad):
        g = grad * factor
        first = MOMENT_ONE * m[t][index] + (1.0 - MOMENT_ONE) * g
        second = MOMENT_TWO * v[t][index] + (1.0 - MOMENT_TWO) * g * g
        step = first / (1.0 - MOMENT_ONE**STEP) / (
            jnp.sqrt(second / (1.0 - MOMENT_TWO**STEP)) + ADAM_EPSILON
        )
        weight = w[t][index]
        fresh = weight - LEARN_RATE * (step + WEIGHT_DECAY * weight)
        new_o[t][index] = fresh
        mom_o[t][index] = first
        sec_o[t][index] = second
        low_o[t][index] = fresh.astype(BF16)

    def piece(name, size, offset=0):
        return total[at[name] + offset : at[name] + offset + size, :]

    for k in range(3):
        for t in range(9):
            apply(0, (k, slice(None), pl.ds(t * 128, 128)), piece(f"conv{k}", 64, t * 64))
        apply(1, (k,), piece(f"res{k}", 64))
    for k in range(5):
        apply(2, (k,), piece(f"from{k}", 64))
    for k in range(2):
        apply(3, (k,), piece(f"to{k}", 64))
        apply(4, (k,), piece(f"pixel{k}", 48))
    for k in range(4):
        apply(5, (k,), piece("down", 128, k * 128))

    dead = jnp.concatenate(
        [piece("dead", DEAD), jnp.zeros((128 - DEAD, 128), F32)], axis=0
    )
    dead = jnp.transpose(dead)
    for level in range(2):
        for b in range(4):
            lanes = pl.ds(b * 128, 128)
            ids = lane_iota((64, 128)) + b * 128
            count = CODE_DECAY * ema_count[level : level + 1, b * 128 : b * 128 + 128] + (
                1.0 - CODE_DECAY
            ) * piece("count", 1, level * 4 + b)
            sums = CODE_DECAY * ema_sum[level, :, lanes] + (
                1.0 - CODE_DECAY
            ) * piece("sums", 64, (level * 4 + b) * 64)
            for r in range(8):
                taken = ids == dead_codes[level, r]
                count = jnp.where(taken[:1], 1.0, count)
                sums = jnp.where(taken, dead[level * 64 : level * 64 + 64, r : r + 1], sums)
            count_o[level : level + 1, b * 128 : b * 128 + 128] = count
            sum_o[level, :, lanes] = sums
            book_o[level, :, lanes] = sums / count


def update(devices, dead_codes, valid_rows, total, weights, firsts, seconds, ema_count, ema_sum):
    sds = jax.ShapeDtypeStruct
    shapes = [sds((1,), F32), sds((2,), F32)]
    for _ in range(3):
        shapes += [sds(w.shape, F32) for w in weights]
    shapes += [sds(w.shape, BF16) for w in weights]
    shapes += [sds(ema_sum.shape, F32), sds(ema_count.shape, F32), sds(ema_sum.shape, F32)]
    vm = pl.BlockSpec(memory_space=pltpu.VMEM)
    sm = pl.BlockSpec(memory_space=pltpu.SMEM)
    return pl.pallas_call(
        functools.partial(update_kernel, devices),
        out_shape=shapes,
        in_specs=[sm] + [vm] * 22,
        out_specs=[sm, sm] + [vm] * 27,
        compiler_params=pltpu.CompilerParams(vmem_limit_bytes=VMEM_LIMIT),
        name="step_update",
    )(dead_codes, valid_rows, total, *weights, *firsts, *seconds, ema_count, ema_sum)


def body(sections, devices, *args):
    pixels, codes_top, codes_bottom, valid_rows, dead_codes, dead_source = args[:6]
    weights, firsts, seconds = args[6:12], args[12:18], args[18:24]
    codebook, ema_count, ema_sum = args[24:27]
    batches, part_rows, lanes = pixels.shape
    height = lanes // 3
    parts = height // part_rows
    assert parts == 2 and sections == 2

    def turn(arrays):
        return [x.transpose(0, 2, 1) if x.shape[2] == 64 else x for x in arrays]

    weights, firsts, seconds = turn(weights), turn(firsts), turn(seconds)
    codebook, ema_sum = turn([codebook, ema_sum])
    total = compute(
        devices, valid_rows, dead_source, pixels, codes_top, codes_bottom, weights, codebook
    )
    outs = update(devices, dead_codes, valid_rows, total, weights, firsts, seconds, ema_count, ema_sum)
    outs = [x.transpose(0, 2, 1) if len(x.shape) == 3 and x.shape[1] == 64 and turned else x for x, turned in zip(outs, TURNED)]
    return (outs[0].reshape(()),) + tuple(outs[1:])


TURNED = (False, False) + (True, False, False, True, False, False) * 4 + (True, False, True)


def solution(mesh):
    return jax.shard_map(
        functools.partial(body, mesh.shape["section"], mesh.shape["dp"]),
        mesh=mesh,
        in_specs=(P(None, "dp", None),) * 3 + (P(),) * 24,
        out_specs=(P(),) * 29,
        check_vma=False,
    )
```
